32 devices in a mesh: rep: 4 (over y, x), fsdp: 8 (over z, core).
Axes of the slice: x: 2, y: 2, z: 4, core: 2. Of those that a mesh axis runs over, the one named last changes fastest.
Arguments:
- block_input: bfloat16 [4096, 4096], P(('rep', 'fsdp')), may hold values from -6 to 6
- ssd_input: bfloat16 [4096, 4096], P(('rep', 'fsdp')), may hold values from -6 to 6
- out_grad: bfloat16 [4096, 4096], P(('rep', 'fsdp')), may hold values from -0.29882812 to 0.29882812
- start_state: bfloat16 [32, 64, 4096], P(('rep', 'fsdp')), may hold values from -12 to 12
- step_bias: float32 [64], replicated, may hold values from -1 to 1
- decay_log: float32 [64], replicated, may hold values from -7 to -2.5
- local_params: float32 [4, 192, 4096], P('rep', 'fsdp'), may hold values from -0.09375 to 0.09375
- global_params: float32 [192, 4096], P('fsdp'), may hold values from -0.75 to 0.75
- momentum: float32 [192, 4096], P('fsdp'), may hold values from -3 to 3
Outputs:
- block_grad: bfloat16 [4096, 4096], P(('rep', 'fsdp'))
- new_params: float32 [192, 4096], P('fsdp')
- new_momentum: float32 [192, 4096], P('fsdp')
The draws below stay inside these ranges and needn't reach their ends.
All inputs are finite; a program needn't handle non-finite values.
Results may differ from the reference program's by a relative error of at most 0.012.
Values may be sent and summed in bfloat16 or wider, within the bound.
No kernel may reach another device: no remote copies, remote signals or barrier semaphores. Data moves between devices by JAX's collectives and lax.ppermute only.
A program may use at most 64 MiB of HBM per device.

```python
import jax
import jax.numpy as jnp
from jax import lax

D = 4096
HEADS = 64
HEAD_DIM = 64
STATE = 64
BLOCK = 128
COLS = 192
REPLICAS = 4
SEQS = 32
TOKENS = 4096


def shard_levels(rng, dims, shards, least, top_value):
    def one(axis_at, blocks):
        draws = jax.random.uniform(jax.random.fold_in(jax.random.fold_in(rng, 6), axis_at), (blocks,), jnp.float32, least / len(shards), top_value / len(shards))
        return jnp.repeat(jnp.exp(draws), dims[axis_at] // blocks).reshape((-1,) + (1,) * (len(dims) - axis_at - 1))

    loudness = one(*shards[0])
    for cut in shards[1:]:
        loudness = loudness * one(*cut)
    return loudness


def scatter_about(own_key, shape, deviation, limit, split=(), kind=jnp.bfloat16):
    values = deviation * jax.random.normal(own_key, shape, jnp.float32)
    if split:
        values = values * shard_levels(own_key, shape, split, -0.22, 0.18)
    return jnp.clip(values, -limit, limit).astype(kind)


def setup_inputs(seed: int = 0) -> dict:
    splits = jax.random.split(jax.random.key(seed), 10)
    block_input = scatter_about(splits[0], (TOKENS, D), 1.0, 6.0, ((0, 32),))
    ssd_input = scatter_about(splits[1], (TOKENS, HEADS * HEAD_DIM), 1.0, 6.0, ((0, 32),))
    out_grad = scatter_about(splits[2], (TOKENS, HEADS * HEAD_DIM), 0.05, 0.29882812, ((0, 32),))
    start_state = scatter_about(splits[3], (SEQS, HEADS, HEAD_DIM * STATE), 2.0, 12.0, ((0, 32),))
    step_bias = jnp.clip(jax.random.uniform(splits[4], (HEADS,), jnp.float32, -1.0, 1.0), -1.0, 1.0)
    decay_log = jnp.clip(jax.random.uniform(splits[5], (HEADS,), jnp.float32, -7.0, -2.5), -7.0, -2.5)
    local_params = scatter_about(splits[6], (REPLICAS, COLS, D), D ** -0.5, 0.09375, ((0, 4), (1, 8)), jnp.float32)
    global_params = scatter_about(splits[7], (COLS, D), (D // 64) ** -0.5, 0.75, ((0, 8),), jnp.float32)
    momentum = scatter_about(splits[8], (COLS, D), 0.5, 3.0, ((0, 8),), jnp.float32)
    return dict(block_input=block_input, ssd_input=ssd_input, out_grad=out_grad, start_state=start_state, step_bias=step_bias, decay_log=decay_log, local_params=local_params, global_params=global_params, momentum=momentum)


inner_rate = 0.002
outer_rate = 0.7
momentum_decay = 0.9

def contract_last(left, right):
    return lax.dot_general(left, right, (((1,), (1,)), ((), ())), preferred_element_type=jnp.float32)

def ssd_forward(projected, values, carried_in, step_bias, decay_log):
    key_side = projected[:, :STATE]
    query_side = projected[:, STATE:2 * STATE]
    step_size = jax.nn.softplus(projected[:, 2 * STATE:] + step_bias)
    cumulative = jnp.cumsum(-step_size * jnp.exp(decay_log), axis=0)
    positions = jnp.arange(BLOCK)
    causal = positions[:, None] >= positions[None, :]
    spans = cumulative.T[:, :, None] - cumulative.T[:, None, :]
    decays = jnp.where(causal, jnp.exp(jnp.where(causal, spans, 0.0)), 0.0)
    scores = jnp.dot(query_side, key_side.T, precision=lax.Precision.HIGHEST)
    mixing = scores[None] * decays
    scaled = values.astype(jnp.float32).reshape(BLOCK, HEADS, HEAD_DIM) * step_size[:, :, None]
    within = jnp.einsum('hts,shp->thp', mixing, scaled, precision=lax.Precision.HIGHEST)
    state_f = carried_in.astype(jnp.float32).reshape(HEADS, HEAD_DIM, STATE)
    entering = jnp.einsum('tn,hpn->thp', query_side, state_f, precision=lax.Precision.HIGHEST)
    entering = entering * jnp.exp(cumulative)[:, :, None]
    return (within + entering).reshape(BLOCK, HEADS * HEAD_DIM)

def sequence_grads(projected, ssd_rows, cot_rows, states, step_bias, decay_log):
    blocks = projected.shape[0] // BLOCK

    def single(members):
        proj_one, values, cotangent, carried_in = members
        _, pullback = jax.vjp(lambda probe: ssd_forward(probe, values, carried_in, step_bias, decay_log), proj_one)
        return pullback(cotangent.astype(jnp.float32))[0]
    grads = lax.map(single, (projected.reshape(blocks, BLOCK, -1), ssd_rows.reshape(blocks, BLOCK, -1), cot_rows.reshape(blocks, BLOCK, -1), states))
    return grads.reshape(blocks * BLOCK, -1)

def reference(block_input, ssd_input, out_grad, start_state, step_bias, decay_log, local_params, global_params, momentum):
    replicas = local_params.shape[0]

    def replica(members):
        rows_in, ssd_rows, cot_rows, states, params = members
        weights = params.astype(jnp.bfloat16)
        projected = contract_last(rows_in, weights)
        proj_grad = sequence_grads(projected, ssd_rows, cot_rows, states, step_bias, decay_log).astype(jnp.bfloat16)
        block_grad = jnp.dot(proj_grad, weights, preferred_element_type=jnp.float32).astype(jnp.bfloat16)
        gradient = jnp.dot(proj_grad.T, rows_in, preferred_element_type=jnp.float32)
        return (block_grad, params - inner_rate * gradient)
    stacked = (block_input.reshape(replicas, -1, D), ssd_input.reshape(replicas, -1, HEADS * HEAD_DIM), out_grad.reshape(replicas, -1, HEADS * HEAD_DIM), start_state.reshape(replicas, -1, HEADS, HEAD_DIM * STATE), local_params)
    block_grad, stepped = lax.map(replica, stacked)
    pseudo = global_params[None] - stepped
    mean_pseudo = lax.optimization_barrier(jnp.sum(pseudo, axis=0)) / replicas
    new_momentum = momentum_decay * momentum + mean_pseudo
    new_params = global_params - outer_rate * (mean_pseudo + momentum_decay * new_momentum)
    return (block_grad.reshape(-1, D), new_params, new_momentum)
```

```python
import functools

import jax
import jax.numpy as jnp
from jax import lax
from jax.experimental import pallas as pl
from jax.experimental.pallas import tpu as pltpu
from jax.sharding import PartitionSpec as P

STATE = 64
LOG2E = 1.4426950408889634

inner_rate = 0.002
outer_rate = 0.7
momentum_decay = 0.9

VMEM_LIMIT = 48 * 1024 * 1024
EXACT = lax.Precision.HIGHEST


def params(**more):
    return pltpu.CompilerParams(vmem_limit_bytes=VMEM_LIMIT, **more)


def whole_vmem(count):
    return [pl.BlockSpec(memory_space=pltpu.VMEM)] * count


def contract(left, right, dims, precision=None):
    return lax.dot_general(
        left, right, (dims, ((), ())), preferred_element_type=jnp.float32, precision=precision
    )


def early_kernel(cot_ref, val_ref, state_ref, cross_ref, enter_ref):
    block = cot_ref.shape[0]
    lanes = lax.broadcasted_iota(jnp.int32, (block, 2 * STATE), 1)
    rows = lax.broadcasted_iota(jnp.int32, (block, block), 0)
    cols = lax.broadcasted_iota(jnp.int32, (block, block), 1)
    causal = rows >= cols
    low = lanes < STATE
    square = (2 * STATE, 2 * STATE)
    same_head = (lax.broadcasted_iota(jnp.int32, square, 0) < STATE) == (
        lax.broadcasted_iota(jnp.int32, square, 1) < STATE
    )
    for pair in range(cot_ref.shape[1] // (2 * STATE)):
        span = slice(pair * 2 * STATE, (pair + 1) * 2 * STATE)
        cot = cot_ref[:, span]
        val = val_ref[:, span]
        zero = jnp.zeros_like(cot)
        for odd in range(2):
            one = jnp.where(low, zero, cot) if odd else jnp.where(low, cot, zero)
            cross = contract(one, val, ((1,), (1,)))
            cross_ref[2 * pair + odd] = jnp.where(causal, cross, 0.0).astype(cross_ref.dtype)
        state = state_ref[span, :]
        wide = jnp.concatenate([state, state], axis=1)
        wide = jnp.where(same_head, wide, jnp.zeros_like(wide))
        enter_ref[:, span] = contract(cot, wide, ((1,), (0,)))


def early_products(out_grad, ssd_input, state):
    block, width = out_grad.shape
    heads = width // STATE
    steps = 8
    piece = width // steps
    return pl.pallas_call(
        early_kernel,
        grid=(steps,),
        in_specs=[
            pl.BlockSpec((block, piece), lambda i: (0, i)),
            pl.BlockSpec((block, piece), lambda i: (0, i)),
            pl.BlockSpec((piece, STATE), lambda i: (i, 0)),
        ],
        out_specs=[
            pl.BlockSpec((heads // steps, block, block), lambda i: (i, 0, 0)),
            pl.BlockSpec((block, piece), lambda i: (0, i)),
        ],
        out_shape=[
            jax.ShapeDtypeStruct((heads, block, block), jnp.bfloat16),
            jax.ShapeDtypeStruct((block, width), jnp.float32),
        ],
        compiler_params=params(),
        cost_estimate=pl.CostEstimate(
            flops=2 * block * width * 4 * block, bytes_accessed=8 * block * width, transcendentals=0
        ),
        name="early_products",
    )(out_grad, ssd_input, state)


def ssd_kernel(shards, owners_ref, rows_ref, bias_ref, decay_ref, cross_ref, enter_ref, *rest):
    weight_refs = rest[:shards]
    grad_ref, grad_rel_ref, proj_ref, col_ref, out_ref = rest[shards:]
    block = rows_ref.shape[0]
    heads = bias_ref.shape[0]
    per = weight_refs[0].shape[0]
    rows_in = rows_ref[...]
    for k in range(shards):
        start = pl.multiple_of(owners_ref[k] * per, 8) if shards > 1 else 0
        proj_ref[pl.ds(start, per), :] = contract(weight_refs[k][...], rows_in, ((1,), (1,)))
    key_t = proj_ref[:STATE, :]
    query_t = proj_ref[STATE : 2 * STATE, :]
    raw = proj_ref[2 * STATE :, :] + bias_ref[...]
    step_t = jnp.maximum(raw, 0.0) + jnp.log1p(jnp.exp(-jnp.abs(raw)))
    rate = jnp.exp(decay_ref[...])
    up = lax.broadcasted_iota(jnp.int32, (block, block), 0)
    across = lax.broadcasted_iota(jnp.int32, (block, block), 1)
    before = jnp.where(up <= across, 1.0, 0.0)
    after = jnp.where(up >= across, 1.0, 0.0)
    cum_t = contract(-step_t * rate, before, ((1,), (0,)), EXACT) * LOG2E
    cum = cum_t.T
    step = step_t.T
    query = query_t.T
    key = key_t.T
    scores = contract(query, key_t, ((1,), (0,)), EXACT)
    entered = jnp.exp2(cum)
    query_twice = jnp.concatenate([query, query], axis=1)
    low = lax.broadcasted_iota(jnp.int32, (block, 2 * STATE), 1) < STATE
    head_of = lax.broadcasted_iota(jnp.int32, (block, heads), 1)
    below = lax.broadcasted_iota(jnp.int32, (block, heads), 0) < STATE

    score_grad = jnp.zeros((block, block), jnp.float32)
    query_grad = jnp.zeros((block, 2 * STATE), jnp.float32)
    row_sums = jnp.zeros((block, heads), jnp.float32)
    for h0 in range(0, heads, 4):
        left, right = [], []
        for h in range(h0, h0 + 4):
            span = cum[:, h : h + 1] - cum_t[h : h + 1, :]
            weight = cross_ref[h].astype(jnp.float32) * jnp.exp2(jnp.minimum(span, 0.0))
            score_grad = score_grad + weight * step_t[h : h + 1, :]
            mixed = weight * scores
            col_ref[h : h + 1, :] = jnp.sum(mixed, axis=0, keepdims=True)
            left.append(mixed.astype(jnp.bfloat16))
            right.append(jnp.where(head_of == h, step, 0.0).astype(jnp.bfloat16))
        for h in range(h0, h0 + 4, 2):
            gain = jnp.where(low, entered[:, h : h + 1], entered[:, h + 1 : h + 2])
            part = enter_ref[:, h * STATE : (h + 2) * STATE] * gain
            query_grad = query_grad + part
            left.append((part * query_twice).astype(jnp.bfloat16))
            right.append(
                jnp.where(head_of == jnp.where(below, h, h + 1), 1.0, 0.0).astype(jnp.bfloat16)
            )
        row_sums = row_sums + contract(
            jnp.concatenate(left, axis=1), jnp.concatenate(right, axis=0), ((1,), (0,))
        )

    cols_t = col_ref[...]
    cum_grad = row_sums.T - step_t * cols_t
    later = contract(cum_grad, after, ((1,), (0,)), EXACT)
    step_grad = cols_t - rate * later
    raw_grad = step_grad / (1.0 + jnp.exp(-raw))
    out_ref[:STATE, :] = contract(query_t, score_grad, ((1,), (0,)), EXACT)
    query_all = (query_grad[:, :STATE] + query_grad[:, STATE:]).T
    out_ref[STATE : 2 * STATE, :] = query_all + contract(key_t, score_grad, ((1,), (1,)), EXACT)
    out_ref[2 * STATE :, :] = raw_grad
    grad_ref[...] = out_ref[...].astype(jnp.bfloat16)
    if shards > 1:
        for k in range(shards):
            start = pl.multiple_of(owners_ref[k] * per, 8)
            proj_ref[k * per : (k + 1) * per, :] = out_ref[pl.ds(start, per), :]
        grad_rel_ref[...] = proj_ref[...].astype(jnp.bfloat16)
    else:
        grad_rel_ref[...] = out_ref[...].astype(jnp.bfloat16)


def ssd_backward(owners, rows_in, step_bias, decay_log, cross, enter, weights):
    block = rows_in.shape[0]
    heads = step_bias.shape[0]
    cols = sum(w.shape[0] for w in weights)
    shards = len(weights)
    return pl.pallas_call(
        functools.partial(ssd_kernel, shards),
        in_specs=[pl.BlockSpec(memory_space=pltpu.SMEM)] + whole_vmem(5 + shards),
        out_specs=whole_vmem(2),
        out_shape=[jax.ShapeDtypeStruct((cols, block), jnp.bfloat16)] * 2,
        scratch_shapes=[
            pltpu.VMEM((cols, block), jnp.float32),
            pltpu.VMEM((heads, block), jnp.float32),
            pltpu.VMEM((cols, block), jnp.float32),
        ],
        compiler_params=params(),
        cost_estimate=pl.CostEstimate(
            flops=2 * block * cols * rows_in.shape[1],
            bytes_accessed=16 * rows_in.size,
            transcendentals=heads * block * block,
        ),
        name="ssd_backward",
    )(owners, rows_in, step_bias.reshape(-1, 1), decay_log.reshape(-1, 1), cross, enter, *weights)


def slice_kernel(parts, chips, dest_ref, *refs):
    left = jnp.concatenate([r[...] for r in refs[:parts]], axis=1)
    right = jnp.concatenate([r[...] for r in refs[parts : 2 * parts]], axis=0)
    outs = refs[2 * parts : 2 * parts + chips]
    total = refs[-1]
    total[...] = contract(left, right, ((1,), (0,)))
    per = outs[0].shape[0]
    for k in range(chips):
        start = pl.multiple_of(dest_ref[k] * per, 8)
        outs[k][...] = total[pl.ds(start, per), :].astype(jnp.bfloat16)


def gradient_slices(dests, grads_t, inputs, chips):
    cols = grads_t[0].shape[0]
    width = inputs[0].shape[1]
    parts = len(inputs)
    return pl.pallas_call(
        functools.partial(slice_kernel, parts, chips),
        in_specs=[pl.BlockSpec(memory_space=pltpu.SMEM)] + whole_vmem(2 * parts),
        out_specs=whole_vmem(chips),
        out_shape=[jax.ShapeDtypeStruct((cols // chips, width), jnp.bfloat16)] * chips,
        scratch_shapes=[pltpu.VMEM((cols, width), jnp.float32)],
        compiler_params=params(),
        name="gradient_slices",
    )(dests, *grads_t, *inputs)


def line_kernel(parts, core_ref, *refs):
    total = refs[-1]
    acc = refs[0][...].astype(jnp.float32)
    for r in refs[1:parts]:
        acc = acc + r[...].astype(jnp.float32)
    total[...] = acc
    for k, out in enumerate(refs[parts:-1]):
        per = out.shape[0]
        start = pl.multiple_of(core_ref[k] * per, 8)
        out[...] = total[pl.ds(start, per), :].astype(jnp.bfloat16)


def line_sum(cores, pieces):
    rows, width = pieces[0].shape
    return pl.pallas_call(
        functools.partial(line_kernel, len(pieces)),
        in_specs=[pl.BlockSpec(memory_space=pltpu.SMEM)] + whole_vmem(len(pieces)),
        out_specs=whole_vmem(2),
        out_shape=[jax.ShapeDtypeStruct((rows // 2, width), jnp.bfloat16)] * 2,
        scratch_shapes=[pltpu.VMEM((rows, width), jnp.float32)],
        compiler_params=params(),
        name="line_sum",
    )(cores, *pieces)


def outer_kernel(parts, scale, spots_ref, mom_ref, par_ref, *refs):
    width = refs[0].shape[1]
    new_par, new_mom = refs[parts:]
    for k in range(parts):
        cols = pl.ds(pl.multiple_of(spots_ref[k] * width, 128), width)
        term = refs[k][...].astype(jnp.float32) * scale
        new_mom[:, cols] = mom_ref[:, cols] + term
        new_par[:, cols] = par_ref[:, cols] - (outer_rate * (1.0 + momentum_decay)) * term


def outer_step(spots, early_momentum, early_params, pieces, scale):
    return pl.pallas_call(
        functools.partial(outer_kernel, len(pieces), scale),
        in_specs=[pl.BlockSpec(memory_space=pltpu.SMEM)] + whole_vmem(2 + len(pieces)),
        out_specs=whole_vmem(2),
        out_shape=[jax.ShapeDtypeStruct(early_params.shape, jnp.float32)] * 2,
        compiler_params=params(),
        name="outer_step",
    )(spots, early_momentum, early_params, *pieces)


def power_of_two(n):
    return n & (n - 1) == 0


def on_device(
    replicas,
    shards,
    block_input,
    ssd_input,
    out_grad,
    start_state,
    step_bias,
    decay_log,
    local_params,
    global_params,
    momentum,
):
    local_rows = local_params[0]
    rows, depth = local_rows.shape
    own = local_rows.astype(jnp.bfloat16)
    seq_width = ssd_input.shape[1]
    chips = shards // 2
    plane = 2 * replicas
    fast = (
        shards % 2 == 0
        and shards <= 16
        and rows % 8 == 0
        and power_of_two(replicas)
        and power_of_two(chips)
        and depth % (128 * plane) == 0
    )
    rep = lax.axis_index("rep")
    spot = lax.axis_index("fsdp")
    blocks = start_state.shape[0]
    block = block_input.shape[0] // blocks

    def send(value, where):
        pairs = []
        for r in range(replicas):
            for f in range(shards):
                to_r, to_f = where(r, f)
                pairs.append((r * shards + f, to_r * shards + to_f))
        return lax.ppermute(value, ("rep", "fsdp"), pairs)

    if fast:
        ring = [2 * z for z in range(chips)] + [2 * z + 1 for z in reversed(range(chips))]
        place = [ring.index(f) for f in range(shards)]

        def around(by):
            return lambda r, f: (r, ring[(place[f] + by) % shards])

        weights = [own]
        owners = [spot]
        ring_table = jnp.array(ring, jnp.int32)
        my_place = jnp.array(place, jnp.int32)[spot]
        forward = backward = own
        for k in range(1, shards // 2 + 1):
            forward = send(forward, around(1))
            weights.append(forward)
            owners.append(ring_table[(my_place - k) % shards])
            if k < shards - k:
                backward = send(backward, around(-1))
                weights.append(backward)
                owners.append(ring_table[(my_place + k) % shards])
        owners = jnp.stack(owners).astype(jnp.int32)
    else:
        weights = [lax.all_gather(own, "fsdp", axis=0, tiled=True)]
        owners = jnp.zeros((1,), jnp.int32)

    grads_t, grads_rel_t = [], []
    for b in range(blocks):
        seq = slice(b * block, (b + 1) * block)
        cross, enter = early_products(
            out_grad[seq], ssd_input[seq], start_state[b].reshape(seq_width, STATE)
        )
        one, one_rel = ssd_backward(
            owners, block_input[seq], step_bias, decay_log, cross, enter, weights
        )
        grads_t.append(one)
        grads_rel_t.append(one_rel)
    grad_t = grads_t[0] if blocks == 1 else jnp.concatenate(grads_t, axis=1)
    grad_rel_t = grads_rel_t[0] if blocks == 1 else jnp.concatenate(grads_rel_t, axis=1)
    gathered = weights[0] if len(weights) == 1 else jnp.concatenate(weights, axis=0)
    block_grad = contract(grad_rel_t, gathered, ((0,), (0,))).astype(jnp.bfloat16)

    if not fast:
        gradient = lax.psum_scatter(
            contract(grad_t, block_input, ((1,), (0,))), "fsdp", scatter_dimension=0, tiled=True
        )
        pseudo = global_params - (local_rows - inner_rate * gradient)
        mean_pseudo = lax.psum(pseudo.astype(jnp.bfloat16), "rep").astype(jnp.float32) / replicas
        new_momentum = momentum_decay * momentum + mean_pseudo
        new_params = global_params - outer_rate * (mean_pseudo + momentum_decay * new_momentum)
        return (block_grad, new_params, new_momentum)

    shares = [own] + [
        send(own, lambda r, f, k=k: (r ^ k, f)) for k in range(1, replicas)
    ]
    shares = [s.astype(jnp.float32) for s in shares]
    while len(shares) > 1:
        shares = [shares[i] + shares[i + 1] for i in range(0, len(shares), 2)]
    early_pseudo = global_params - shares[0] / replicas
    early_momentum = momentum_decay * momentum + early_pseudo
    early_params = global_params - outer_rate * (early_pseudo + momentum_decay * early_momentum)

    core = spot % 2
    chip = spot // 2
    mine = rep * 2 + core
    width = depth // plane

    def in_plane(k):
        def where(r, f):
            q = (2 * r + f % 2) ^ k
            return q // 2, (f // 2) * 2 + q % 2

        return where

    inputs = []
    for k in range(plane):
        piece = lax.dynamic_slice_in_dim(block_input, (mine ^ k) * width, width, axis=1)
        inputs.append(send(piece, in_plane(k)) if k else piece)
    plane_grads = [grad_t] + [send(grad_t, in_plane(k)) for k in range(1, plane)]
    dests = jnp.stack([chip ^ k for k in range(chips)]).astype(jnp.int32)
    slices = gradient_slices(dests, plane_grads, inputs, chips)
    pieces = [slices[0]] + [
        send(slices[k], lambda r, f, k=k: (r, ((f // 2) ^ k) * 2 + f % 2)) for k in range(1, chips)
    ]
    cores = jnp.stack([core, 1 - core]).astype(jnp.int32)
    same, other = line_sum(cores, pieces)
    final = [same] + [
        send(other if k % 2 else same, in_plane(k)) for k in range(1, plane)
    ]
    spots = jnp.stack([mine ^ k for k in range(plane)]).astype(jnp.int32)
    new_params, new_momentum = outer_step(
        spots, early_momentum, early_params, final, inner_rate / replicas
    )
    return (block_grad, new_params, new_momentum)


def solution(mesh):
    placed = (
        P(("rep", "fsdp"), None),
        P(("rep", "fsdp"), None),
        P(("rep", "fsdp"), None),
        P(("rep", "fsdp"), None, None),
        P(),
        P(),
        P("rep", "fsdp", None),
        P("fsdp", None),
        P("fsdp", None),
    )
    return jax.shard_map(
        functools.partial(on_device, mesh.shape["rep"], mesh.shape["fsdp"]),
        mesh=mesh,
        in_specs=placed,
        out_specs=(P(("rep", "fsdp"), None), P("fsdp", None), P("fsdp", None)),
        check_vma=False,
    )
```

```python
import functools

import jax
import jax.numpy as jnp
from jax import lax
from jax.experimental import pallas as pl
from jax.experimental.pallas import tpu as pltpu
from jax.sharding import PartitionSpec as P

STATE = 64
LOG2E = 1.4426950408889634

inner_rate = 0.002
outer_rate = 0.7
momentum_decay = 0.9

VMEM_LIMIT = 48 * 1024 * 1024
EXACT = lax.Precision.HIGHEST


def params(**more):
    return pltpu.CompilerParams(vmem_limit_bytes=VMEM_LIMIT, **more)


def whole_vmem(count):
    return [pl.BlockSpec(memory_space=pltpu.VMEM)] * count


def contract(left, right, dims, precision=None):
    return lax.dot_general(
        left, right, (dims, ((), ())), preferred_element_type=jnp.float32, precision=precision
    )


def early_kernel(cot_ref, val_ref, state_ref, cross_ref, enter_ref):
    block = cot_ref.shape[0]
    lanes = lax.broadcasted_iota(jnp.int32, (block, 2 * STATE), 1)
    rows = lax.broadcasted_iota(jnp.int32, (block, block), 0)
    cols = lax.broadcasted_iota(jnp.int32, (block, block), 1)
    causal = rows >= cols
    low = lanes < STATE
    square = (2 * STATE, 2 * STATE)
    same_head = (lax.broadcasted_iota(jnp.int32, square, 0) < STATE) == (
        lax.broadcasted_iota(jnp.int32, square, 1) < STATE
    )
    for pair in range(cot_ref.shape[1] // (2 * STATE)):
        span = slice(pair * 2 * STATE, (pair + 1) * 2 * STATE)
        cot = cot_ref[:, span]
        val = val_ref[:, span]
        zero = jnp.zeros_like(cot)
        for odd in range(2):
            one = jnp.where(low, zero, cot) if odd else jnp.where(low, cot, zero)
            cross = contract(one, val, ((1,), (1,)))
            cross_ref[2 * pair + odd] = jnp.where(causal, cross, 0.0).astype(cross_ref.dtype)
        state = state_ref[span, :]
        wide = jnp.concatenate([state, state], axis=1)
        wide = jnp.where(same_head, wide, jnp.zeros_like(wide))
        enter_ref[:, span] = contract(cot, wide, ((1,), (0,)))


def early_products(out_grad, ssd_input, state):
    block, width = out_grad.shape
    heads = width // STATE
    steps = 8
    piece = width // steps
    return pl.pallas_call(
        early_kernel,
        grid=(steps,),
        in_specs=[
            pl.BlockSpec((block, piece), lambda i: (0, i)),
            pl.BlockSpec((block, piece), lambda i: (0, i)),
            pl.BlockSpec((piece, STATE), lambda i: (i, 0)),
        ],
        out_specs=[
            pl.BlockSpec((heads // steps, block, block), lambda i: (i, 0, 0)),
            pl.BlockSpec((block, piece), lambda i: (0, i)),
        ],
        out_shape=[
            jax.ShapeDtypeStruct((heads, block, block), jnp.bfloat16),
            jax.ShapeDtypeStruct((block, width), jnp.float32),
        ],
        compiler_params=params(),
        cost_estimate=pl.CostEstimate(
            flops=2 * block * width * 4 * block, bytes_accessed=8 * block * width, transcendentals=0
        ),
        name="early_products",
    )(out_grad, ssd_input, state)


def stacked(refs):
    if len(refs) == 1:
        return refs[0][...]
    return jnp.concatenate([r[...].astype(jnp.float32) for r in refs], axis=0).astype(jnp.bfloat16)


def shard_rows(where_ref, k, rows):
    return pl.ds(pl.multiple_of((where_ref[1] ^ k) * rows, 8), rows)


def ssd_kernel(order, replicas, where_ref, rows_ref, bias_ref, decay_ref, cross_ref, enter_ref, *rest):
    shards = len(order)
    weight_refs = rest[:shards]
    grad_ref, send_ref, proj_ref, col_ref, out_ref = rest[shards:]
    block = rows_ref.shape[0]
    heads = bias_ref.shape[1]
    per = weight_refs[0].shape[0]
    arrived = contract(stacked(weight_refs), rows_ref[...], ((1,), (1,)))
    for at, k in enumerate(order):
        if shards > 1:
            proj_ref[shard_rows(where_ref, k, per), :] = arrived[at * per : (at + 1) * per]
        else:
            proj_ref[...] = arrived
    key_t = proj_ref[:STATE, :]
    query_t = proj_ref[STATE : 2 * STATE, :]
    bias_t = jnp.broadcast_to(bias_ref[...], (block, heads)).T
    rate = jnp.exp(jnp.broadcast_to(decay_ref[...], (block, heads)).T)
    raw = proj_ref[2 * STATE :, :] + bias_t
    step_t = jnp.maximum(raw, 0.0) + jnp.log1p(jnp.exp(-jnp.abs(raw)))
    up = lax.broadcasted_iota(jnp.int32, (block, block), 0)
    across = lax.broadcasted_iota(jnp.int32, (block, block), 1)
    before = jnp.where(up <= across, 1.0, 0.0)
    after = jnp.where(up >= across, 1.0, 0.0)
    cum_t = contract(-step_t * rate, before, ((1,), (0,)), EXACT) * LOG2E
    cum = cum_t.T
    step = step_t.T
    query = query_t.T
    scores = contract(query, key_t, ((1,), (0,)), EXACT)
    entered = jnp.exp2(cum)
    query_twice = jnp.concatenate([query, query], axis=1)
    low = lax.broadcasted_iota(jnp.int32, (block, 2 * STATE), 1) < STATE
    head_of = lax.broadcasted_iota(jnp.int32, (block, heads), 1)
    below = lax.broadcasted_iota(jnp.int32, (block, heads), 0) < STATE

    score_grad = jnp.zeros((block, block), jnp.float32)
    query_grad = jnp.zeros((block, 2 * STATE), jnp.float32)
    row_sums = jnp.zeros((block, heads), jnp.float32)
    for h0 in range(0, heads, 4):
        left, right = [], []
        for h in range(h0, h0 + 4):
            span = cum[:, h : h + 1] - cum_t[h : h + 1, :]
            weight = cross_ref[h].astype(jnp.float32) * jnp.exp2(jnp.minimum(span, 0.0))
            score_grad = score_grad + weight * step_t[h : h + 1, :]
            mixed = weight * scores
            col_ref[h : h + 1, :] = jnp.sum(mixed, axis=0, keepdims=True)
            left.append(mixed.astype(jnp.bfloat16))
            right.append(jnp.where(head_of == h, step, 0.0).astype(jnp.bfloat16))
        for h in range(h0, h0 + 4, 2):
            gain = jnp.where(low, entered[:, h : h + 1], entered[:, h + 1 : h + 2])
            part = enter_ref[:, h * STATE : (h + 2) * STATE] * gain
            query_grad = query_grad + part
            left.append((part * query_twice).astype(jnp.bfloat16))
            right.append(
                jnp.where(head_of == jnp.where(below, h, h + 1), 1.0, 0.0).astype(jnp.bfloat16)
            )
        row_sums = row_sums + contract(
            jnp.concatenate(left, axis=1), jnp.concatenate(right, axis=0), ((1,), (0,))
        )

    cols_t = col_ref[...]
    cum_grad = row_sums.T - step_t * cols_t
    later = contract(cum_grad, after, ((1,), (0,)), EXACT)
    step_grad = cols_t - rate * later
    raw_grad = step_grad / (1.0 + jnp.exp(-raw))
    out_ref[:STATE, :] = contract(query_t, score_grad, ((1,), (0,)), EXACT)
    query_all = (query_grad[:, :STATE] + query_grad[:, STATE:]).T
    out_ref[STATE : 2 * STATE, :] = query_all + contract(key_t, score_grad, ((1,), (1,)), EXACT)
    out_ref[2 * STATE :, :] = raw_grad
    if shards == 1:
        grad_ref[...] = out_ref[...].astype(jnp.bfloat16)
        send_ref[...] = jnp.zeros_like(send_ref)
        return
    for core in range(2):
        of_core = [
            out_ref[f * per : (f + 1) * per, :] for f in range(core, shards, 2)
        ]
        of_core = jnp.concatenate(of_core, axis=0).astype(jnp.bfloat16)
        for r in range(replicas):
            send_ref[2 * r + core] = of_core
    for at, k in enumerate(order):
        proj_ref[at * per : (at + 1) * per, :] = out_ref[shard_rows(where_ref, k, per), :]
    grad_ref[...] = proj_ref[...].astype(jnp.bfloat16)


def ssd_backward(where, rows_in, step_bias, decay_log, cross, enter, weights, order, replicas):
    block = rows_in.shape[0]
    heads = step_bias.shape[0]
    cols = sum(w.shape[0] for w in weights)
    apart = (2 * replicas, cols // 2, block) if len(order) > 1 else (16, 128)
    return pl.pallas_call(
        functools.partial(ssd_kernel, order, replicas),
        in_specs=[pl.BlockSpec(memory_space=pltpu.SMEM)] + whole_vmem(5 + len(order)),
        out_specs=whole_vmem(2),
        out_shape=[
            jax.ShapeDtypeStruct((cols, block), jnp.bfloat16),
            jax.ShapeDtypeStruct(apart, jnp.bfloat16),
        ],
        scratch_shapes=[
            pltpu.VMEM((cols, block), jnp.float32),
            pltpu.VMEM((heads, block), jnp.float32),
            pltpu.VMEM((cols, block), jnp.float32),
        ],
        compiler_params=params(),
        cost_estimate=pl.CostEstimate(
            flops=2 * block * cols * rows_in.shape[1],
            bytes_accessed=16 * rows_in.size,
            transcendentals=heads * block * block,
        ),
        name="ssd_backward",
    )(where, rows_in, step_bias.reshape(1, -1), decay_log.reshape(1, -1), cross, enter, *weights)


def block_grad_kernel(grad_ref, *refs):
    out_ref = refs[-1]
    weights = stacked(refs[:-1])
    out_ref[...] = contract(grad_ref[...].T, weights, ((1,), (0,))).astype(out_ref.dtype)


def block_gradient(grad, weights):
    depth = weights[0].shape[1]
    cols, block = grad.shape
    return pl.pallas_call(
        block_grad_kernel,
        in_specs=whole_vmem(1 + len(weights)),
        out_specs=pl.BlockSpec(memory_space=pltpu.VMEM),
        out_shape=jax.ShapeDtypeStruct((block, depth), jnp.bfloat16),
        compiler_params=params(),
        cost_estimate=pl.CostEstimate(
            flops=2 * block * cols * depth, bytes_accessed=4 * cols * depth, transcendentals=0
        ),
        name="block_gradient",
    )(grad, *weights)


def pieces_kernel(where_ref, rows_ref, own_ref, *outs):
    block = rows_ref.shape[0]
    width = outs[0].shape[1]
    for k, out in enumerate(outs):
        cols = pl.ds(pl.multiple_of((where_ref[0] ^ k) * width, 128), width)
        out[:block, :] = rows_ref[:, cols]
        out[block:, :] = own_ref[:, cols]


def column_pieces(where, rows_in, own, replicas):
    tokens, depth = rows_in.shape
    shape = (tokens + own.shape[0], depth // replicas)
    return pl.pallas_call(
        pieces_kernel,
        in_specs=[pl.BlockSpec(memory_space=pltpu.SMEM)] + whole_vmem(2),
        out_specs=whole_vmem(replicas),
        out_shape=[jax.ShapeDtypeStruct(shape, jnp.bfloat16)] * replicas,
        compiler_params=params(),
        name="column_pieces",
    )(where, rows_in, own)


def slice_kernel(replicas, where_ref, grads_ref, *refs):
    pieces, twin, out_ref = refs[:replicas], refs[replicas], refs[-1]
    tokens = twin.shape[0] // replicas
    core = where_ref[1] % 2
    left, right = [], []
    for other in range(2):
        for k in range(replicas):
            left.append(grads_ref[(where_ref[0] ^ k) * 2 + (core ^ other)])
            right.append(
                twin[k * tokens : (k + 1) * tokens, :] if other else pieces[k][:tokens, :]
            )
    total = contract(jnp.concatenate(left, axis=1), jnp.concatenate(right, axis=0), ((1,), (0,)))
    per = out_ref.shape[1]
    for z in range(out_ref.shape[0]):
        out_ref[z] = total[z * per : (z + 1) * per].astype(jnp.bfloat16)


def gradient_slice(where, grads, pieces, twin, chips):
    rows = grads.shape[1] // chips
    width = twin.shape[1]
    return pl.pallas_call(
        functools.partial(slice_kernel, len(pieces)),
        in_specs=[pl.BlockSpec(memory_space=pltpu.SMEM)] + whole_vmem(2 + len(pieces)),
        out_specs=pl.BlockSpec(memory_space=pltpu.VMEM),
        out_shape=jax.ShapeDtypeStruct((chips, rows, width), jnp.bfloat16),
        compiler_params=params(),
        name="gradient_slice",
    )(where, grads, *pieces, twin)


def stepped_kernel(sums_ref, *refs):
    pieces, out_ref = refs[:-1], refs[-1]
    replicas = len(pieces)
    rows = out_ref.shape[1]
    total = sums_ref[0].astype(jnp.float32)
    for z in range(1, sums_ref.shape[0]):
        total = total + sums_ref[z].astype(jnp.float32)
    level = pieces[0][-rows:, :].astype(jnp.float32)
    for piece in pieces[1:]:
        level = level + piece[-rows:, :].astype(jnp.float32)
    mean = ((level - inner_rate * total) * (1.0 / replicas)).astype(jnp.bfloat16)
    for r in range(replicas):
        out_ref[r] = mean


def stepped_slice(sums, pieces):
    _, rows, width = sums.shape
    return pl.pallas_call(
        stepped_kernel,
        in_specs=whole_vmem(1 + len(pieces)),
        out_specs=pl.BlockSpec(memory_space=pltpu.VMEM),
        out_shape=jax.ShapeDtypeStruct((len(pieces), rows, width), jnp.bfloat16),
        compiler_params=params(),
        name="stepped_slice",
    )(sums, *pieces)


def outer_kernel(stepped_ref, par_ref, mom_ref, new_par, new_mom):
    replicas, _, width = stepped_ref.shape
    for r in range(replicas):
        cols = slice(r * width, (r + 1) * width)
        old = par_ref[:, cols]
        pseudo = old - stepped_ref[r].astype(jnp.float32)
        fresh = momentum_decay * mom_ref[:, cols] + pseudo
        new_mom[:, cols] = fresh
        new_par[:, cols] = old - outer_rate * (pseudo + momentum_decay * fresh)


def outer_step(stepped, global_params, momentum):
    return pl.pallas_call(
        outer_kernel,
        in_specs=whole_vmem(3),
        out_specs=whole_vmem(2),
        out_shape=[jax.ShapeDtypeStruct(global_params.shape, jnp.float32)] * 2,
        compiler_params=params(),
        name="outer_step",
    )(stepped, global_params, momentum)


def on_device(
    sizes,
    block_input,
    ssd_input,
    out_grad,
    start_state,
    step_bias,
    decay_log,
    local_params,
    global_params,
    momentum,
):
    replicas, chips, cores = sizes
    local_rows = local_params[0]
    rows, depth = local_rows.shape
    own = local_rows.astype(jnp.bfloat16)
    seq_width = ssd_input.shape[1]
    blocks = start_state.shape[0]
    block = block_input.shape[0] // blocks
    fast = (
        cores == 2
        and chips == 4
        and rows % 8 == 0
        and replicas & (replicas - 1) == 0
        and depth % (128 * replicas) == 0
    )
    rep = lax.axis_index("rep")
    spot = lax.axis_index("line") * cores + lax.axis_index("core")
    where = jnp.stack([rep, spot]).astype(jnp.int32)

    def send(value, axis, k):
        count = dict(rep=replicas, line=chips, core=cores)[axis]
        return lax.ppermute(value, axis, [(i, i ^ k) for i in range(count)])

    if fast:
        near = send(own, "line", 1)
        far = send(own, "line", 3)
        middle = send(far, "line", 1)
        by_line = [own, near, far, middle]
        weights = by_line + [send(w, "core", 1) for w in by_line]
        order = (0, 2, 6, 4, 1, 3, 7, 5)
    else:
        weights = [lax.all_gather(own, ("line", "core"), axis=0, tiled=True)]
        order = (0,)

    grads, sends = [], []
    for b in range(blocks):
        seq = slice(b * block, (b + 1) * block)
        cross, enter = early_products(
            out_grad[seq], ssd_input[seq], start_state[b].reshape(seq_width, STATE)
        )
        grad, apart = ssd_backward(
            where, block_input[seq], step_bias, decay_log, cross, enter, weights, order, replicas
        )
        grads.append(grad)
        sends.append(apart)
    grad = grads[0] if blocks == 1 else jnp.concatenate(grads, axis=1)
    block_grad = block_gradient(grad, weights)

    if not fast:
        gradient = lax.psum_scatter(
            contract(grad, block_input, ((1,), (0,))),
            ("line", "core"),
            scatter_dimension=0,
            tiled=True,
        )
        pseudo = global_params - (local_rows - inner_rate * gradient)
        mean_pseudo = lax.psum(pseudo.astype(jnp.bfloat16), "rep").astype(jnp.float32) / replicas
        new_momentum = momentum_decay * momentum + mean_pseudo
        new_params = global_params - outer_rate * (mean_pseudo + momentum_decay * new_momentum)
        return (block_grad, new_params, new_momentum)

    apart = sends[0] if blocks == 1 else jnp.concatenate(sends, axis=2)
    tokens = blocks * block
    pieces = column_pieces(where, block_input, own, replicas)
    pieces = [pieces[0]] + [send(pieces[k], "rep", k) for k in range(1, replicas)]
    twin = send(jnp.concatenate([p[:tokens] for p in pieces], axis=0), "core", 1)

    def swap(value, axes):
        return lax.all_to_all(value, axes, split_axis=0, concat_axis=0, tiled=True)

    sums = gradient_slice(where, swap(apart, ("rep", "core")), pieces, twin, chips)
    stepped = stepped_slice(swap(sums, "line"), pieces)
    new_params, new_momentum = outer_step(swap(stepped, "rep"), global_params, momentum)
    return (block_grad, new_params, new_momentum)


def solution(mesh):
    replicas, shards = mesh.shape["rep"], mesh.shape["fsdp"]
    cores = 2 if shards % 2 == 0 else 1
    sizes = (replicas, shards // cores, cores)
    apart = jax.sharding.Mesh(mesh.devices.reshape(sizes), ("rep", "line", "core"))
    fsdp = ("line", "core")
    rows = P(("rep", "line", "core"), None)
    placed = (
        rows,
        rows,
        rows,
        P(("rep", "line", "core"), None, None),
        P(),
        P(),
        P("rep", fsdp, None),
        P(fsdp, None),
        P(fsdp, None),
    )
    return jax.shard_map(
        functools.partial(on_device, sizes),
        mesh=apart,
        in_specs=placed,
        out_specs=(rows, P(fsdp, None), P(fsdp, None)),
        check_vma=False,
    )
```

```python
import functools

import jax
import jax.numpy as jnp
from jax import lax
from jax.experimental import pallas as pl
from jax.experimental.pallas import tpu as pltpu
from jax.sharding import PartitionSpec as P

STATE = 64
LOG2E = 1.4426950408889634

inner_rate = 0.002
outer_rate = 0.7
momentum_decay = 0.9

VMEM_LIMIT = 48 * 1024 * 1024
EXACT = lax.Precision.HIGHEST


def params(**more):
    return pltpu.CompilerParams(vmem_limit_bytes=VMEM_LIMIT, **more)


def whole_vmem(count):
    return [pl.BlockSpec(memory_space=pltpu.VMEM)] * count


def contract(left, right, dims, precision=None):
    return lax.dot_general(
        left, right, (dims, ((), ())), preferred_element_type=jnp.float32, precision=precision
    )


def early_kernel(cot_ref, val_ref, state_ref, cross_ref, enter_ref):
    block = cot_ref.shape[0]
    lanes = lax.broadcasted_iota(jnp.int32, (block, 2 * STATE), 1)
    rows = lax.broadcasted_iota(jnp.int32, (block, block), 0)
    cols = lax.broadcasted_iota(jnp.int32, (block, block), 1)
    causal = rows >= cols
    low = lanes < STATE
    square = (2 * STATE, 2 * STATE)
    same_head = (lax.broadcasted_iota(jnp.int32, square, 0) < STATE) == (
        lax.broadcasted_iota(jnp.int32, square, 1) < STATE
    )
    for pair in range(cot_ref.shape[1] // (2 * STATE)):
        span = slice(pair * 2 * STATE, (pair + 1) * 2 * STATE)
        cot = cot_ref[:, span]
        val = val_ref[:, span]
        zero = jnp.zeros_like(cot)
        for odd in range(2):
            one = jnp.where(low, zero, cot) if odd else jnp.where(low, cot, zero)
            cross = contract(one, val, ((1,), (1,)))
            cross_ref[2 * pair + odd] = jnp.where(causal, cross, 0.0).astype(cross_ref.dtype)
        state = state_ref[span, :]
        wide = jnp.concatenate([state, state], axis=1)
        wide = jnp.where(same_head, wide, jnp.zeros_like(wide))
        enter_ref[:, span] = contract(cot, wide, ((1,), (0,)))


def early_products(out_grad, ssd_input, state, part, width):
    block = out_grad.shape[0]
    heads = width // STATE
    steps = 4
    piece = width // steps
    return pl.pallas_call(
        early_kernel,
        grid=(steps,),
        in_specs=[
            pl.BlockSpec((block, piece), lambda i: (0, part * steps + i)),
            pl.BlockSpec((block, piece), lambda i: (0, part * steps + i)),
            pl.BlockSpec((piece, STATE), lambda i: (part * steps + i, 0)),
        ],
        out_specs=[
            pl.BlockSpec((heads // steps, block, block), lambda i: (i, 0, 0)),
            pl.BlockSpec((block, piece), lambda i: (0, i)),
        ],
        out_shape=[
            jax.ShapeDtypeStruct((heads, block, block), jnp.bfloat16),
            jax.ShapeDtypeStruct((block, width), jnp.float32),
        ],
        compiler_params=params(),
        cost_estimate=pl.CostEstimate(
            flops=2 * block * width * 4 * block, bytes_accessed=8 * block * width, transcendentals=0
        ),
        name="early_products",
    )(out_grad, ssd_input, state)


def stacked(refs):
    if len(refs) == 1:
        return refs[0][...]
    return jnp.concatenate([r[...].astype(jnp.float32) for r in refs], axis=0).astype(jnp.bfloat16)


def shard_rows(index, k, rows):
    return pl.ds(pl.multiple_of((index ^ k) * rows, 8), rows)


def ssd_kernel(order, replicas, where_ref, rows_ref, bias_ref, decay_ref, *rest):
    shards = len(order)
    cross_refs, enter_refs, rest = rest[:2], rest[2:4], rest[4:]
    weight_refs = rest[:shards]
    grad_ref, send_ref, proj_ref, col_ref, out_ref = rest[shards:]
    block = rows_ref.shape[0]
    heads = bias_ref.shape[1]
    per = weight_refs[0].shape[0]
    arrived = contract(stacked(weight_refs), rows_ref[...], ((1,), (1,)))
    for at, k in enumerate(order):
        if shards > 1:
            proj_ref[shard_rows(where_ref[1], k, per), :] = arrived[at * per : (at + 1) * per]
        else:
            proj_ref[...] = arrived
    key_t = proj_ref[:STATE, :]
    query_t = proj_ref[STATE : 2 * STATE, :]
    bias_t = jnp.broadcast_to(bias_ref[...], (block, heads)).T
    rate = jnp.exp(jnp.broadcast_to(decay_ref[...], (block, heads)).T)
    raw = proj_ref[2 * STATE :, :] + bias_t
    step_t = jnp.maximum(raw, 0.0) + jnp.log1p(jnp.exp(-jnp.abs(raw)))
    up = lax.broadcasted_iota(jnp.int32, (block, block), 0)
    across = lax.broadcasted_iota(jnp.int32, (block, block), 1)
    before = jnp.where(up <= across, 1.0, 0.0)
    after = jnp.where(up >= across, 1.0, 0.0)
    cum_t = contract(-step_t * rate, before, ((1,), (0,)), EXACT) * LOG2E
    cum = cum_t.T
    step = step_t.T
    query = query_t.T
    scores = contract(query, key_t, ((1,), (0,)), EXACT)
    entered = jnp.exp2(cum)
    query_twice = jnp.concatenate([query, query], axis=1)
    low = lax.broadcasted_iota(jnp.int32, (block, 2 * STATE), 1) < STATE
    head_of = lax.broadcasted_iota(jnp.int32, (block, heads), 1)
    below = lax.broadcasted_iota(jnp.int32, (block, heads), 0) < STATE

    score_grad = jnp.zeros((block, block), jnp.float32)
    query_grad = jnp.zeros((block, 2 * STATE), jnp.float32)
    row_sums = jnp.zeros((block, heads), jnp.float32)
    for h0 in range(0, heads, 4):
        left, right = [], []
        for h in range(h0, h0 + 4):
            span = cum[:, h : h + 1] - cum_t[h : h + 1, :]
            cross = cross_refs[2 * h // heads][h % (heads // 2)]
            weight = cross.astype(jnp.float32) * jnp.exp2(jnp.minimum(span, 0.0))
            score_grad = score_grad + weight * step_t[h : h + 1, :]
            mixed = weight * scores
            col_ref[h : h + 1, :] = jnp.sum(mixed, axis=0, keepdims=True)
            left.append(mixed.astype(jnp.bfloat16))
            right.append(jnp.where(head_of == h, step, 0.0).astype(jnp.bfloat16))
        for h in range(h0, h0 + 4, 2):
            gain = jnp.where(low, entered[:, h : h + 1], entered[:, h + 1 : h + 2])
            at = h % (heads // 2) * STATE
            part = enter_refs[2 * h // heads][:, at : at + 2 * STATE] * gain
            query_grad = query_grad + part
            left.append((part * query_twice).astype(jnp.bfloat16))
            right.append(
                jnp.where(head_of == jnp.where(below, h, h + 1), 1.0, 0.0).astype(jnp.bfloat16)
            )
        row_sums = row_sums + contract(
            jnp.concatenate(left, axis=1), jnp.concatenate(right, axis=0), ((1,), (0,))
        )

    cols_t = col_ref[...]
    cum_grad = row_sums.T - step_t * cols_t
    later = contract(cum_grad, after, ((1,), (0,)), EXACT)
    step_grad = cols_t - rate * later
    raw_grad = step_grad / (1.0 + jnp.exp(-raw))
    out_ref[:STATE, :] = contract(query_t, score_grad, ((1,), (0,)), EXACT)
    query_all = (query_grad[:, :STATE] + query_grad[:, STATE:]).T
    out_ref[STATE : 2 * STATE, :] = query_all + contract(key_t, score_grad, ((1,), (1,)), EXACT)
    out_ref[2 * STATE :, :] = raw_grad
    if shards == 1:
        grad_ref[...] = out_ref[...].astype(jnp.bfloat16)
        send_ref[...] = jnp.zeros_like(send_ref)
        return
    for core in range(2):
        of_core = [
            out_ref[f * per : (f + 1) * per, :] for f in range(core, shards, 2)
        ]
        of_core = jnp.concatenate(of_core, axis=0).astype(jnp.bfloat16)
        for r in range(replicas):
            send_ref[2 * r + core] = of_core
    for at, k in enumerate(order):
        proj_ref[at * per : (at + 1) * per, :] = out_ref[shard_rows(where_ref[1], k, per), :]
    grad_ref[...] = proj_ref[...].astype(jnp.bfloat16)


def ssd_backward(where, rows_in, step_bias, decay_log, cross, enter, weights, order, replicas):
    block = rows_in.shape[0]
    heads = step_bias.shape[0]
    cols = sum(w.shape[0] for w in weights)
    apart = (2 * replicas, cols // 2, block) if len(order) > 1 else (16, 128)
    return pl.pallas_call(
        functools.partial(ssd_kernel, order, replicas),
        in_specs=[pl.BlockSpec(memory_space=pltpu.SMEM)] + whole_vmem(7 + len(order)),
        out_specs=whole_vmem(2),
        out_shape=[
            jax.ShapeDtypeStruct((cols, block), jnp.bfloat16),
            jax.ShapeDtypeStruct(apart, jnp.bfloat16),
        ],
        scratch_shapes=[
            pltpu.VMEM((cols, block), jnp.float32),
            pltpu.VMEM((heads, block), jnp.float32),
            pltpu.VMEM((cols, block), jnp.float32),
        ],
        compiler_params=params(),
        cost_estimate=pl.CostEstimate(
            flops=2 * block * cols * rows_in.shape[1],
            bytes_accessed=16 * rows_in.size,
            transcendentals=heads * block * block,
        ),
        name="ssd_backward",
    )(where, rows_in, step_bias.reshape(1, -1), decay_log.reshape(1, -1), *cross, *enter, *weights)


def block_grad_kernel(grad_ref, *refs):
    out_ref = refs[-1]
    weights = stacked(refs[:-1])
    out_ref[...] = contract(grad_ref[...].T, weights, ((1,), (0,))).astype(out_ref.dtype)


def block_gradient(grad, weights):
    depth = weights[0].shape[1]
    cols, block = grad.shape
    return pl.pallas_call(
        block_grad_kernel,
        in_specs=whole_vmem(1 + len(weights)),
        out_specs=pl.BlockSpec(memory_space=pltpu.VMEM),
        out_shape=jax.ShapeDtypeStruct((block, depth), jnp.bfloat16),
        compiler_params=params(),
        cost_estimate=pl.CostEstimate(
            flops=2 * block * cols * depth, bytes_accessed=4 * cols * depth, transcendentals=0
        ),
        name="block_gradient",
    )(grad, *weights)


def pieces_kernel(where_ref, rows_ref, own_ref, *outs):
    block = rows_ref.shape[0]
    width = outs[0].shape[1]
    for k, out in enumerate(outs):
        cols = pl.ds(pl.multiple_of((where_ref[0] ^ k) * width, 128), width)
        out[:block, :] = rows_ref[:, cols]
        out[block:, :] = own_ref[:, cols]


def column_pieces(where, rows_in, own, replicas):
    tokens, depth = rows_in.shape
    shape = (tokens + own.shape[0], depth // replicas)
    return pl.pallas_call(
        pieces_kernel,
        in_specs=[pl.BlockSpec(memory_space=pltpu.SMEM)] + whole_vmem(2),
        out_specs=whole_vmem(replicas),
        out_shape=[jax.ShapeDtypeStruct(shape, jnp.bfloat16)] * replicas,
        compiler_params=params(),
        name="column_pieces",
    )(where, rows_in, own)


def slice_kernel(replicas, where_ref, grads_ref, *refs):
    pieces, twin, outs, total = refs[:replicas], refs[replicas], refs[replicas + 1 : -1], refs[-1]
    tokens = twin.shape[0] // replicas
    core = where_ref[1] % 2
    left, right = [], []
    for other in range(2):
        for k in range(replicas):
            left.append(grads_ref[(where_ref[0] ^ k) * 2 + (core ^ other)])
            right.append(
                twin[k * tokens : (k + 1) * tokens, :] if other else pieces[k][:tokens, :]
            )
    total[...] = contract(
        jnp.concatenate(left, axis=1), jnp.concatenate(right, axis=0), ((1,), (0,))
    )
    per = outs[0].shape[0]
    chip = where_ref[1] // 2
    for k, out in enumerate(outs):
        out[...] = total[shard_rows(chip, k, per), :].astype(jnp.bfloat16)


def gradient_slice(where, grads, pieces, twin, chips):
    rows = grads.shape[1] // chips
    width = twin.shape[1]
    return pl.pallas_call(
        functools.partial(slice_kernel, len(pieces)),
        in_specs=[pl.BlockSpec(memory_space=pltpu.SMEM)] + whole_vmem(2 + len(pieces)),
        out_specs=whole_vmem(chips),
        out_shape=[jax.ShapeDtypeStruct((rows, width), jnp.bfloat16)] * chips,
        scratch_shapes=[pltpu.VMEM((rows * chips, width), jnp.float32)],
        compiler_params=params(),
        name="gradient_slice",
    )(where, grads, *pieces, twin)


def stepped_kernel(chips, *refs):
    sums, pieces, out_ref = refs[:chips], refs[chips:-1], refs[-1]
    rows = out_ref.shape[0]
    total = sums[0][...].astype(jnp.float32)
    for part in sums[1:]:
        total = total + part[...].astype(jnp.float32)
    level = pieces[0][-rows:, :].astype(jnp.float32)
    for piece in pieces[1:]:
        level = level + piece[-rows:, :].astype(jnp.float32)
    mean = (level - inner_rate * total) * (1.0 / len(pieces))
    out_ref[...] = mean.astype(jnp.bfloat16)


def stepped_slice(sums, pieces):
    return pl.pallas_call(
        functools.partial(stepped_kernel, len(sums)),
        in_specs=whole_vmem(len(sums) + len(pieces)),
        out_specs=pl.BlockSpec(memory_space=pltpu.VMEM),
        out_shape=jax.ShapeDtypeStruct(sums[0].shape, jnp.bfloat16),
        compiler_params=params(),
        name="stepped_slice",
    )(*sums, *pieces)


def outer_kernel(where_ref, par_ref, mom_ref, *refs):
    stepped, (new_par, new_mom) = refs[:-2], refs[-2:]
    width = stepped[0].shape[1]
    for k, part in enumerate(stepped):
        cols = pl.ds(pl.multiple_of((where_ref[0] ^ k) * width, 128), width)
        old = par_ref[:, cols]
        pseudo = old - part[...].astype(jnp.float32)
        fresh = momentum_decay * mom_ref[:, cols] + pseudo
        new_mom[:, cols] = fresh
        new_par[:, cols] = old - outer_rate * (pseudo + momentum_decay * fresh)


def outer_step(where, global_params, momentum, stepped):
    return pl.pallas_call(
        outer_kernel,
        in_specs=[pl.BlockSpec(memory_space=pltpu.SMEM)] + whole_vmem(2 + len(stepped)),
        out_specs=whole_vmem(2),
        out_shape=[jax.ShapeDtypeStruct(global_params.shape, jnp.float32)] * 2,
        compiler_params=params(),
        name="outer_step",
    )(where, global_params, momentum, *stepped)


def on_device(
    sizes,
    block_input,
    ssd_input,
    out_grad,
    start_state,
    step_bias,
    decay_log,
    local_params,
    global_params,
    momentum,
):
    replicas, chips, cores = sizes
    local_rows = local_params[0]
    rows, depth = local_rows.shape
    own = local_rows.astype(jnp.bfloat16)
    seq_width = ssd_input.shape[1]
    blocks = start_state.shape[0]
    block = block_input.shape[0] // blocks
    fast = (
        cores == 2
        and chips == 4
        and rows % 8 == 0
        and replicas & (replicas - 1) == 0
        and depth % (128 * replicas) == 0
    )
    rep = lax.axis_index("rep")
    spot = lax.axis_index("line") * cores + lax.axis_index("core")
    where = jnp.stack([rep, spot]).astype(jnp.int32)

    def send(value, axis, k):
        count = dict(rep=replicas, line=chips, core=cores)[axis]
        return lax.ppermute(value, axis, [(i, i ^ k) for i in range(count)])

    if fast:
        near = send(own, "line", 1)
        far = send(own, "line", 3)
        near, own_late = lax.optimization_barrier((near, own))
        order = (0, 2, 6, 4, 1, 3, 7, 5)
    else:
        weights = [lax.all_gather(own, ("line", "core"), axis=0, tiled=True)]
        order = (0,)

    early = [[], []]
    for b in range(blocks):
        seq = slice(b * block, (b + 1) * block)
        state = start_state[b].reshape(seq_width, STATE)
        for half in range(2):
            early[half].append(
                early_products(out_grad[seq], ssd_input[seq], state, half, seq_width // 2)
            )
    if fast:
        far, early[0] = lax.optimization_barrier((far, early[0]))
        middle = send(far, "line", 1)
        twins = [send(own, "core", 1), send(near, "core", 1)]
        middle, early[1], twins = lax.optimization_barrier((middle, early[1], twins))
        twins = twins + [send(far, "core", 1), send(middle, "core", 1)]
        weights = [own, near, far, middle] + twins

    grads, sends = [], []
    for b in range(blocks):
        seq = slice(b * block, (b + 1) * block)
        grad, apart = ssd_backward(
            where,
            block_input[seq],
            step_bias,
            decay_log,
            [early[0][b][0], early[1][b][0]],
            [early[0][b][1], early[1][b][1]],
            weights,
            order,
            replicas,
        )
        grads.append(grad)
        sends.append(apart)
    grad = grads[0] if blocks == 1 else jnp.concatenate(grads, axis=1)
    block_grad = block_gradient(grad, weights)

    if not fast:
        gradient = lax.psum_scatter(
            contract(grad, block_input, ((1,), (0,))),
            ("line", "core"),
            scatter_dimension=0,
            tiled=True,
        )
        pseudo = global_params - (local_rows - inner_rate * gradient)
        mean_pseudo = lax.psum(pseudo.astype(jnp.bfloat16), "rep").astype(jnp.float32) / replicas
        new_momentum = momentum_decay * momentum + mean_pseudo
        new_params = global_params - outer_rate * (mean_pseudo + momentum_decay * new_momentum)
        return (block_grad, new_params, new_momentum)

    apart = sends[0] if blocks == 1 else jnp.concatenate(sends, axis=2)
    tokens = blocks * block
    pieces = column_pieces(where, block_input, own_late, replicas)
    pieces = [pieces[0]] + [send(pieces[k], "rep", k) for k in range(1, replicas)]
    _, _, pieces = lax.optimization_barrier((middle, twins[2], pieces))
    twin = send(jnp.concatenate([p[:tokens] for p in pieces], axis=0), "core", 1)

    plane = lax.all_to_all(apart, ("rep", "core"), split_axis=0, concat_axis=0, tiled=True)
    sums = gradient_slice(where, plane, pieces, twin, chips)
    sums = [sums[0]] + [send(sums[k], "line", k) for k in range(1, chips)]
    stepped = stepped_slice(sums, pieces)
    stepped = [stepped] + [send(stepped, "rep", k) for k in range(1, replicas)]
    new_params, new_momentum = outer_step(where, global_params, momentum, stepped)
    return (block_grad, new_params, new_momentum)


def solution(mesh):
    replicas, shards = mesh.shape["rep"], mesh.shape["fsdp"]
    cores = 2 if shards % 2 == 0 else 1
    sizes = (replicas, shards // cores, cores)
    apart = jax.sharding.Mesh(mesh.devices.reshape(sizes), ("rep", "line", "core"))
    fsdp = ("line", "core")
    rows = P(("rep", "line", "core"), None)
    placed = (
        rows,
        rows,
        rows,
        P(("rep", "line", "core"), None, None),
        P(),
        P(),
        P("rep", fsdp, None),
        P(fsdp, None),
        P(fsdp, None),
    )
    return jax.shard_map(
        functools.partial(on_device, sizes),
        mesh=apart,
        in_specs=placed,
        out_specs=(rows, P(fsdp, None), P(fsdp, None)),
        check_vma=False,
    )
```

```python
import functools

import jax
import jax.numpy as jnp
from jax import lax
from jax.experimental import pallas as pl
from jax.experimental.pallas import tpu as pltpu
from jax.sharding import PartitionSpec as P

STATE = 64
LOG2E = 1.4426950408889634

inner_rate = 0.002
outer_rate = 0.7
momentum_decay = 0.9

VMEM_LIMIT = 48 * 1024 * 1024


def params(**more):
    return pltpu.CompilerParams(vmem_limit_bytes=VMEM_LIMIT, **more)


def whole_vmem(count):
    return [pl.BlockSpec(memory_space=pltpu.VMEM)] * count


def contract(left, right, dims):
    return lax.dot_general(left, right, (dims, ((), ())), preferred_element_type=jnp.float32)


def terms(value, count):
    out = []
    for _ in range(count):
        out.append(value.astype(jnp.bfloat16))
        value = value - out[-1].astype(jnp.float32)
    return out


def early_kernel(cot_ref, val_ref, state_ref, cross_ref, enter_ref):
    block = cot_ref.shape[0]
    lanes = lax.broadcasted_iota(jnp.int32, (block, 2 * STATE), 1)
    rows = lax.broadcasted_iota(jnp.int32, (block, block), 0)
    cols = lax.broadcasted_iota(jnp.int32, (block, block), 1)
    causal = rows >= cols
    low = lanes < STATE
    square = (2 * STATE, 2 * STATE)
    same_head = (lax.broadcasted_iota(jnp.int32, square, 0) < STATE) == (
        lax.broadcasted_iota(jnp.int32, square, 1) < STATE
    )
    for pair in range(cot_ref.shape[1] // (2 * STATE)):
        span = slice(pair * 2 * STATE, (pair + 1) * 2 * STATE)
        cot = cot_ref[:, span]
        val = val_ref[:, span]
        zero = jnp.zeros_like(cot)
        for odd in range(2):
            one = jnp.where(low, zero, cot) if odd else jnp.where(low, cot, zero)
            cross = contract(one, val, ((1,), (1,)))
            cross_ref[2 * pair + odd] = jnp.where(causal, cross, 0.0).astype(cross_ref.dtype)
        state = state_ref[span, :]
        wide = jnp.concatenate([state, state], axis=1)
        wide = jnp.where(same_head, wide, jnp.zeros_like(wide))
        enter_ref[:, span] = contract(cot, wide, ((1,), (0,)))


def early_products(out_grad, ssd_input, state, part, width):
    block = out_grad.shape[0]
    heads = width // STATE
    steps = 4
    piece = width // steps
    return pl.pallas_call(
        early_kernel,
        grid=(steps,),
        in_specs=[
            pl.BlockSpec((block, piece), lambda i: (0, part * steps + i)),
            pl.BlockSpec((block, piece), lambda i: (0, part * steps + i)),
            pl.BlockSpec((piece, STATE), lambda i: (part * steps + i, 0)),
        ],
        out_specs=[
            pl.BlockSpec((heads // steps, block, block), lambda i: (i, 0, 0)),
            pl.BlockSpec((block, piece), lambda i: (0, i)),
        ],
        out_shape=[
            jax.ShapeDtypeStruct((heads, block, block), jnp.bfloat16),
            jax.ShapeDtypeStruct((block, width), jnp.float32),
        ],
        compiler_params=params(),
        cost_estimate=pl.CostEstimate(
            flops=2 * block * width * 4 * block, bytes_accessed=8 * block * width, transcendentals=0
        ),
        name="early_products",
    )(out_grad, ssd_input, state)


def stacked(refs):
    if len(refs) == 1:
        return refs[0][...]
    return jnp.concatenate([r[...].astype(jnp.float32) for r in refs], axis=0).astype(jnp.bfloat16)


def shard_rows(index, k, rows):
    return pl.ds(pl.multiple_of((index ^ k) * rows, 8), rows)


def ssd_kernel(order, where_ref, rows_ref, bias_ref, decay_ref, *rest):
    shards = len(order)
    cross_refs, enter_refs, rest = rest[:2], rest[2:4], rest[4:]
    weight_refs = rest[:shards]
    grad_ref, mine_ref, other_ref, proj_ref, col_ref, out_ref = rest[shards:]
    block = rows_ref.shape[0]
    heads = bias_ref.shape[1]
    per = weight_refs[0].shape[0]
    arrived = contract(stacked(weight_refs), rows_ref[...], ((1,), (1,)))
    for at, k in enumerate(order):
        if shards > 1:
            proj_ref[shard_rows(where_ref[1], k, per), :] = arrived[at * per : (at + 1) * per]
        else:
            proj_ref[...] = arrived
    key_t = proj_ref[:STATE, :]
    query_t = proj_ref[STATE : 2 * STATE, :]
    bias_t = jnp.broadcast_to(bias_ref[...], (block, heads)).T
    rate = jnp.exp(jnp.broadcast_to(decay_ref[...], (block, heads)).T)
    raw = proj_ref[2 * STATE :, :] + bias_t
    step_t = jnp.maximum(raw, 0.0) + jnp.log1p(jnp.exp(-jnp.abs(raw)))
    up = lax.broadcasted_iota(jnp.int32, (block, block), 0)
    across = lax.broadcasted_iota(jnp.int32, (block, block), 1)
    before = jnp.where(up <= across, 1.0, 0.0).astype(jnp.bfloat16)
    after = jnp.where(up >= across, 1.0, 0.0).astype(jnp.bfloat16)
    cum_t = LOG2E * contract(
        jnp.concatenate(terms(-step_t * rate, 3), axis=1),
        jnp.concatenate([before] * 3, axis=0),
        ((1,), (0,)),
    )
    cum = cum_t.T
    step = step_t.T
    query = query_t.T
    query_high, query_low = terms(query, 2)
    key_high, key_low = terms(key_t, 2)
    scores = contract(
        jnp.concatenate([query_high, query_high, query_low], axis=1),
        jnp.concatenate([key_high, key_low, key_high], axis=0),
        ((1,), (0,)),
    )
    entered = jnp.exp2(cum)
    query_twice = jnp.concatenate([query, query], axis=1)
    low = lax.broadcasted_iota(jnp.int32, (block, 2 * STATE), 1) < STATE
    head_of = lax.broadcasted_iota(jnp.int32, (block, heads), 1)
    below = lax.broadcasted_iota(jnp.int32, (block, heads), 0) < STATE

    score_grad = jnp.zeros((block, block), jnp.float32)
    query_grad = jnp.zeros((block, 2 * STATE), jnp.float32)
    row_sums = jnp.zeros((block, heads), jnp.float32)
    for h0 in range(0, heads, 4):
        left, right = [], []
        for h in range(h0, h0 + 4):
            span = cum[:, h : h + 1] - cum_t[h : h + 1, :]
            cross = cross_refs[2 * h // heads][h % (heads // 2)]
            weight = cross.astype(jnp.float32) * jnp.exp2(jnp.minimum(span, 0.0))
            score_grad = score_grad + weight * step_t[h : h + 1, :]
            mixed = weight * scores
            col_ref[h : h + 1, :] = jnp.sum(mixed, axis=0, keepdims=True)
            left.append(mixed.astype(jnp.bfloat16))
            right.append(jnp.where(head_of == h, step, 0.0).astype(jnp.bfloat16))
        for h in range(h0, h0 + 4, 2):
            gain = jnp.where(low, entered[:, h : h + 1], entered[:, h + 1 : h + 2])
            at = h % (heads // 2) * STATE
            part = enter_refs[2 * h // heads][:, at : at + 2 * STATE] * gain
            query_grad = query_grad + part
            left.append((part * query_twice).astype(jnp.bfloat16))
            right.append(
                jnp.where(head_of == jnp.where(below, h, h + 1), 1.0, 0.0).astype(jnp.bfloat16)
            )
        row_sums = row_sums + contract(
            jnp.concatenate(left, axis=1), jnp.concatenate(right, axis=0), ((1,), (0,))
        )

    cols_t = col_ref[...]
    cum_grad = row_sums.T - step_t * cols_t
    later = contract(
        jnp.concatenate(terms(cum_grad, 2), axis=1),
        jnp.concatenate([after] * 2, axis=0),
        ((1,), (0,)),
    )
    step_grad = cols_t - rate * later
    raw_grad = step_grad / (1.0 + jnp.exp(-raw))
    score_grad = score_grad.astype(jnp.bfloat16)
    out_ref[:STATE, :] = contract(query_t.astype(jnp.bfloat16), score_grad, ((1,), (0,)))
    query_all = (query_grad[:, :STATE] + query_grad[:, STATE:]).T
    out_ref[STATE : 2 * STATE, :] = query_all + contract(key_high, score_grad, ((1,), (1,)))
    out_ref[2 * STATE :, :] = raw_grad
    if shards == 1:
        grad_ref[...] = out_ref[...].astype(jnp.bfloat16)
        mine_ref[...] = jnp.zeros_like(mine_ref)
        other_ref[...] = jnp.zeros_like(other_ref)
        return
    core = where_ref[1] % 2
    for part, ref in ((core, mine_ref), (1 - core, other_ref)):
        of_core = [out_ref[shard_rows(f + part, 0, per), :] for f in range(0, shards, 2)]
        ref[...] = jnp.concatenate(of_core, axis=0).astype(jnp.bfloat16)
    for at, k in enumerate(order):
        proj_ref[at * per : (at + 1) * per, :] = out_ref[shard_rows(where_ref[1], k, per), :]
    grad_ref[...] = proj_ref[...].astype(jnp.bfloat16)


def ssd_backward(where, rows_in, step_bias, decay_log, cross, enter, weights, order):
    block = rows_in.shape[0]
    heads = step_bias.shape[0]
    cols = sum(w.shape[0] for w in weights)
    half = (cols // 2, block)
    return pl.pallas_call(
        functools.partial(ssd_kernel, order),
        in_specs=[pl.BlockSpec(memory_space=pltpu.SMEM)] + whole_vmem(7 + len(order)),
        out_specs=whole_vmem(3),
        out_shape=[
            jax.ShapeDtypeStruct((cols, block), jnp.bfloat16),
            jax.ShapeDtypeStruct(half, jnp.bfloat16),
            jax.ShapeDtypeStruct(half, jnp.bfloat16),
        ],
        scratch_shapes=[
            pltpu.VMEM((cols, block), jnp.float32),
            pltpu.VMEM((heads, block), jnp.float32),
            pltpu.VMEM((cols, block), jnp.float32),
        ],
        compiler_params=params(),
        cost_estimate=pl.CostEstimate(
            flops=2 * block * cols * rows_in.shape[1],
            bytes_accessed=16 * rows_in.size,
            transcendentals=heads * block * block,
        ),
        name="ssd_backward",
    )(where, rows_in, step_bias.reshape(1, -1), decay_log.reshape(1, -1), *cross, *enter, *weights)


def block_grad_kernel(grad_ref, *refs):
    out_ref = refs[-1]
    weights = stacked(refs[:-1])
    out_ref[...] = contract(grad_ref[...].T, weights, ((1,), (0,))).astype(out_ref.dtype)


def block_gradient(grad, weights):
    depth = weights[0].shape[1]
    cols, block = grad.shape
    return pl.pallas_call(
        block_grad_kernel,
        in_specs=whole_vmem(1 + len(weights)),
        out_specs=pl.BlockSpec(memory_space=pltpu.VMEM),
        out_shape=jax.ShapeDtypeStruct((block, depth), jnp.bfloat16),
        compiler_params=params(),
        cost_estimate=pl.CostEstimate(
            flops=2 * block * cols * depth, bytes_accessed=4 * cols * depth, transcendentals=0
        ),
        name="block_gradient",
    )(grad, *weights)


def pieces_kernel(where_ref, rows_ref, own_ref, *outs):
    block = rows_ref.shape[0]
    width = outs[0].shape[1]
    for k, out in enumerate(outs):
        cols = pl.ds(pl.multiple_of((where_ref[0] ^ k) * width, 128), width)
        out[:block, :] = rows_ref[:, cols]
        out[block:, :] = own_ref[:, cols]


def column_pieces(where, rows_in, own, replicas):
    tokens, depth = rows_in.shape
    shape = (tokens + own.shape[0], depth // replicas)
    return pl.pallas_call(
        pieces_kernel,
        in_specs=[pl.BlockSpec(memory_space=pltpu.SMEM)] + whole_vmem(2),
        out_specs=whole_vmem(replicas),
        out_shape=[jax.ShapeDtypeStruct(shape, jnp.bfloat16)] * replicas,
        compiler_params=params(),
        name="column_pieces",
    )(where, rows_in, own)


def slice_kernel(replicas, where_ref, *refs):
    grads, pieces, refs = refs[:replicas], refs[replicas : 2 * replicas], refs[2 * replicas :]
    twin, outs, total = refs[0], refs[1:-1], refs[-1]
    tokens = twin.shape[0] // replicas
    rows = total.shape[0]
    left, right = [], []
    for other in range(2):
        for k in range(replicas):
            left.append(grads[k][other * rows : (other + 1) * rows, :])
            right.append(
                twin[k * tokens : (k + 1) * tokens, :] if other else pieces[k][:tokens, :]
            )
    total[...] = contract(
        jnp.concatenate(left, axis=1), jnp.concatenate(right, axis=0), ((1,), (0,))
    )
    per = outs[0].shape[0]
    chip = where_ref[1] // 2
    for k, out in enumerate(outs):
        out[...] = total[shard_rows(chip, k, per), :].astype(jnp.bfloat16)


def gradient_slice(where, grads, pieces, twin, chips):
    rows = grads[0].shape[0] // (2 * chips)
    width = twin.shape[1]
    return pl.pallas_call(
        functools.partial(slice_kernel, len(pieces)),
        in_specs=[pl.BlockSpec(memory_space=pltpu.SMEM)] + whole_vmem(1 + 2 * len(pieces)),
        out_specs=whole_vmem(chips),
        out_shape=[jax.ShapeDtypeStruct((rows, width), jnp.bfloat16)] * chips,
        scratch_shapes=[pltpu.VMEM((rows * chips, width), jnp.float32)],
        compiler_params=params(),
        name="gradient_slice",
    )(where, *grads, *pieces, twin)


def stepped_kernel(chips, *refs):
    sums, pieces, out_ref = refs[:chips], refs[chips:-1], refs[-1]
    rows = out_ref.shape[0]
    total = sums[0][...].astype(jnp.float32)
    for part in sums[1:]:
        total = total + part[...].astype(jnp.float32)
    level = pieces[0][-rows:, :].astype(jnp.float32)
    for piece in pieces[1:]:
        level = level + piece[-rows:, :].astype(jnp.float32)
    mean = (level - inner_rate * total) * (1.0 / len(pieces))
    out_ref[...] = mean.astype(jnp.bfloat16)


def stepped_slice(sums, pieces):
    return pl.pallas_call(
        functools.partial(stepped_kernel, len(sums)),
        in_specs=whole_vmem(len(sums) + len(pieces)),
        out_specs=pl.BlockSpec(memory_space=pltpu.VMEM),
        out_shape=jax.ShapeDtypeStruct(sums[0].shape, jnp.bfloat16),
        compiler_params=params(),
        name="stepped_slice",
    )(*sums, *pieces)


def outer_kernel(where_ref, par_ref, mom_ref, *refs):
    stepped, (new_par, new_mom) = refs[:-2], refs[-2:]
    width = stepped[0].shape[1]
    for k, part in enumerate(stepped):
        cols = pl.ds(pl.multiple_of((where_ref[0] ^ k) * width, 128), width)
        old = par_ref[:, cols]
        pseudo = old - part[...].astype(jnp.float32)
        fresh = momentum_decay * mom_ref[:, cols] + pseudo
        new_mom[:, cols] = fresh
        new_par[:, cols] = old - outer_rate * (pseudo + momentum_decay * fresh)


def outer_step(where, global_params, momentum, stepped):
    return pl.pallas_call(
        outer_kernel,
        in_specs=[pl.BlockSpec(memory_space=pltpu.SMEM)] + whole_vmem(2 + len(stepped)),
        out_specs=whole_vmem(2),
        out_shape=[jax.ShapeDtypeStruct(global_params.shape, jnp.float32)] * 2,
        compiler_params=params(),
        name="outer_step",
    )(where, global_params, momentum, *stepped)


def on_device(
    sizes,
    block_input,
    ssd_input,
    out_grad,
    start_state,
    step_bias,
    decay_log,
    local_params,
    global_params,
    momentum,
):
    replicas, chips, cores = sizes
    local_rows = local_params[0]
    rows, depth = local_rows.shape
    own = local_rows.astype(jnp.bfloat16)
    seq_width = ssd_input.shape[1]
    blocks = start_state.shape[0]
    block = block_input.shape[0] // blocks
    fast = (
        cores == 2
        and chips == 4
        and rows % 8 == 0
        and replicas & (replicas - 1) == 0
        and depth % (128 * replicas) == 0
    )
    rep = lax.axis_index("rep")
    spot = lax.axis_index("line") * cores + lax.axis_index("core")
    where = jnp.stack([rep, spot]).astype(jnp.int32)

    def send(value, axis, k):
        count = dict(rep=replicas, line=chips, core=cores)[axis]
        return lax.ppermute(value, axis, [(i, i ^ k) for i in range(count)])

    if fast:
        near = send(own, "line", 1)
        far = send(own, "line", 3)
        order = (0, 2, 6, 4, 1, 3, 7, 5)
    else:
        weights = [lax.all_gather(own, ("line", "core"), axis=0, tiled=True)]
        order = (0,)

    early = [[], []]
    states = [start_state[b].reshape(seq_width, STATE) for b in range(blocks)]
    states, own_late = lax.optimization_barrier((states, own))
    for b in range(blocks):
        seq = slice(b * block, (b + 1) * block)
        for half in range(2):
            early[half].append(
                early_products(out_grad[seq], ssd_input[seq], states[b], half, seq_width // 2)
            )
    if fast:
        pieces = column_pieces(where, block_input, own_late, replicas)
        far, _ = lax.optimization_barrier((far, pieces))
        pieces = [pieces[0]] + [send(pieces[k], "rep", k) for k in range(1, replicas)]
        middle = send(far, "line", 1)
        twins = [send(own, "core", 1), send(near, "core", 1)]
        middle, early, twins = lax.optimization_barrier((middle, early, twins))
        twins = twins + [send(far, "core", 1), send(middle, "core", 1)]
        weights = [own, near, far, middle] + twins

    grads, mine, other = [], [], []
    for b in range(blocks):
        seq = slice(b * block, (b + 1) * block)
        parts = ssd_backward(
            where,
            block_input[seq],
            step_bias,
            decay_log,
            [early[0][b][0], early[1][b][0]],
            [early[0][b][1], early[1][b][1]],
            weights,
            order,
        )
        for kept, part in zip((grads, mine, other), parts):
            kept.append(part)
    grad, mine, other = (
        kept[0] if blocks == 1 else jnp.concatenate(kept, axis=1) for kept in (grads, mine, other)
    )
    block_grad = block_gradient(grad, weights)

    if not fast:
        gradient = lax.psum_scatter(
            contract(grad, block_input, ((1,), (0,))),
            ("line", "core"),
            scatter_dimension=0,
            tiled=True,
        )
        pseudo = global_params - (local_rows - inner_rate * gradient)
        mean_pseudo = lax.psum(pseudo.astype(jnp.bfloat16), "rep").astype(jnp.float32) / replicas
        new_momentum = momentum_decay * momentum + mean_pseudo
        new_params = global_params - outer_rate * (mean_pseudo + momentum_decay * new_momentum)
        return (block_grad, new_params, new_momentum)

    tokens = blocks * block
    mine, pieces = lax.optimization_barrier((mine, pieces))
    twin = send(jnp.concatenate([p[:tokens] for p in pieces], axis=0), "core", 1)

    both = jnp.concatenate([mine, send(other, "core", 1)], axis=0)
    plane = [both] + [send(both, "rep", k) for k in range(1, replicas)]
    sums = gradient_slice(where, plane, pieces, twin, chips)
    sums = [sums[0]] + [send(sums[k], "line", k) for k in range(1, chips)]
    stepped = stepped_slice(sums, pieces)
    stepped = [stepped] + [send(stepped, "rep", k) for k in range(1, replicas)]
    new_params, new_momentum = outer_step(where, global_params, momentum, stepped)
    return (block_grad, new_params, new_momentum)


def solution(mesh):
    replicas, shards = mesh.shape["rep"], mesh.shape["fsdp"]
    cores = 2 if shards % 2 == 0 else 1
    sizes = (replicas, shards // cores, cores)
    apart = jax.sharding.Mesh(mesh.devices.reshape(sizes), ("rep", "line", "core"))
    fsdp = ("line", "core")
    rows = P(("rep", "line", "core"), None)
    placed = (
        rows,
        rows,
        rows,
        P(("rep", "line", "core"), None, None),
        P(),
        P(),
        P("rep", fsdp, None),
        P(fsdp, None),
        P(fsdp, None),
    )
    return jax.shard_map(
        functools.partial(on_device, sizes),
        mesh=apart,
        in_specs=placed,
        out_specs=(rows, P(fsdp, None), P(fsdp, None)),
        check_vma=False,
    )
```

```python
import functools

import jax
import jax.numpy as jnp
from jax import lax
from jax.experimental import pallas as pl
from jax.experimental.pallas import tpu as pltpu
from jax.sharding import PartitionSpec as P

STATE = 64
LOG2E = 1.4426950408889634

inner_rate = 0.002
outer_rate = 0.7
momentum_decay = 0.9

VMEM_LIMIT = 48 * 1024 * 1024


def params(**more):
    return pltpu.CompilerParams(vmem_limit_bytes=VMEM_LIMIT, **more)


def whole_vmem(count):
    return [pl.BlockSpec(memory_space=pltpu.VMEM)] * count


def contract(left, right, dims):
    return lax.dot_general(left, right, (dims, ((), ())), preferred_element_type=jnp.float32)


def terms(value, count):
    out = []
    for _ in range(count):
        out.append(value.astype(jnp.bfloat16))
        value = value - out[-1].astype(jnp.float32)
    return out


def early_kernel(cot_ref, val_ref, state_ref, cross_ref, enter_ref):
    block = cot_ref.shape[0]
    lanes = lax.broadcasted_iota(jnp.int32, (block, 2 * STATE), 1)
    rows = lax.broadcasted_iota(jnp.int32, (block, block), 0)
    cols = lax.broadcasted_iota(jnp.int32, (block, block), 1)
    causal = rows >= cols
    low = lanes < STATE
    square = (2 * STATE, 2 * STATE)
    same_head = (lax.broadcasted_iota(jnp.int32, square, 0) < STATE) == (
        lax.broadcasted_iota(jnp.int32, square, 1) < STATE
    )
    for pair in range(cot_ref.shape[1] // (2 * STATE)):
        span = slice(pair * 2 * STATE, (pair + 1) * 2 * STATE)
        cot = cot_ref[:, span]
        val = val_ref[:, span]
        zero = jnp.zeros_like(cot)
        for odd in range(2):
            one = jnp.where(low, zero, cot) if odd else jnp.where(low, cot, zero)
            cross = contract(one, val, ((1,), (1,)))
            cross_ref[2 * pair + odd] = jnp.where(causal, cross, 0.0).astype(cross_ref.dtype)
        state = state_ref[span, :]
        wide = jnp.concatenate([state, state], axis=1)
        wide = jnp.where(same_head, wide, jnp.zeros_like(wide))
        enter_ref[:, span] = contract(cot, wide, ((1,), (0,)))


def early_products(out_grad, ssd_input, state, part, width):
    block = out_grad.shape[0]
    heads = width // STATE
    steps = 4
    piece = width // steps
    return pl.pallas_call(
        early_kernel,
        grid=(steps,),
        in_specs=[
            pl.BlockSpec((block, piece), lambda i: (0, part * steps + i)),
            pl.BlockSpec((block, piece), lambda i: (0, part * steps + i)),
            pl.BlockSpec((piece, STATE), lambda i: (part * steps + i, 0)),
        ],
        out_specs=[
            pl.BlockSpec((heads // steps, block, block), lambda i: (i, 0, 0)),
            pl.BlockSpec((block, piece), lambda i: (0, i)),
        ],
        out_shape=[
            jax.ShapeDtypeStruct((heads, block, block), jnp.bfloat16),
            jax.ShapeDtypeStruct((block, width), jnp.float32),
        ],
        compiler_params=params(),
        cost_estimate=pl.CostEstimate(flops=1, bytes_accessed=1, transcendentals=0),
        name="early_products",
    )(out_grad, ssd_input, state)


def stacked(refs):
    if len(refs) == 1:
        return refs[0][...]
    return jnp.concatenate([r[...].astype(jnp.float32) for r in refs], axis=0).astype(jnp.bfloat16)


def shard_rows(index, k, rows):
    return pl.ds(pl.multiple_of((index ^ k) * rows, 8), rows)


def ssd_kernel(order, where_ref, rows_ref, bias_ref, decay_ref, *rest):
    shards = len(order)
    cross_refs, enter_refs, rest = rest[:2], rest[2:4], rest[4:]
    weight_refs = rest[:shards]
    grad_ref, mine_ref, other_ref, proj_ref, col_ref, out_ref = rest[shards:]
    block = rows_ref.shape[0]
    heads = bias_ref.shape[1]
    per = weight_refs[0].shape[0]
    arrived = contract(stacked(weight_refs), rows_ref[...], ((1,), (1,)))
    for at, k in enumerate(order):
        if shards > 1:
            proj_ref[shard_rows(where_ref[1], k, per), :] = arrived[at * per : (at + 1) * per]
        else:
            proj_ref[...] = arrived
    key_t = proj_ref[:STATE, :]
    query_t = proj_ref[STATE : 2 * STATE, :]
    bias_t = jnp.broadcast_to(bias_ref[...], (block, heads)).T
    rate = jnp.exp(jnp.broadcast_to(decay_ref[...], (block, heads)).T)
    raw = proj_ref[2 * STATE :, :] + bias_t
    step_t = jnp.maximum(raw, 0.0) + jnp.log1p(jnp.exp(-jnp.abs(raw)))
    up = lax.broadcasted_iota(jnp.int32, (block, block), 0)
    across = lax.broadcasted_iota(jnp.int32, (block, block), 1)
    before = jnp.where(up <= across, 1.0, 0.0).astype(jnp.bfloat16)
    after = jnp.where(up >= across, 1.0, 0.0).astype(jnp.bfloat16)
    cum_t = LOG2E * contract(
        jnp.concatenate(terms(-step_t * rate, 3), axis=1),
        jnp.concatenate([before] * 3, axis=0),
        ((1,), (0,)),
    )
    cum = cum_t.T
    step = step_t.T
    query = query_t.T
    query_high, query_low = terms(query, 2)
    key_high, key_low = terms(key_t, 2)
    scores = contract(
        jnp.concatenate([query_high, query_high, query_low], axis=1),
        jnp.concatenate([key_high, key_low, key_high], axis=0),
        ((1,), (0,)),
    )
    entered = jnp.exp2(cum)
    query_twice = jnp.concatenate([query, query], axis=1)
    low = lax.broadcasted_iota(jnp.int32, (block, 2 * STATE), 1) < STATE
    head_of = lax.broadcasted_iota(jnp.int32, (block, heads), 1)
    below = lax.broadcasted_iota(jnp.int32, (block, heads), 0) < STATE

    score_grad = jnp.zeros((block, block), jnp.float32)
    query_grad = jnp.zeros((block, 2 * STATE), jnp.float32)
    row_sums = jnp.zeros((block, heads), jnp.float32)
    for h0 in range(0, heads, 4):
        left, right = [], []
        for h in range(h0, h0 + 4):
            span = cum[:, h : h + 1] - cum_t[h : h + 1, :]
            cross = cross_refs[2 * h // heads][h % (heads // 2)]
            weight = cross.astype(jnp.float32) * jnp.exp2(jnp.minimum(span, 0.0))
            score_grad = score_grad + weight * step_t[h : h + 1, :]
            mixed = weight * scores
            col_ref[h : h + 1, :] = jnp.sum(mixed, axis=0, keepdims=True)
            left.append(mixed.astype(jnp.bfloat16))
            right.append(jnp.where(head_of == h, step, 0.0).astype(jnp.bfloat16))
        for h in range(h0, h0 + 4, 2):
            gain = jnp.where(low, entered[:, h : h + 1], entered[:, h + 1 : h + 2])
            at = h % (heads // 2) * STATE
            part = enter_refs[2 * h // heads][:, at : at + 2 * STATE] * gain
            query_grad = query_grad + part
            left.append((part * query_twice).astype(jnp.bfloat16))
            right.append(
                jnp.where(head_of == jnp.where(below, h, h + 1), 1.0, 0.0).astype(jnp.bfloat16)
            )
        row_sums = row_sums + contract(
            jnp.concatenate(left, axis=1), jnp.concatenate(right, axis=0), ((1,), (0,))
        )

    cols_t = col_ref[...]
    cum_grad = row_sums.T - step_t * cols_t
    later = contract(
        jnp.concatenate(terms(cum_grad, 2), axis=1),
        jnp.concatenate([after] * 2, axis=0),
        ((1,), (0,)),
    )
    step_grad = cols_t - rate * later
    raw_grad = step_grad / (1.0 + jnp.exp(-raw))
    score_grad = score_grad.astype(jnp.bfloat16)
    out_ref[:STATE, :] = contract(query_t.astype(jnp.bfloat16), score_grad, ((1,), (0,)))
    query_all = (query_grad[:, :STATE] + query_grad[:, STATE:]).T
    out_ref[STATE : 2 * STATE, :] = query_all + contract(key_high, score_grad, ((1,), (1,)))
    out_ref[2 * STATE :, :] = raw_grad
    if shards == 1:
        grad_ref[...] = out_ref[...].astype(jnp.bfloat16)
        mine_ref[...] = jnp.zeros_like(mine_ref)
        other_ref[...] = jnp.zeros_like(other_ref)
        return
    core = where_ref[1] % 2
    for part, ref in ((core, mine_ref), (1 - core, other_ref)):
        of_core = [out_ref[shard_rows(f + part, 0, per), :] for f in range(0, shards, 2)]
        ref[...] = jnp.concatenate(of_core, axis=0).astype(jnp.bfloat16)
    for at, k in enumerate(order):
        proj_ref[at * per : (at + 1) * per, :] = out_ref[shard_rows(where_ref[1], k, per), :]
    grad_ref[...] = proj_ref[...].astype(jnp.bfloat16)


def ssd_backward(where, rows_in, step_bias, decay_log, cross, enter, weights, order):
    block = rows_in.shape[0]
    heads = step_bias.shape[0]
    cols = sum(w.shape[0] for w in weights)
    half = (cols // 2, block)
    return pl.pallas_call(
        functools.partial(ssd_kernel, order),
        in_specs=[pl.BlockSpec(memory_space=pltpu.SMEM)] + whole_vmem(7 + len(order)),
        out_specs=whole_vmem(3),
        out_shape=[
            jax.ShapeDtypeStruct((cols, block), jnp.bfloat16),
            jax.ShapeDtypeStruct(half, jnp.bfloat16),
            jax.ShapeDtypeStruct(half, jnp.bfloat16),
        ],
        scratch_shapes=[
            pltpu.VMEM((cols, block), jnp.float32),
            pltpu.VMEM((heads, block), jnp.float32),
            pltpu.VMEM((cols, block), jnp.float32),
        ],
        compiler_params=params(),
        cost_estimate=pl.CostEstimate(flops=1, bytes_accessed=1, transcendentals=0),
        name="ssd_backward",
    )(where, rows_in, step_bias.reshape(1, -1), decay_log.reshape(1, -1), *cross, *enter, *weights)


def block_grad_kernel(grad_ref, *refs):
    out_ref = refs[-1]
    weights = stacked(refs[:-1])
    out_ref[...] = contract(grad_ref[...].T, weights, ((1,), (0,))).astype(out_ref.dtype)


def block_gradient(grad, weights):
    depth = weights[0].shape[1]
    cols, block = grad.shape
    return pl.pallas_call(
        block_grad_kernel,
        in_specs=whole_vmem(1 + len(weights)),
        out_specs=pl.BlockSpec(memory_space=pltpu.VMEM),
        out_shape=jax.ShapeDtypeStruct((block, depth), jnp.bfloat16),
        compiler_params=params(),
        cost_estimate=pl.CostEstimate(
            flops=2 * block * cols * depth, bytes_accessed=4 * cols * depth, transcendentals=0
        ),
        name="block_gradient",
    )(grad, *weights)


def pieces_kernel(where_ref, rows_ref, own_ref, *outs):
    block = rows_ref.shape[0]
    width = outs[0].shape[1]
    for k, out in enumerate(outs):
        cols = pl.ds(pl.multiple_of((where_ref[0] ^ k) * width, 128), width)
        out[:block, :] = rows_ref[:, cols]
        out[block:, :] = own_ref[:, cols]


def column_pieces(where, rows_in, own, replicas):
    tokens, depth = rows_in.shape
    shape = (tokens + own.shape[0], depth // replicas)
    return pl.pallas_call(
        pieces_kernel,
        in_specs=[pl.BlockSpec(memory_space=pltpu.SMEM)] + whole_vmem(2),
        out_specs=whole_vmem(replicas),
        out_shape=[jax.ShapeDtypeStruct(shape, jnp.bfloat16)] * replicas,
        compiler_params=params(),
        name="column_pieces",
    )(where, rows_in, own)


def slice_kernel(replicas, where_ref, *refs):
    grads, pieces, refs = refs[:replicas], refs[replicas : 2 * replicas], refs[2 * replicas :]
    twin, outs, total = refs[0], refs[1:-1], refs[-1]
    tokens = twin.shape[0] // replicas
    rows = total.shape[0]
    left, right = [], []
    for other in range(2):
        for k in range(replicas):
            left.append(grads[k][other * rows : (other + 1) * rows, :])
            right.append(
                twin[k * tokens : (k + 1) * tokens, :] if other else pieces[k][:tokens, :]
            )
    total[...] = contract(
        jnp.concatenate(left, axis=1), jnp.concatenate(right, axis=0), ((1,), (0,))
    )
    per = outs[0].shape[0]
    chip = where_ref[1] // 2
    for k, out in enumerate(outs):
        out[...] = total[shard_rows(chip, k, per), :].astype(jnp.bfloat16)


def gradient_slice(where, grads, pieces, twin, chips):
    rows = grads[0].shape[0] // (2 * chips)
    width = twin.shape[1]
    return pl.pallas_call(
        functools.partial(slice_kernel, len(pieces)),
        in_specs=[pl.BlockSpec(memory_space=pltpu.SMEM)] + whole_vmem(1 + 2 * len(pieces)),
        out_specs=whole_vmem(chips),
        out_shape=[jax.ShapeDtypeStruct((rows, width), jnp.bfloat16)] * chips,
        scratch_shapes=[pltpu.VMEM((rows * chips, width), jnp.float32)],
        compiler_params=params(),
        name="gradient_slice",
    )(where, *grads, *pieces, twin)


def stepped_kernel(chips, *refs):
    sums, pieces, out_ref = refs[:chips], refs[chips:-1], refs[-1]
    rows = out_ref.shape[0]
    total = sums[0][...].astype(jnp.float32)
    for part in sums[1:]:
        total = total + part[...].astype(jnp.float32)
    level = pieces[0][-rows:, :].astype(jnp.float32)
    for piece in pieces[1:]:
        level = level + piece[-rows:, :].astype(jnp.float32)
    mean = (level - inner_rate * total) * (1.0 / len(pieces))
    out_ref[...] = mean.astype(jnp.bfloat16)


def stepped_slice(sums, pieces):
    return pl.pallas_call(
        functools.partial(stepped_kernel, len(sums)),
        in_specs=whole_vmem(len(sums) + len(pieces)),
        out_specs=pl.BlockSpec(memory_space=pltpu.VMEM),
        out_shape=jax.ShapeDtypeStruct(sums[0].shape, jnp.bfloat16),
        compiler_params=params(),
        name="stepped_slice",
    )(*sums, *pieces)


def outer_kernel(where_ref, par_ref, mom_ref, *refs):
    stepped, (new_par, new_mom, all_ref) = refs[:-3], refs[-3:]
    width = stepped[0].shape[1]
    for k, part in enumerate(stepped):
        all_ref[where_ref[0] ^ k] = part[...].astype(jnp.float32)
    for r in range(len(stepped)):
        cols = slice(r * width, (r + 1) * width)
        old = par_ref[:, cols]
        pseudo = old - all_ref[r]
        fresh = momentum_decay * mom_ref[:, cols] + pseudo
        new_mom[:, cols] = fresh
        new_par[:, cols] = old - outer_rate * (pseudo + momentum_decay * fresh)


def outer_step(where, global_params, momentum, stepped):
    return pl.pallas_call(
        outer_kernel,
        in_specs=[pl.BlockSpec(memory_space=pltpu.SMEM)] + whole_vmem(2 + len(stepped)),
        out_specs=whole_vmem(2),
        out_shape=[jax.ShapeDtypeStruct(global_params.shape, jnp.float32)] * 2,
        scratch_shapes=[pltpu.VMEM((len(stepped),) + stepped[0].shape, jnp.float32)],
        compiler_params=params(),
        name="outer_step",
    )(where, global_params, momentum, *stepped)


def on_device(
    sizes,
    block_input,
    ssd_input,
    out_grad,
    start_state,
    step_bias,
    decay_log,
    local_params,
    global_params,
    momentum,
):
    replicas, chips, cores = sizes
    local_rows = local_params[0]
    rows, depth = local_rows.shape
    own = local_rows.astype(jnp.bfloat16)
    seq_width = ssd_input.shape[1]
    blocks = start_state.shape[0]
    block = block_input.shape[0] // blocks
    fast = (
        cores == 2
        and chips == 4
        and rows % 8 == 0
        and replicas & (replicas - 1) == 0
        and depth % (128 * replicas) == 0
    )
    rep = lax.axis_index("rep")
    spot = lax.axis_index("line") * cores + lax.axis_index("core")
    where = jnp.stack([rep, spot]).astype(jnp.int32)

    def send(value, axis, k):
        count = dict(rep=replicas, line=chips, core=cores)[axis]
        return lax.ppermute(value, axis, [(i, i ^ k) for i in range(count)])

    def send_each(values, axis):
        values = [(k, v) for k, v in enumerate(values, 1)]
        return [sent for sent in reversed([send(v, axis, k) for k, v in reversed(values)])]

    if fast:
        far = send(own, "line", 3)
        near = send(own, "line", 1)
        order = (0, 2, 6, 4, 1, 3, 7, 5)
    else:
        weights = [lax.all_gather(own, ("line", "core"), axis=0, tiled=True)]
        order = (0,)

    early = [[], []]
    states = [start_state[b].reshape(seq_width, STATE) for b in range(blocks)]
    states, own_late = lax.optimization_barrier((states, own))
    for b in range(blocks):
        seq = slice(b * block, (b + 1) * block)
        for half in range(2):
            early[half].append(
                early_products(out_grad[seq], ssd_input[seq], states[b], half, seq_width // 2)
            )
    if fast:
        pieces = column_pieces(where, block_input, own_late, replicas)
        far, _ = lax.optimization_barrier((far, pieces))
        pieces = [pieces[0]] + send_each(pieces[1:], "rep")
        far, early[0] = lax.optimization_barrier((far, early[0]))
        middle = send(far, "line", 1)
        twins = [send(own, "core", 1), send(near, "core", 1)]
        middle, early[1], twins = lax.optimization_barrier((middle, early[1], twins))
        twins = twins + [send(far, "core", 1), send(middle, "core", 1)]
        weights = [own, near, far, middle] + twins

    grads, mine, other = [], [], []
    for b in range(blocks):
        seq = slice(b * block, (b + 1) * block)
        parts = ssd_backward(
            where,
            block_input[seq],
            step_bias,
            decay_log,
            [early[0][b][0], early[1][b][0]],
            [early[0][b][1], early[1][b][1]],
            weights,
            order,
        )
        for kept, part in zip((grads, mine, other), parts):
            kept.append(part)
    grad, mine, other = (
        kept[0] if blocks == 1 else jnp.concatenate(kept, axis=1) for kept in (grads, mine, other)
    )
    block_grad = block_gradient(grad, weights)

    if not fast:
        gradient = lax.psum_scatter(
            contract(grad, block_input, ((1,), (0,))),
            ("line", "core"),
            scatter_dimension=0,
            tiled=True,
        )
        pseudo = global_params - (local_rows - inner_rate * gradient)
        mean_pseudo = lax.psum(pseudo.astype(jnp.bfloat16), "rep").astype(jnp.float32) / replicas
        new_momentum = momentum_decay * momentum + mean_pseudo
        new_params = global_params - outer_rate * (mean_pseudo + momentum_decay * new_momentum)
        return (block_grad, new_params, new_momentum)

    tokens = blocks * block
    other = send(other, "core", 1)
    other, pieces = lax.optimization_barrier((other, pieces))
    twin = send(jnp.concatenate([p[:tokens] for p in pieces], axis=0), "core", 1)
    both = jnp.concatenate([mine, other], axis=0)
    plane = [both] + send_each([both] * (replicas - 1), "rep")
    sums = gradient_slice(where, plane, pieces, twin, chips)
    sums = [sums[0]] + send_each(sums[1:], "line")
    stepped = stepped_slice(sums, pieces)
    stepped = [stepped] + send_each([stepped] * (replicas - 1), "rep")
    new_params, new_momentum = outer_step(where, global_params, momentum, stepped)
    return (block_grad, new_params, new_momentum)


def solution(mesh):
    replicas, shards = mesh.shape["rep"], mesh.shape["fsdp"]
    cores = 2 if shards % 2 == 0 else 1
    sizes = (replicas, shards // cores, cores)
    apart = jax.sharding.Mesh(mesh.devices.reshape(sizes), ("rep", "line", "core"))
    fsdp = ("line", "core")
    rows = P(("rep", "line", "core"), None)
    placed = (
        rows,
        rows,
        rows,
        P(("rep", "line", "core"), None, None),
        P(),
        P(),
        P("rep", fsdp, None),
        P(fsdp, None),
        P(fsdp, None),
    )
    return jax.shard_map(
        functools.partial(on_device, sizes),
        mesh=apart,
        in_specs=placed,
        out_specs=(rows, P(fsdp, None), P(fsdp, None)),
        check_vma=False,
    )
```

```python
import functools

import jax
import jax.numpy as jnp
from jax import lax
from jax.experimental import pallas as pl
from jax.experimental.pallas import tpu as pltpu
from jax.sharding import PartitionSpec as P

STATE = 64
LOG2E = 1.4426950408889634

inner_rate = 0.002
outer_rate = 0.7
momentum_decay = 0.9

VMEM_LIMIT = 20 * 1024 * 1024


def params(**more):
    return pltpu.CompilerParams(vmem_limit_bytes=VMEM_LIMIT, **more)


def whole_vmem(count):
    return [pl.BlockSpec(memory_space=pltpu.VMEM)] * count


def contract(left, right, dims):
    return lax.dot_general(left, right, (dims, ((), ())), preferred_element_type=jnp.float32)


def terms(value, count):
    out = []
    for _ in range(count):
        out.append(value.astype(jnp.bfloat16))
        value = value - out[-1].astype(jnp.float32)
    return out


def early_kernel(cot_ref, val_ref, state_ref, cross_ref, enter_ref):
    block = cot_ref.shape[0]
    lanes = lax.broadcasted_iota(jnp.int32, (block, 2 * STATE), 1)
    rows = lax.broadcasted_iota(jnp.int32, (block, block), 0)
    cols = lax.broadcasted_iota(jnp.int32, (block, block), 1)
    causal = rows >= cols
    low = lanes < STATE
    square = (2 * STATE, 2 * STATE)
    same_head = (lax.broadcasted_iota(jnp.int32, square, 0) < STATE) == (
        lax.broadcasted_iota(jnp.int32, square, 1) < STATE
    )
    for pair in range(cot_ref.shape[1] // (2 * STATE)):
        span = slice(pair * 2 * STATE, (pair + 1) * 2 * STATE)
        cot = cot_ref[:, span]
        val = val_ref[:, span]
        zero = jnp.zeros_like(cot)
        for odd in range(2):
            one = jnp.where(low, zero, cot) if odd else jnp.where(low, cot, zero)
            cross = contract(one, val, ((1,), (1,)))
            cross_ref[2 * pair + odd] = jnp.where(causal, cross, 0.0).astype(cross_ref.dtype)
        state = state_ref[span, :]
        wide = jnp.concatenate([state, state], axis=1)
        wide = jnp.where(same_head, wide, jnp.zeros_like(wide))
        enter_ref[:, span] = contract(cot, wide, ((1,), (0,)))


def early_products(out_grad, ssd_input, state, part, width):
    block = out_grad.shape[0]
    heads = width // STATE
    steps = 4
    piece = width // steps
    return pl.pallas_call(
        early_kernel,
        grid=(steps,),
        in_specs=[
            pl.BlockSpec((block, piece), lambda i: (0, part * steps + i)),
            pl.BlockSpec((block, piece), lambda i: (0, part * steps + i)),
            pl.BlockSpec((piece, STATE), lambda i: (part * steps + i, 0)),
        ],
        out_specs=[
            pl.BlockSpec((heads // steps, block, block), lambda i: (i, 0, 0)),
            pl.BlockSpec((block, piece), lambda i: (0, i)),
        ],
        out_shape=[
            jax.ShapeDtypeStruct((heads, block, block), jnp.bfloat16),
            jax.ShapeDtypeStruct((block, width), jnp.float32),
        ],
        compiler_params=params(),
        cost_estimate=pl.CostEstimate(flops=1, bytes_accessed=1, transcendentals=0),
        name="early_products",
    )(out_grad, ssd_input, state)


def stacked(refs):
    if len(refs) == 1:
        return refs[0][...]
    return jnp.concatenate([r[...].astype(jnp.float32) for r in refs], axis=0).astype(jnp.bfloat16)


def shard_rows(index, k, rows):
    return pl.ds(pl.multiple_of((index ^ k) * rows, 8), rows)


def first_kernel(rows_ref, *refs):
    refs[-1][...] = contract(stacked(refs[:-1]), rows_ref[...], ((1,), (1,)))


def first_projection(rows_in, weights):
    rows = sum(w.shape[0] for w in weights)
    return pl.pallas_call(
        first_kernel,
        in_specs=whole_vmem(1 + len(weights)),
        out_specs=pl.BlockSpec(memory_space=pltpu.VMEM),
        out_shape=jax.ShapeDtypeStruct((rows, rows_in.shape[0]), jnp.float32),
        compiler_params=params(),
        name="first_projection",
    )(rows_in, *weights)


def ssd_kernel(order, first, where_ref, rows_ref, bias_ref, decay_ref, *rest):
    shards = len(order)
    cross_refs, enter_refs, rest = rest[:2], rest[2:4], rest[4:]
    first_ref, rest = (rest[0], rest[1:]) if first else (None, rest)
    weight_refs, rest = rest[: shards - first], rest[shards - first :]
    grad_ref, mine_ref, other_ref, proj_ref, col_ref, out_ref = rest
    block = rows_ref.shape[0]
    heads = bias_ref.shape[1]
    per = weight_refs[0].shape[0]
    arrived = contract(stacked(weight_refs), rows_ref[...], ((1,), (1,)))
    if shards == 1:
        proj_ref[...] = arrived
    else:
        for at, k in enumerate(order):
            source, line = (first_ref, at) if at < first else (arrived, at - first)
            proj_ref[shard_rows(where_ref[1], k, per), :] = source[line * per : (line + 1) * per]
    key_t = proj_ref[:STATE, :]
    query_t = proj_ref[STATE : 2 * STATE, :]
    bias_t = jnp.broadcast_to(bias_ref[...], (block, heads)).T
    rate = jnp.exp(jnp.broadcast_to(decay_ref[...], (block, heads)).T)
    raw = proj_ref[2 * STATE :, :] + bias_t
    step_t = jnp.maximum(raw, 0.0) + jnp.log1p(jnp.exp(-jnp.abs(raw)))
    up = lax.broadcasted_iota(jnp.int32, (block, block), 0)
    across = lax.broadcasted_iota(jnp.int32, (block, block), 1)
    before = jnp.where(up <= across, 1.0, 0.0).astype(jnp.bfloat16)
    after = jnp.where(up >= across, 1.0, 0.0).astype(jnp.bfloat16)
    cum_t = LOG2E * contract(
        jnp.concatenate(terms(-step_t * rate, 3), axis=1),
        jnp.concatenate([before] * 3, axis=0),
        ((1,), (0,)),
    )
    cum = cum_t.T
    step = step_t.T
    query = query_t.T
    query_high, query_low = terms(query, 2)
    key_high, key_low = terms(key_t, 2)
    scores = contract(
        jnp.concatenate([query_high, query_high, query_low], axis=1),
        jnp.concatenate([key_high, key_low, key_high], axis=0),
        ((1,), (0,)),
    )
    entered = jnp.exp2(cum)
    query_twice = jnp.concatenate([query, query], axis=1)
    low = lax.broadcasted_iota(jnp.int32, (block, 2 * STATE), 1) < STATE
    head_of = lax.broadcasted_iota(jnp.int32, (block, heads), 1)
    below = lax.broadcasted_iota(jnp.int32, (block, heads), 0) < STATE

    score_grad = jnp.zeros((block, block), jnp.float32)
    query_grad = jnp.zeros((block, 2 * STATE), jnp.float32)
    row_sums = jnp.zeros((block, heads), jnp.float32)
    for h0 in range(0, heads, 4):
        left, right = [], []
        for h in range(h0, h0 + 4):
            span = cum[:, h : h + 1] - cum_t[h : h + 1, :]
            cross = cross_refs[2 * h // heads][h % (heads // 2)]
            weight = cross.astype(jnp.float32) * jnp.exp2(jnp.minimum(span, 0.0))
            score_grad = score_grad + weight * step_t[h : h + 1, :]
            mixed = weight * scores
            col_ref[h : h + 1, :] = jnp.sum(mixed, axis=0, keepdims=True)
            left.append(mixed.astype(jnp.bfloat16))
            right.append(jnp.where(head_of == h, step, 0.0).astype(jnp.bfloat16))
        for h in range(h0, h0 + 4, 2):
            gain = jnp.where(low, entered[:, h : h + 1], entered[:, h + 1 : h + 2])
            at = h % (heads // 2) * STATE
            part = enter_refs[2 * h // heads][:, at : at + 2 * STATE] * gain
            query_grad = query_grad + part
            left.append((part * query_twice).astype(jnp.bfloat16))
            right.append(
                jnp.where(head_of == jnp.where(below, h, h + 1), 1.0, 0.0).astype(jnp.bfloat16)
            )
        row_sums = row_sums + contract(
            jnp.concatenate(left, axis=1), jnp.concatenate(right, axis=0), ((1,), (0,))
        )

    cols_t = col_ref[...]
    cum_grad = row_sums.T - step_t * cols_t
    later = contract(
        jnp.concatenate(terms(cum_grad, 2), axis=1),
        jnp.concatenate([after] * 2, axis=0),
        ((1,), (0,)),
    )
    step_grad = cols_t - rate * later
    raw_grad = step_grad / (1.0 + jnp.exp(-raw))
    score_grad = score_grad.astype(jnp.bfloat16)
    out_ref[:STATE, :] = contract(query_t.astype(jnp.bfloat16), score_grad, ((1,), (0,)))
    query_all = (query_grad[:, :STATE] + query_grad[:, STATE:]).T
    out_ref[STATE : 2 * STATE, :] = query_all + contract(key_high, score_grad, ((1,), (1,)))
    out_ref[2 * STATE :, :] = raw_grad
    if shards == 1:
        grad_ref[...] = out_ref[...].astype(jnp.bfloat16)
        mine_ref[...] = jnp.zeros_like(mine_ref)
        other_ref[...] = jnp.zeros_like(other_ref)
        return
    core = where_ref[1] % 2
    for part, ref in ((core, mine_ref), (1 - core, other_ref)):
        of_core = [out_ref[shard_rows(f + part, 0, per), :] for f in range(0, shards, 2)]
        ref[...] = jnp.concatenate(of_core, axis=0).astype(jnp.bfloat16)
    for at, k in enumerate(order):
        proj_ref[at * per : (at + 1) * per, :] = out_ref[shard_rows(where_ref[1], k, per), :]
    grad_ref[...] = proj_ref[...].astype(jnp.bfloat16)


def ssd_backward(where, rows_in, step_bias, decay_log, cross, enter, first, weights, order):
    block = rows_in.shape[0]
    heads = step_bias.shape[0]
    cols = len(order) * weights[0].shape[0]
    half = (cols // 2, block)
    return pl.pallas_call(
        functools.partial(ssd_kernel, order, len(order) - len(weights)),
        in_specs=[pl.BlockSpec(memory_space=pltpu.SMEM)]
        + whole_vmem(7 + len(first) + len(weights)),
        out_specs=whole_vmem(3),
        out_shape=[
            jax.ShapeDtypeStruct((cols, block), jnp.bfloat16),
            jax.ShapeDtypeStruct(half, jnp.bfloat16),
            jax.ShapeDtypeStruct(half, jnp.bfloat16),
        ],
        scratch_shapes=[
            pltpu.VMEM((cols, block), jnp.float32),
            pltpu.VMEM((heads, block), jnp.float32),
            pltpu.VMEM((cols, block), jnp.float32),
        ],
        compiler_params=params(),
        cost_estimate=pl.CostEstimate(flops=1, bytes_accessed=1, transcendentals=0),
        name="ssd_backward",
    )(where, rows_in, step_bias.reshape(1, -1), decay_log.reshape(1, -1), *cross, *enter, *first, *weights)


def block_grad_kernel(grad_ref, *refs):
    out_ref = refs[-1]
    weights = stacked(refs[:-1])
    out_ref[...] = contract(grad_ref[...].T, weights, ((1,), (0,))).astype(out_ref.dtype)


def block_gradient(grad, weights):
    depth = weights[0].shape[1]
    cols, block = grad.shape
    return pl.pallas_call(
        block_grad_kernel,
        in_specs=whole_vmem(1 + len(weights)),
        out_specs=pl.BlockSpec(memory_space=pltpu.VMEM),
        out_shape=jax.ShapeDtypeStruct((block, depth), jnp.bfloat16),
        compiler_params=params(),
        cost_estimate=pl.CostEstimate(
            flops=2 * block * cols * depth, bytes_accessed=4 * cols * depth, transcendentals=0
        ),
        name="block_gradient",
    )(grad, *weights)


def pieces_kernel(where_ref, rows_ref, own_ref, *outs):
    block = rows_ref.shape[0]
    width = outs[0].shape[1]
    for k, out in enumerate(outs):
        cols = pl.ds(pl.multiple_of((where_ref[0] ^ k) * width, 128), width)
        out[:block, :] = rows_ref[:, cols]
        out[block:, :] = own_ref[:, cols]


def column_pieces(where, rows_in, own, replicas):
    tokens, depth = rows_in.shape
    shape = (tokens + own.shape[0], depth // replicas)
    return pl.pallas_call(
        pieces_kernel,
        in_specs=[pl.BlockSpec(memory_space=pltpu.SMEM)] + whole_vmem(2),
        out_specs=whole_vmem(replicas),
        out_shape=[jax.ShapeDtypeStruct(shape, jnp.bfloat16)] * replicas,
        compiler_params=params(),
        name="column_pieces",
    )(where, rows_in, own)


def slice_kernel(replicas, where_ref, *refs):
    grads, pieces, refs = refs[:replicas], refs[replicas : 2 * replicas], refs[2 * replicas :]
    twin, outs, total = refs[0], refs[1:-1], refs[-1]
    tokens = twin.shape[0] // replicas
    rows = total.shape[0]
    left, right = [], []
    for other in range(2):
        for k in range(replicas):
            left.append(grads[k][other * rows : (other + 1) * rows, :])
            right.append(
                twin[k * tokens : (k + 1) * tokens, :] if other else pieces[k][:tokens, :]
            )
    total[...] = contract(
        jnp.concatenate(left, axis=1), jnp.concatenate(right, axis=0), ((1,), (0,))
    )
    per = outs[0].shape[0]
    chip = where_ref[1] // 2
    for k, out in enumerate(outs):
        out[...] = total[shard_rows(chip, k, per), :].astype(jnp.bfloat16)


def gradient_slice(where, grads, pieces, twin, chips):
    rows = grads[0].shape[0] // (2 * chips)
    width = twin.shape[1]
    return pl.pallas_call(
        functools.partial(slice_kernel, len(pieces)),
        in_specs=[pl.BlockSpec(memory_space=pltpu.SMEM)] + whole_vmem(1 + 2 * len(pieces)),
        out_specs=whole_vmem(chips),
        out_shape=[jax.ShapeDtypeStruct((rows, width), jnp.bfloat16)] * chips,
        scratch_shapes=[pltpu.VMEM((rows * chips, width), jnp.float32)],
        compiler_params=params(),
        name="gradient_slice",
    )(where, *grads, *pieces, twin)


def stepped_kernel(chips, *refs):
    sums, pieces, out_ref = refs[:chips], refs[chips:-1], refs[-1]
    rows = out_ref.shape[0]
    total = sums[0][...].astype(jnp.float32)
    for part in sums[1:]:
        total = total + part[...].astype(jnp.float32)
    level = pieces[0][-rows:, :].astype(jnp.float32)
    for piece in pieces[1:]:
        level = level + piece[-rows:, :].astype(jnp.float32)
    mean = (level - inner_rate * total) * (1.0 / len(pieces))
    out_ref[...] = mean.astype(jnp.bfloat16)


def stepped_slice(sums, pieces):
    return pl.pallas_call(
        functools.partial(stepped_kernel, len(sums)),
        in_specs=whole_vmem(len(sums) + len(pieces)),
        out_specs=pl.BlockSpec(memory_space=pltpu.VMEM),
        out_shape=jax.ShapeDtypeStruct(sums[0].shape, jnp.bfloat16),
        compiler_params=params(),
        name="stepped_slice",
    )(*sums, *pieces)


def outer_kernel(where_ref, par_ref, mom_ref, *refs):
    stepped, (new_par, new_mom, all_ref) = refs[:-3], refs[-3:]
    width = stepped[0].shape[1]
    for k, part in enumerate(stepped):
        all_ref[where_ref[0] ^ k] = part[...].astype(jnp.float32)
    for r in range(len(stepped)):
        cols = slice(r * width, (r + 1) * width)
        old = par_ref[:, cols]
        pseudo = old - all_ref[r]
        fresh = momentum_decay * mom_ref[:, cols] + pseudo
        new_mom[:, cols] = fresh
        new_par[:, cols] = old - outer_rate * (pseudo + momentum_decay * fresh)


def outer_step(where, global_params, momentum, stepped):
    return pl.pallas_call(
        outer_kernel,
        in_specs=[pl.BlockSpec(memory_space=pltpu.SMEM)] + whole_vmem(2 + len(stepped)),
        out_specs=whole_vmem(2),
        out_shape=[jax.ShapeDtypeStruct(global_params.shape, jnp.float32)] * 2,
        scratch_shapes=[pltpu.VMEM((len(stepped),) + stepped[0].shape, jnp.float32)],
        compiler_params=params(),
        name="outer_step",
    )(where, global_params, momentum, *stepped)


def on_device(
    sizes,
    block_input,
    ssd_input,
    out_grad,
    start_state,
    step_bias,
    decay_log,
    local_params,
    global_params,
    momentum,
):
    replicas, chips, cores = sizes
    local_rows = local_params[0]
    rows, depth = local_rows.shape
    own = local_rows.astype(jnp.bfloat16)
    seq_width = ssd_input.shape[1]
    blocks = start_state.shape[0]
    block = block_input.shape[0] // blocks
    fast = (
        cores == 2
        and chips == 4
        and rows % 8 == 0
        and replicas & (replicas - 1) == 0
        and depth % (128 * replicas) == 0
    )
    rep = lax.axis_index("rep")
    spot = lax.axis_index("line") * cores + lax.axis_index("core")
    where = jnp.stack([rep, spot]).astype(jnp.int32)

    def send(value, axis, k):
        count = dict(rep=replicas, line=chips, core=cores)[axis]
        return lax.ppermute(value, axis, [(i, i ^ k) for i in range(count)])

    def send_each(values, axis):
        values = [(k, v) for k, v in enumerate(values, 1)]
        return [sent for sent in reversed([send(v, axis, k) for k, v in reversed(values)])]

    if fast:
        far = send(own, "line", 3)
        near = send(own, "line", 1)
        order = (0, 2, 6, 1, 3, 7, 4, 5)
    else:
        weights = [lax.all_gather(own, ("line", "core"), axis=0, tiled=True)]
        order = (0,)
        first = 0

    early = [[], []]
    states = [start_state[b].reshape(seq_width, STATE) for b in range(blocks)]
    states, own_late = lax.optimization_barrier((states, own))
    for b in range(blocks):
        seq = slice(b * block, (b + 1) * block)
        for half in range(2):
            early[half].append(
                early_products(out_grad[seq], ssd_input[seq], states[b], half, seq_width // 2)
            )
    if fast:
        pieces = column_pieces(where, block_input, own_late, replicas)
        far, _ = lax.optimization_barrier((far, pieces))
        pieces = [pieces[0]] + send_each(pieces[1:], "rep")
        far, early[0] = lax.optimization_barrier((far, early[0]))
        middle = send(far, "line", 1)
        weights = [own, near, far] + [send(w, "core", 1) for w in (own, near, far)]
        middle, early[1], weights = lax.optimization_barrier((middle, early[1], weights))
        weights = weights + [middle, send(middle, "core", 1)]
        first = 6

    begun = []
    if fast:
        begun = [
            first_projection(block_input[b * block : (b + 1) * block], weights[:first])
            for b in range(blocks)
        ]
        begun, pieces[:-1] = lax.optimization_barrier((begun, pieces[:-1]))

    grads, mine, other = [], [], []
    for b in range(blocks):
        seq = slice(b * block, (b + 1) * block)
        parts = ssd_backward(
            where,
            block_input[seq],
            step_bias,
            decay_log,
            [early[0][b][0], early[1][b][0]],
            [early[0][b][1], early[1][b][1]],
            begun[b : b + 1],
            weights[first:],
            order,
        )
        for kept, part in zip((grads, mine, other), parts):
            kept.append(part)
    grad, mine, other = (
        kept[0] if blocks == 1 else jnp.concatenate(kept, axis=1) for kept in (grads, mine, other)
    )
    block_grad = block_gradient(grad, weights)

    if not fast:
        gradient = lax.psum_scatter(
            contract(grad, block_input, ((1,), (0,))),
            ("line", "core"),
            scatter_dimension=0,
            tiled=True,
        )
        pseudo = global_params - (local_rows - inner_rate * gradient)
        mean_pseudo = lax.psum(pseudo.astype(jnp.bfloat16), "rep").astype(jnp.float32) / replicas
        new_momentum = momentum_decay * momentum + mean_pseudo
        new_params = global_params - outer_rate * (mean_pseudo + momentum_decay * new_momentum)
        return (block_grad, new_params, new_momentum)

    tokens = blocks * block
    both = jnp.concatenate([mine, send(other, "core", 1)], axis=0)
    plane = [both] + send_each([both] * (replicas - 1), "rep")
    plane[-1], pieces[-1] = lax.optimization_barrier((plane[-1], pieces[-1]))
    twin = send(jnp.concatenate([p[:tokens] for p in pieces], axis=0), "core", 1)
    sums = gradient_slice(where, plane, pieces, twin, chips)
    sums = [sums[0]] + send_each(sums[1:], "line")
    sums, block_grad = lax.optimization_barrier((sums, block_grad))
    stepped = stepped_slice(sums, pieces)
    stepped = [stepped] + send_each([stepped] * (replicas - 1), "rep")
    new_params, new_momentum = outer_step(where, global_params, momentum, stepped)
    return (block_grad, new_params, new_momentum)


def solution(mesh):
    replicas, shards = mesh.shape["rep"], mesh.shape["fsdp"]
    cores = 2 if shards % 2 == 0 else 1
    sizes = (replicas, shards // cores, cores)
    apart = jax.sharding.Mesh(mesh.devices.reshape(sizes), ("rep", "line", "core"))
    fsdp = ("line", "core")
    rows = P(("rep", "line", "core"), None)
    placed = (
        rows,
        rows,
        rows,
        P(("rep", "line", "core"), None, None),
        P(),
        P(),
        P("rep", fsdp, None),
        P(fsdp, None),
        P(fsdp, None),
    )
    return jax.shard_map(
        functools.partial(on_device, sizes),
        mesh=apart,
        in_specs=placed,
        out_specs=(rows, P(fsdp, None), P(fsdp, None)),
        check_vma=False,
    )
```

```python
import functools

import jax
import jax.numpy as jnp
from jax import lax
from jax.experimental import pallas as pl
from jax.experimental.pallas import tpu as pltpu
from jax.sharding import PartitionSpec as P

STATE = 64
LOG2E = 1.4426950408889634

inner_rate = 0.002
outer_rate = 0.7
momentum_decay = 0.9

VMEM_LIMIT = 20 * 1024 * 1024


def params(**more):
    return pltpu.CompilerParams(vmem_limit_bytes=VMEM_LIMIT, **more)


def whole_vmem(count):
    return [pl.BlockSpec(memory_space=pltpu.VMEM)] * count


def contract(left, right, dims):
    return lax.dot_general(left, right, (dims, ((), ())), preferred_element_type=jnp.float32)


def terms(value, count):
    out = []
    for _ in range(count):
        out.append(value.astype(jnp.bfloat16))
        value = value - out[-1].astype(jnp.float32)
    return out


def early_kernel(cot_ref, val_ref, state_ref, cross_ref, enter_ref):
    block = cot_ref.shape[0]
    lanes = lax.broadcasted_iota(jnp.int32, (block, 2 * STATE), 1)
    rows = lax.broadcasted_iota(jnp.int32, (block, block), 0)
    cols = lax.broadcasted_iota(jnp.int32, (block, block), 1)
    causal = rows >= cols
    low = lanes < STATE
    square = (2 * STATE, 2 * STATE)
    same_head = (lax.broadcasted_iota(jnp.int32, square, 0) < STATE) == (
        lax.broadcasted_iota(jnp.int32, square, 1) < STATE
    )
    for pair in range(cot_ref.shape[1] // (2 * STATE)):
        span = slice(pair * 2 * STATE, (pair + 1) * 2 * STATE)
        cot = cot_ref[:, span]
        val = val_ref[:, span]
        zero = jnp.zeros_like(cot)
        for odd in range(2):
            one = jnp.where(low, zero, cot) if odd else jnp.where(low, cot, zero)
            cross = contract(one, val, ((1,), (1,)))
            cross_ref[2 * pair + odd] = jnp.where(causal, cross, 0.0).astype(cross_ref.dtype)
        state = state_ref[span, :]
        wide = jnp.concatenate([state, state], axis=1)
        wide = jnp.where(same_head, wide, jnp.zeros_like(wide))
        enter_ref[:, span] = contract(cot, wide, ((1,), (0,)))


def early_products(out_grad, ssd_input, state, part, width):
    block = out_grad.shape[0]
    heads = width // STATE
    steps = 4
    piece = width // steps
    return pl.pallas_call(
        early_kernel,
        grid=(steps,),
        in_specs=[
            pl.BlockSpec((block, piece), lambda i: (0, part * steps + i)),
            pl.BlockSpec((block, piece), lambda i: (0, part * steps + i)),
            pl.BlockSpec((piece, STATE), lambda i: (part * steps + i, 0)),
        ],
        out_specs=[
            pl.BlockSpec((heads // steps, block, block), lambda i: (i, 0, 0)),
            pl.BlockSpec((block, piece), lambda i: (0, i)),
        ],
        out_shape=[
            jax.ShapeDtypeStruct((heads, block, block), jnp.bfloat16),
            jax.ShapeDtypeStruct((block, width), jnp.float32),
        ],
        compiler_params=params(),
        cost_estimate=pl.CostEstimate(flops=1, bytes_accessed=1, transcendentals=0),
        name="early_products",
    )(out_grad, ssd_input, state)


def stacked(refs):
    if len(refs) == 1:
        return refs[0][...]
    return jnp.concatenate([r[...].astype(jnp.float32) for r in refs], axis=0).astype(jnp.bfloat16)


def shard_rows(index, k, rows):
    return pl.ds(pl.multiple_of((index ^ k) * rows, 8), rows)


def first_kernel(rows_ref, *refs):
    refs[-1][...] = contract(stacked(refs[:-1]), rows_ref[...], ((1,), (1,)))


def first_projection(rows_in, weights):
    rows = sum(w.shape[0] for w in weights)
    return pl.pallas_call(
        first_kernel,
        in_specs=whole_vmem(1 + len(weights)),
        out_specs=pl.BlockSpec(memory_space=pltpu.VMEM),
        out_shape=jax.ShapeDtypeStruct((rows, rows_in.shape[0]), jnp.float32),
        compiler_params=params(),
        cost_estimate=pl.CostEstimate(flops=1, bytes_accessed=1, transcendentals=0),
        name="first_projection",
    )(rows_in, *weights)


def ssd_kernel(order, first, where_ref, rows_ref, bias_ref, decay_ref, *rest):
    shards = len(order)
    cross_refs, enter_refs, rest = rest[:2], rest[2:4], rest[4:]
    first_ref, rest = (rest[0], rest[1:]) if first else (None, rest)
    weight_refs, rest = rest[: shards - first], rest[shards - first :]
    grad_ref, mine_ref, other_ref, proj_ref, col_ref, out_ref = rest
    block = rows_ref.shape[0]
    heads = bias_ref.shape[1]
    per = weight_refs[0].shape[0]
    arrived = contract(stacked(weight_refs), rows_ref[...], ((1,), (1,)))
    if shards == 1:
        proj_ref[...] = arrived
    else:
        for at, k in enumerate(order):
            source, line = (first_ref, at) if at < first else (arrived, at - first)
            proj_ref[shard_rows(where_ref[1], k, per), :] = source[line * per : (line + 1) * per]
    key_t = proj_ref[:STATE, :]
    query_t = proj_ref[STATE : 2 * STATE, :]
    bias_t = jnp.broadcast_to(bias_ref[...], (block, heads)).T
    rate = jnp.exp(jnp.broadcast_to(decay_ref[...], (block, heads)).T)
    raw = proj_ref[2 * STATE :, :] + bias_t
    step_t = jnp.maximum(raw, 0.0) + jnp.log1p(jnp.exp(-jnp.abs(raw)))
    up = lax.broadcasted_iota(jnp.int32, (block, block), 0)
    across = lax.broadcasted_iota(jnp.int32, (block, block), 1)
    before = jnp.where(up <= across, 1.0, 0.0).astype(jnp.bfloat16)
    after = jnp.where(up >= across, 1.0, 0.0).astype(jnp.bfloat16)
    cum_t = LOG2E * contract(
        jnp.concatenate(terms(-step_t * rate, 3), axis=1),
        jnp.concatenate([before] * 3, axis=0),
        ((1,), (0,)),
    )
    cum = cum_t.T
    step = step_t.T
    query = query_t.T
    query_high, query_low = terms(query, 2)
    key_high, key_low = terms(key_t, 2)
    scores = contract(
        jnp.concatenate([query_high, query_high, query_low], axis=1),
        jnp.concatenate([key_high, key_low, key_high], axis=0),
        ((1,), (0,)),
    )
    entered = jnp.exp2(cum)
    query_twice = jnp.concatenate([query, query], axis=1)
    low = lax.broadcasted_iota(jnp.int32, (block, 2 * STATE), 1) < STATE
    head_of = lax.broadcasted_iota(jnp.int32, (block, heads), 1)
    below = lax.broadcasted_iota(jnp.int32, (block, heads), 0) < STATE

    score_grad = jnp.zeros((block, block), jnp.float32)
    query_grad = jnp.zeros((block, 2 * STATE), jnp.float32)
    row_sums = jnp.zeros((block, heads), jnp.float32)
    for h0 in range(0, heads, 4):
        left, right = [], []
        for h in range(h0, h0 + 4):
            span = cum[:, h : h + 1] - cum_t[h : h + 1, :]
            cross = cross_refs[2 * h // heads][h % (heads // 2)]
            weight = cross.astype(jnp.float32) * jnp.exp2(jnp.minimum(span, 0.0))
            score_grad = score_grad + weight * step_t[h : h + 1, :]
            mixed = weight * scores
            col_ref[h : h + 1, :] = jnp.sum(mixed, axis=0, keepdims=True)
            left.append(mixed.astype(jnp.bfloat16))
            right.append(jnp.where(head_of == h, step, 0.0).astype(jnp.bfloat16))
        for h in range(h0, h0 + 4, 2):
            gain = jnp.where(low, entered[:, h : h + 1], entered[:, h + 1 : h + 2])
            at = h % (heads // 2) * STATE
            part = enter_refs[2 * h // heads][:, at : at + 2 * STATE] * gain
            query_grad = query_grad + part
            left.append((part * query_twice).astype(jnp.bfloat16))
            right.append(
                jnp.where(head_of == jnp.where(below, h, h + 1), 1.0, 0.0).astype(jnp.bfloat16)
            )
        row_sums = row_sums + contract(
            jnp.concatenate(left, axis=1), jnp.concatenate(right, axis=0), ((1,), (0,))
        )

    cols_t = col_ref[...]
    cum_grad = row_sums.T - step_t * cols_t
    later = contract(
        jnp.concatenate(terms(cum_grad, 2), axis=1),
        jnp.concatenate([after] * 2, axis=0),
        ((1,), (0,)),
    )
    step_grad = cols_t - rate * later
    raw_grad = step_grad / (1.0 + jnp.exp(-raw))
    score_grad = score_grad.astype(jnp.bfloat16)
    out_ref[:STATE, :] = contract(query_t.astype(jnp.bfloat16), score_grad, ((1,), (0,)))
    query_all = (query_grad[:, :STATE] + query_grad[:, STATE:]).T
    out_ref[STATE : 2 * STATE, :] = query_all + contract(key_high, score_grad, ((1,), (1,)))
    out_ref[2 * STATE :, :] = raw_grad
    if shards == 1:
        grad_ref[...] = out_ref[...].astype(jnp.bfloat16)
        mine_ref[...] = jnp.zeros_like(mine_ref)
        other_ref[...] = jnp.zeros_like(other_ref)
        return
    core = where_ref[1] % 2
    for part, ref in ((core, mine_ref), (1 - core, other_ref)):
        of_core = [out_ref[shard_rows(f + part, 0, per), :] for f in range(0, shards, 2)]
        ref[...] = jnp.concatenate(of_core, axis=0).astype(jnp.bfloat16)
    for at, k in enumerate(order):
        proj_ref[at * per : (at + 1) * per, :] = out_ref[shard_rows(where_ref[1], k, per), :]
    grad_ref[...] = proj_ref[...].astype(jnp.bfloat16)


def ssd_backward(where, rows_in, step_bias, decay_log, cross, enter, first, weights, order):
    block = rows_in.shape[0]
    heads = step_bias.shape[0]
    cols = len(order) * weights[0].shape[0]
    half = (cols // 2, block)
    return pl.pallas_call(
        functools.partial(ssd_kernel, order, len(order) - len(weights)),
        in_specs=[pl.BlockSpec(memory_space=pltpu.SMEM)]
        + whole_vmem(7 + len(first) + len(weights)),
        out_specs=whole_vmem(3),
        out_shape=[
            jax.ShapeDtypeStruct((cols, block), jnp.bfloat16),
            jax.ShapeDtypeStruct(half, jnp.bfloat16),
            jax.ShapeDtypeStruct(half, jnp.bfloat16),
        ],
        scratch_shapes=[
            pltpu.VMEM((cols, block), jnp.float32),
            pltpu.VMEM((heads, block), jnp.float32),
            pltpu.VMEM((cols, block), jnp.float32),
        ],
        compiler_params=params(),
        cost_estimate=pl.CostEstimate(flops=1, bytes_accessed=1, transcendentals=0),
        name="ssd_backward",
    )(where, rows_in, step_bias.reshape(1, -1), decay_log.reshape(1, -1), *cross, *enter, *first, *weights)


def block_grad_kernel(grad_ref, *refs):
    out_ref = refs[-1]
    weights = stacked(refs[:-1])
    out_ref[...] = contract(grad_ref[...].T, weights, ((1,), (0,))).astype(out_ref.dtype)


def block_gradient(grad, weights):
    depth = weights[0].shape[1]
    cols, block = grad.shape
    return pl.pallas_call(
        block_grad_kernel,
        in_specs=whole_vmem(1 + len(weights)),
        out_specs=pl.BlockSpec(memory_space=pltpu.VMEM),
        out_shape=jax.ShapeDtypeStruct((block, depth), jnp.bfloat16),
        compiler_params=params(),
        cost_estimate=pl.CostEstimate(
            flops=2 * block * cols * depth, bytes_accessed=4 * cols * depth, transcendentals=0
        ),
        name="block_gradient",
    )(grad, *weights)


def pieces_kernel(where_ref, rows_ref, own_ref, *outs):
    block = rows_ref.shape[0]
    width = outs[0].shape[1]
    for k, out in enumerate(outs):
        cols = pl.ds(pl.multiple_of((where_ref[0] ^ k) * width, 128), width)
        out[:block, :] = rows_ref[:, cols]
        out[block:, :] = own_ref[:, cols]


def column_pieces(where, rows_in, own, replicas):
    tokens, depth = rows_in.shape
    shape = (tokens + own.shape[0], depth // replicas)
    return pl.pallas_call(
        pieces_kernel,
        in_specs=[pl.BlockSpec(memory_space=pltpu.SMEM)] + whole_vmem(2),
        out_specs=whole_vmem(replicas),
        out_shape=[jax.ShapeDtypeStruct(shape, jnp.bfloat16)] * replicas,
        compiler_params=params(),
        name="column_pieces",
    )(where, rows_in, own)


def slice_kernel(replicas, where_ref, *refs):
    grads, pieces, refs = refs[:replicas], refs[replicas : 2 * replicas], refs[2 * replicas :]
    twin, outs, total = refs[0], refs[1:-1], refs[-1]
    tokens = twin.shape[0] // replicas
    rows = total.shape[0]
    left, right = [], []
    for other in range(2):
        for k in range(replicas):
            left.append(grads[k][other * rows : (other + 1) * rows, :])
            right.append(
                twin[k * tokens : (k + 1) * tokens, :] if other else pieces[k][:tokens, :]
            )
    total[...] = contract(
        jnp.concatenate(left, axis=1), jnp.concatenate(right, axis=0), ((1,), (0,))
    )
    per = outs[0].shape[0]
    chip = where_ref[1] // 2
    for k, out in enumerate(outs):
        out[...] = total[shard_rows(chip, k, per), :].astype(jnp.bfloat16)


def gradient_slice(where, grads, pieces, twin, chips):
    rows = grads[0].shape[0] // (2 * chips)
    width = twin.shape[1]
    return pl.pallas_call(
        functools.partial(slice_kernel, len(pieces)),
        in_specs=[pl.BlockSpec(memory_space=pltpu.SMEM)] + whole_vmem(1 + 2 * len(pieces)),
        out_specs=whole_vmem(chips),
        out_shape=[jax.ShapeDtypeStruct((rows, width), jnp.bfloat16)] * chips,
        scratch_shapes=[pltpu.VMEM((rows * chips, width), jnp.float32)],
        compiler_params=params(),
        name="gradient_slice",
    )(where, *grads, *pieces, twin)


def stepped_kernel(chips, *refs):
    sums, pieces, out_ref = refs[:chips], refs[chips:-1], refs[-1]
    rows = out_ref.shape[0]
    total = sums[0][...].astype(jnp.float32)
    for part in sums[1:]:
        total = total + part[...].astype(jnp.float32)
    level = pieces[0][-rows:, :].astype(jnp.float32)
    for piece in pieces[1:]:
        level = level + piece[-rows:, :].astype(jnp.float32)
    mean = (level - inner_rate * total) * (1.0 / len(pieces))
    out_ref[...] = mean.astype(jnp.bfloat16)


def stepped_slice(sums, pieces):
    return pl.pallas_call(
        functools.partial(stepped_kernel, len(sums)),
        in_specs=whole_vmem(len(sums) + len(pieces)),
        out_specs=pl.BlockSpec(memory_space=pltpu.VMEM),
        out_shape=jax.ShapeDtypeStruct(sums[0].shape, jnp.bfloat16),
        compiler_params=params(),
        name="stepped_slice",
    )(*sums, *pieces)


def outer_kernel(where_ref, par_ref, mom_ref, *refs):
    stepped, (new_par, new_mom, all_ref) = refs[:-3], refs[-3:]
    width = stepped[0].shape[1]
    for k, part in enumerate(stepped):
        all_ref[where_ref[0] ^ k] = part[...].astype(jnp.float32)
    for r in range(len(stepped)):
        cols = slice(r * width, (r + 1) * width)
        old = par_ref[:, cols]
        pseudo = old - all_ref[r]
        fresh = momentum_decay * mom_ref[:, cols] + pseudo
        new_mom[:, cols] = fresh
        new_par[:, cols] = old - outer_rate * (pseudo + momentum_decay * fresh)


def outer_step(where, global_params, momentum, stepped):
    return pl.pallas_call(
        outer_kernel,
        in_specs=[pl.BlockSpec(memory_space=pltpu.SMEM)] + whole_vmem(2 + len(stepped)),
        out_specs=whole_vmem(2),
        out_shape=[jax.ShapeDtypeStruct(global_params.shape, jnp.float32)] * 2,
        scratch_shapes=[pltpu.VMEM((len(stepped),) + stepped[0].shape, jnp.float32)],
        compiler_params=params(),
        name="outer_step",
    )(where, global_params, momentum, *stepped)


def on_device(
    sizes,
    block_input,
    ssd_input,
    out_grad,
    start_state,
    step_bias,
    decay_log,
    local_params,
    global_params,
    momentum,
):
    replicas, chips, cores = sizes
    rep = lax.axis_index("rep")
    spot = lax.axis_index("line") * cores + lax.axis_index("core")
    where = jnp.stack([rep, spot]).astype(jnp.int32)
    where, local_params = lax.optimization_barrier((where, local_params))
    local_rows = local_params[0]
    rows, depth = local_rows.shape
    own = local_rows.astype(jnp.bfloat16)
    seq_width = ssd_input.shape[1]
    blocks = start_state.shape[0]
    block = block_input.shape[0] // blocks
    fast = (
        cores == 2
        and chips == 4
        and rows % 8 == 0
        and replicas & (replicas - 1) == 0
        and depth % (128 * replicas) == 0
    )

    def send(value, axis, k):
        count = dict(rep=replicas, line=chips, core=cores)[axis]
        return lax.ppermute(value, axis, [(i, i ^ k) for i in range(count)])

    def send_each(values, axis):
        values = [(k, v) for k, v in enumerate(values, 1)]
        return [sent for sent in reversed([send(v, axis, k) for k, v in reversed(values)])]

    if fast:
        far = send(own, "line", 3)
        near = send(own, "line", 1)
        order = (0, 2, 6, 1, 3, 7, 4, 5)
    else:
        late = [lax.all_gather(own, ("line", "core"), axis=0, tiled=True)]
        weights = []
        order = (0,)

    early = [[], []]
    states = [start_state[b].reshape(seq_width, STATE) for b in range(blocks)]
    for b in range(blocks):
        seq = slice(b * block, (b + 1) * block)
        for half in range(2):
            early[half].append(
                early_products(out_grad[seq], ssd_input[seq], states[b], half, seq_width // 2)
            )
    if fast:
        pieces = column_pieces(where, block_input, own, replicas)
        far, _ = lax.optimization_barrier((far, pieces))
        pieces = [pieces[0]] + send_each(pieces[1:], "rep")
        near, early[0] = lax.optimization_barrier((near, early[0]))
        far, early[0] = lax.optimization_barrier((far, early[0]))
        middle = send(far, "line", 1)
        middle, pieces[-1] = lax.optimization_barrier((middle, pieces[-1]))
        pair = send(jnp.concatenate([own, near], axis=0), "core", 1)
        weights = [own, near, far, pair, send(far, "core", 1)]
        middle, early[1], weights = lax.optimization_barrier((middle, early[1], weights))
        late = [middle, send(middle, "core", 1)]

    begun = []
    if fast:
        begun = [
            first_projection(block_input[b * block : (b + 1) * block], weights)
            for b in range(blocks)
        ]

    grads, mine, other = [], [], []
    for b in range(blocks):
        seq = slice(b * block, (b + 1) * block)
        parts = ssd_backward(
            where,
            block_input[seq],
            step_bias,
            decay_log,
            [early[0][b][0], early[1][b][0]],
            [early[0][b][1], early[1][b][1]],
            begun[b : b + 1],
            late,
            order,
        )
        for kept, part in zip((grads, mine, other), parts):
            kept.append(part)
    grad, mine, other = (
        kept[0] if blocks == 1 else jnp.concatenate(kept, axis=1) for kept in (grads, mine, other)
    )
    block_grad = block_gradient(grad, weights + late)

    if not fast:
        gradient = lax.psum_scatter(
            contract(grad, block_input, ((1,), (0,))),
            ("line", "core"),
            scatter_dimension=0,
            tiled=True,
        )
        pseudo = global_params - (local_rows - inner_rate * gradient)
        mean_pseudo = lax.psum(pseudo.astype(jnp.bfloat16), "rep").astype(jnp.float32) / replicas
        new_momentum = momentum_decay * momentum + mean_pseudo
        new_params = global_params - outer_rate * (mean_pseudo + momentum_decay * new_momentum)
        return (block_grad, new_params, new_momentum)

    tokens = blocks * block
    other = send(other, "core", 1)
    other, pieces = lax.optimization_barrier((other, pieces))
    both = jnp.concatenate([mine, other], axis=0)
    plane = [both] + send_each([both] * (replicas - 1), "rep")
    twin = send(jnp.concatenate([p[:tokens] for p in pieces], axis=0), "core", 1)
    sums = gradient_slice(where, plane, pieces, twin, chips)
    sums = [sums[0]] + send_each(sums[1:], "line")
    sums, block_grad = lax.optimization_barrier((sums, block_grad))
    stepped = stepped_slice(sums, pieces)
    stepped = [stepped] + send_each([stepped] * (replicas - 1), "rep")
    new_params, new_momentum = outer_step(where, global_params, momentum, stepped)
    return (block_grad, new_params, new_momentum)


def solution(mesh):
    replicas, shards = mesh.shape["rep"], mesh.shape["fsdp"]
    cores = 2 if shards % 2 == 0 else 1
    sizes = (replicas, shards // cores, cores)
    apart = jax.sharding.Mesh(mesh.devices.reshape(sizes), ("rep", "line", "core"))
    fsdp = ("line", "core")
    rows = P(("rep", "line", "core"), None)
    placed = (
        rows,
        rows,
        rows,
        P(("rep", "line", "core"), None, None),
        P(),
        P(),
        P("rep", fsdp, None),
        P(fsdp, None),
        P(fsdp, None),
    )
    return jax.shard_map(
        functools.partial(on_device, sizes),
        mesh=apart,
        in_specs=placed,
        out_specs=(rows, P(fsdp, None), P(fsdp, None)),
        check_vma=False,
    )
```

```python
import functools

import jax
import jax.numpy as jnp
from jax import lax
from jax.experimental import pallas as pl
from jax.experimental.pallas import tpu as pltpu
from jax.sharding import PartitionSpec as P

STATE = 64
LOG2E = 1.4426950408889634

inner_rate = 0.002
outer_rate = 0.7
momentum_decay = 0.9

VMEM_LIMIT = 20 * 1024 * 1024


def params(**more):
    return pltpu.CompilerParams(vmem_limit_bytes=VMEM_LIMIT, **more)


def whole_vmem(count):
    return [pl.BlockSpec(memory_space=pltpu.VMEM)] * count


def contract(left, right, dims):
    return lax.dot_general(left, right, (dims, ((), ())), preferred_element_type=jnp.float32)


def terms(value, count):
    out = []
    for _ in range(count):
        out.append(value.astype(jnp.bfloat16))
        value = value - out[-1].astype(jnp.float32)
    return out


def early_kernel(cot_ref, val_ref, state_ref, cross_ref, enter_ref):
    block = cot_ref.shape[0]
    lanes = lax.broadcasted_iota(jnp.int32, (block, 2 * STATE), 1)
    rows = lax.broadcasted_iota(jnp.int32, (block, block), 0)
    cols = lax.broadcasted_iota(jnp.int32, (block, block), 1)
    causal = rows >= cols
    low = lanes < STATE
    square = (2 * STATE, 2 * STATE)
    same_head = (lax.broadcasted_iota(jnp.int32, square, 0) < STATE) == (
        lax.broadcasted_iota(jnp.int32, square, 1) < STATE
    )
    for pair in range(cot_ref.shape[1] // (2 * STATE)):
        span = slice(pair * 2 * STATE, (pair + 1) * 2 * STATE)
        cot = cot_ref[:, span]
        val = val_ref[:, span]
        zero = jnp.zeros_like(cot)
        for odd in range(2):
            one = jnp.where(low, zero, cot) if odd else jnp.where(low, cot, zero)
            cross = contract(one, val, ((1,), (1,)))
            cross_ref[2 * pair + odd] = jnp.where(causal, cross, 0.0).astype(cross_ref.dtype)
        state = state_ref[span, :]
        wide = jnp.concatenate([state, state], axis=1)
        wide = jnp.where(same_head, wide, jnp.zeros_like(wide))
        enter_ref[:, span] = contract(cot, wide, ((1,), (0,)))


def early_products(out_grad, ssd_input, state, part, width):
    block = out_grad.shape[0]
    heads = width // STATE
    steps = 4
    piece = width // steps
    return pl.pallas_call(
        early_kernel,
        grid=(steps,),
        in_specs=[
            pl.BlockSpec((block, piece), lambda i: (0, part * steps + i)),
            pl.BlockSpec((block, piece), lambda i: (0, part * steps + i)),
            pl.BlockSpec((piece, STATE), lambda i: (part * steps + i, 0)),
        ],
        out_specs=[
            pl.BlockSpec((heads // steps, block, block), lambda i: (i, 0, 0)),
            pl.BlockSpec((block, piece), lambda i: (0, i)),
        ],
        out_shape=[
            jax.ShapeDtypeStruct((heads, block, block), jnp.bfloat16),
            jax.ShapeDtypeStruct((block, width), jnp.float32),
        ],
        compiler_params=params(),
        cost_estimate=pl.CostEstimate(flops=1, bytes_accessed=1, transcendentals=0),
        name="early_products",
    )(out_grad, ssd_input, state)


def stacked(refs):
    if len(refs) == 1:
        return refs[0][...]
    return jnp.concatenate([r[...].astype(jnp.float32) for r in refs], axis=0).astype(jnp.bfloat16)


def shard_rows(index, k, rows):
    return pl.ds(pl.multiple_of((index ^ k) * rows, 8), rows)


def first_kernel(rows_ref, *refs):
    refs[-1][...] = contract(stacked(refs[:-1]), rows_ref[...], ((1,), (1,)))


def first_projection(rows_in, weights):
    rows = sum(w.shape[0] for w in weights)
    return pl.pallas_call(
        first_kernel,
        in_specs=whole_vmem(1 + len(weights)),
        out_specs=pl.BlockSpec(memory_space=pltpu.VMEM),
        out_shape=jax.ShapeDtypeStruct((rows, rows_in.shape[0]), jnp.float32),
        compiler_params=params(),
        cost_estimate=pl.CostEstimate(flops=1, bytes_accessed=1, transcendentals=0),
        name="first_projection",
    )(rows_in, *weights)


def ssd_kernel(order, first, where_ref, rows_ref, bias_ref, decay_ref, *rest):
    shards = len(order)
    cross_refs, enter_refs, rest = rest[:2], rest[2:4], rest[4:]
    first_ref, rest = (rest[0], rest[1:]) if first else (None, rest)
    weight_refs, rest = rest[: shards - first], rest[shards - first :]
    grad_ref, mine_ref, other_ref, proj_ref, col_ref, out_ref = rest
    block = rows_ref.shape[0]
    heads = bias_ref.shape[1]
    per = weight_refs[0].shape[0]
    arrived = contract(stacked(weight_refs), rows_ref[...], ((1,), (1,)))
    if shards == 1:
        proj_ref[...] = arrived
    else:
        for at, k in enumerate(order):
            source, line = (first_ref, at) if at < first else (arrived, at - first)
            proj_ref[shard_rows(where_ref[1], k, per), :] = source[line * per : (line + 1) * per]
    key_t = proj_ref[:STATE, :]
    query_t = proj_ref[STATE : 2 * STATE, :]
    bias_t = jnp.broadcast_to(bias_ref[...], (block, heads)).T
    rate = jnp.exp(jnp.broadcast_to(decay_ref[...], (block, heads)).T)
    raw = proj_ref[2 * STATE :, :] + bias_t
    step_t = jnp.maximum(raw, 0.0) + jnp.log1p(jnp.exp(-jnp.abs(raw)))
    up = lax.broadcasted_iota(jnp.int32, (block, block), 0)
    across = lax.broadcasted_iota(jnp.int32, (block, block), 1)
    before = jnp.where(up <= across, 1.0, 0.0).astype(jnp.bfloat16)
    after = jnp.where(up >= across, 1.0, 0.0).astype(jnp.bfloat16)
    cum_t = LOG2E * contract(
        jnp.concatenate(terms(-step_t * rate, 3), axis=1),
        jnp.concatenate([before] * 3, axis=0),
        ((1,), (0,)),
    )
    cum = cum_t.T
    step = step_t.T
    query = query_t.T
    query_high, query_low = terms(query, 2)
    key_high, key_low = terms(key_t, 2)
    scores = contract(
        jnp.concatenate([query_high, query_high, query_low], axis=1),
        jnp.concatenate([key_high, key_low, key_high], axis=0),
        ((1,), (0,)),
    )
    entered = jnp.exp2(cum)
    query_twice = jnp.concatenate([query, query], axis=1)
    low = lax.broadcasted_iota(jnp.int32, (block, 2 * STATE), 1) < STATE
    head_of = lax.broadcasted_iota(jnp.int32, (block, heads), 1)
    below = lax.broadcasted_iota(jnp.int32, (block, heads), 0) < STATE

    score_grad = jnp.zeros((block, block), jnp.float32)
    query_grad = jnp.zeros((block, 2 * STATE), jnp.float32)
    row_sums = jnp.zeros((block, heads), jnp.float32)
    for h0 in range(0, heads, 4):
        left, right = [], []
        for h in range(h0, h0 + 4):
            span = cum[:, h : h + 1] - cum_t[h : h + 1, :]
            cross = cross_refs[2 * h // heads][h % (heads // 2)]
            weight = cross.astype(jnp.float32) * jnp.exp2(jnp.minimum(span, 0.0))
            score_grad = score_grad + weight * step_t[h : h + 1, :]
            mixed = weight * scores
            col_ref[h : h + 1, :] = jnp.sum(mixed, axis=0, keepdims=True)
            left.append(mixed.astype(jnp.bfloat16))
            right.append(jnp.where(head_of == h, step, 0.0).astype(jnp.bfloat16))
        for h in range(h0, h0 + 4, 2):
            gain = jnp.where(low, entered[:, h : h + 1], entered[:, h + 1 : h + 2])
            at = h % (heads // 2) * STATE
            part = enter_refs[2 * h // heads][:, at : at + 2 * STATE] * gain
            query_grad = query_grad + part
            left.append((part * query_twice).astype(jnp.bfloat16))
            right.append(
                jnp.where(head_of == jnp.where(below, h, h + 1), 1.0, 0.0).astype(jnp.bfloat16)
            )
        row_sums = row_sums + contract(
            jnp.concatenate(left, axis=1), jnp.concatenate(right, axis=0), ((1,), (0,))
        )

    cols_t = col_ref[...]
    cum_grad = row_sums.T - step_t * cols_t
    later = contract(
        jnp.concatenate(terms(cum_grad, 2), axis=1),
        jnp.concatenate([after] * 2, axis=0),
        ((1,), (0,)),
    )
    step_grad = cols_t - rate * later
    raw_grad = step_grad / (1.0 + jnp.exp(-raw))
    score_grad = score_grad.astype(jnp.bfloat16)
    out_ref[:STATE, :] = contract(query_t.astype(jnp.bfloat16), score_grad, ((1,), (0,)))
    query_all = (query_grad[:, :STATE] + query_grad[:, STATE:]).T
    out_ref[STATE : 2 * STATE, :] = query_all + contract(key_high, score_grad, ((1,), (1,)))
    out_ref[2 * STATE :, :] = raw_grad
    if shards == 1:
        grad_ref[...] = out_ref[...].astype(jnp.bfloat16)
        mine_ref[...] = jnp.zeros_like(mine_ref)
        other_ref[...] = jnp.zeros_like(other_ref)
        return
    core = where_ref[1] % 2
    for part, ref in ((core, mine_ref), (1 - core, other_ref)):
        of_core = [out_ref[shard_rows(f + part, 0, per), :] for f in range(0, shards, 2)]
        ref[...] = jnp.concatenate(of_core, axis=0).astype(jnp.bfloat16)
    for at, k in enumerate(order):
        proj_ref[at * per : (at + 1) * per, :] = out_ref[shard_rows(where_ref[1], k, per), :]
    grad_ref[...] = proj_ref[...].astype(jnp.bfloat16)


def ssd_backward(where, rows_in, step_bias, decay_log, cross, enter, first, weights, order):
    block = rows_in.shape[0]
    heads = step_bias.shape[0]
    cols = len(order) * weights[0].shape[0]
    half = (cols // 2, block)
    return pl.pallas_call(
        functools.partial(ssd_kernel, order, len(order) - len(weights)),
        in_specs=[pl.BlockSpec(memory_space=pltpu.SMEM)]
        + whole_vmem(7 + len(first) + len(weights)),
        out_specs=whole_vmem(3),
        out_shape=[
            jax.ShapeDtypeStruct((cols, block), jnp.bfloat16),
            jax.ShapeDtypeStruct(half, jnp.bfloat16),
            jax.ShapeDtypeStruct(half, jnp.bfloat16),
        ],
        scratch_shapes=[
            pltpu.VMEM((cols, block), jnp.float32),
            pltpu.VMEM((heads, block), jnp.float32),
            pltpu.VMEM((cols, block), jnp.float32),
        ],
        compiler_params=params(),
        cost_estimate=pl.CostEstimate(flops=1, bytes_accessed=1, transcendentals=0),
        name="ssd_backward",
    )(where, rows_in, step_bias.reshape(1, -1), decay_log.reshape(1, -1), *cross, *enter, *first, *weights)


def block_grad_kernel(grad_ref, *refs):
    out_ref = refs[-1]
    weights = stacked(refs[:-1])
    out_ref[...] = contract(grad_ref[...].T, weights, ((1,), (0,))).astype(out_ref.dtype)


def block_gradient(grad, weights):
    depth = weights[0].shape[1]
    cols, block = grad.shape
    return pl.pallas_call(
        block_grad_kernel,
        in_specs=whole_vmem(1 + len(weights)),
        out_specs=pl.BlockSpec(memory_space=pltpu.VMEM),
        out_shape=jax.ShapeDtypeStruct((block, depth), jnp.bfloat16),
        compiler_params=params(),
        cost_estimate=pl.CostEstimate(
            flops=2 * block * cols * depth, bytes_accessed=4 * cols * depth, transcendentals=0
        ),
        name="block_gradient",
    )(grad, *weights)


def pieces_kernel(where_ref, rows_ref, own_ref, *outs):
    block = rows_ref.shape[0]
    width = outs[0].shape[1]
    for k, out in enumerate(outs):
        cols = pl.ds(pl.multiple_of((where_ref[0] ^ k) * width, 128), width)
        out[:block, :] = rows_ref[:, cols]
        out[block:, :] = own_ref[:, cols]


def column_pieces(where, rows_in, own, replicas):
    tokens, depth = rows_in.shape
    shape = (tokens + own.shape[0], depth // replicas)
    return pl.pallas_call(
        pieces_kernel,
        in_specs=[pl.BlockSpec(memory_space=pltpu.SMEM)] + whole_vmem(2),
        out_specs=whole_vmem(replicas),
        out_shape=[jax.ShapeDtypeStruct(shape, jnp.bfloat16)] * replicas,
        compiler_params=params(),
        name="column_pieces",
    )(where, rows_in, own)


def slice_kernel(replicas, where_ref, *refs):
    grads, pieces, refs = refs[:replicas], refs[replicas : 2 * replicas], refs[2 * replicas :]
    twin, outs, total = refs[0], refs[1:-1], refs[-1]
    tokens = twin.shape[0] // replicas
    rows = total.shape[0]
    left, right = [], []
    for other in range(2):
        for k in range(replicas):
            left.append(grads[k][other * rows : (other + 1) * rows, :])
            right.append(
                twin[k * tokens : (k + 1) * tokens, :] if other else pieces[k][:tokens, :]
            )
    total[...] = contract(
        jnp.concatenate(left, axis=1), jnp.concatenate(right, axis=0), ((1,), (0,))
    )
    per = outs[0].shape[0]
    chip = where_ref[1] // 2
    for k, out in enumerate(outs):
        out[...] = total[shard_rows(chip, k, per), :].astype(jnp.bfloat16)


def gradient_slice(where, grads, pieces, twin, chips):
    rows = grads[0].shape[0] // (2 * chips)
    width = twin.shape[1]
    return pl.pallas_call(
        functools.partial(slice_kernel, len(pieces)),
        in_specs=[pl.BlockSpec(memory_space=pltpu.SMEM)] + whole_vmem(1 + 2 * len(pieces)),
        out_specs=whole_vmem(chips),
        out_shape=[jax.ShapeDtypeStruct((rows, width), jnp.bfloat16)] * chips,
        scratch_shapes=[pltpu.VMEM((rows * chips, width), jnp.float32)],
        compiler_params=params(),
        name="gradient_slice",
    )(where, *grads, *pieces, twin)


def stepped_kernel(chips, *refs):
    sums, pieces, out_ref = refs[:chips], refs[chips:-1], refs[-1]
    rows = out_ref.shape[0]
    total = sums[0][...].astype(jnp.float32)
    for part in sums[1:]:
        total = total + part[...].astype(jnp.float32)
    level = pieces[0][-rows:, :].astype(jnp.float32)
    for piece in pieces[1:]:
        level = level + piece[-rows:, :].astype(jnp.float32)
    mean = (level - inner_rate * total) * (1.0 / len(pieces))
    out_ref[...] = mean.astype(jnp.bfloat16)


def stepped_slice(sums, pieces):
    return pl.pallas_call(
        functools.partial(stepped_kernel, len(sums)),
        in_specs=whole_vmem(len(sums) + len(pieces)),
        out_specs=pl.BlockSpec(memory_space=pltpu.VMEM),
        out_shape=jax.ShapeDtypeStruct(sums[0].shape, jnp.bfloat16),
        compiler_params=params(),
        name="stepped_slice",
    )(*sums, *pieces)


def outer_kernel(where_ref, par_ref, mom_ref, *refs):
    stepped, (new_par, new_mom, all_ref) = refs[:-3], refs[-3:]
    width = stepped[0].shape[1]
    for k, part in enumerate(stepped):
        all_ref[where_ref[0] ^ k] = part[...].astype(jnp.float32)
    for r in range(len(stepped)):
        cols = slice(r * width, (r + 1) * width)
        old = par_ref[:, cols]
        pseudo = old - all_ref[r]
        fresh = momentum_decay * mom_ref[:, cols] + pseudo
        new_mom[:, cols] = fresh
        new_par[:, cols] = old - outer_rate * (pseudo + momentum_decay * fresh)


def outer_step(where, global_params, momentum, stepped):
    return pl.pallas_call(
        outer_kernel,
        in_specs=[pl.BlockSpec(memory_space=pltpu.SMEM)] + whole_vmem(2 + len(stepped)),
        out_specs=whole_vmem(2),
        out_shape=[jax.ShapeDtypeStruct(global_params.shape, jnp.float32)] * 2,
        scratch_shapes=[pltpu.VMEM((len(stepped),) + stepped[0].shape, jnp.float32)],
        compiler_params=params(),
        name="outer_step",
    )(where, global_params, momentum, *stepped)


def on_device(
    sizes,
    block_input,
    ssd_input,
    out_grad,
    start_state,
    step_bias,
    decay_log,
    local_params,
    global_params,
    momentum,
):
    replicas, chips, cores = sizes
    rep = lax.axis_index("rep")
    spot = lax.axis_index("line") * cores + lax.axis_index("core")
    where = jnp.stack([rep, spot]).astype(jnp.int32)
    where, local_params = lax.optimization_barrier((where, local_params))
    local_rows = local_params[0]
    rows, depth = local_rows.shape
    own = local_rows.astype(jnp.bfloat16)
    seq_width = ssd_input.shape[1]
    blocks = start_state.shape[0]
    block = block_input.shape[0] // blocks
    fast = (
        cores == 2
        and chips == 4
        and rows % 8 == 0
        and replicas & (replicas - 1) == 0
        and depth % (128 * replicas) == 0
    )

    def send(value, axis, k):
        count = dict(rep=replicas, line=chips, core=cores)[axis]
        return lax.ppermute(value, axis, [(i, i ^ k) for i in range(count)])

    def send_each(values, axis):
        values = [(k, v) for k, v in enumerate(values, 1)]
        return [sent for sent in reversed([send(v, axis, k) for k, v in reversed(values)])]

    if fast:
        far = send(own, "line", 3)
        near = send(own, "line", 1)
        order = (0, 2, 6, 1, 3, 7, 4, 5)
    else:
        late = [lax.all_gather(own, ("line", "core"), axis=0, tiled=True)]
        weights = []
        order = (0,)

    early = [[], []]
    states = [start_state[b].reshape(seq_width, STATE) for b in range(blocks)]
    states, own_late = lax.optimization_barrier((states, own))
    for b in range(blocks):
        seq = slice(b * block, (b + 1) * block)
        for half in range(2):
            early[half].append(
                early_products(out_grad[seq], ssd_input[seq], states[b], half, seq_width // 2)
            )
    if fast:
        pieces = column_pieces(where, block_input, own_late, replicas)
        far, _ = lax.optimization_barrier((far, pieces))
        pieces = [pieces[0]] + send_each(pieces[1:], "rep")
        near, early[0] = lax.optimization_barrier((near, early[0]))
        far, early[0] = lax.optimization_barrier((far, early[0]))
        middle = send(far, "line", 1)
        middle, pieces[-1] = lax.optimization_barrier((middle, pieces[-1]))
        pair = send(jnp.concatenate([own, near], axis=0), "core", 1)
        weights = [own, near, far, pair, send(far, "core", 1)]
        middle, early[1], weights = lax.optimization_barrier((middle, early[1], weights))
        late = [middle, send(middle, "core", 1)]

    begun = []
    if fast:
        begun = [
            first_projection(block_input[b * block : (b + 1) * block], weights)
            for b in range(blocks)
        ]

    grads, mine, other = [], [], []
    for b in range(blocks):
        seq = slice(b * block, (b + 1) * block)
        parts = ssd_backward(
            where,
            block_input[seq],
            step_bias,
            decay_log,
            [early[0][b][0], early[1][b][0]],
            [early[0][b][1], early[1][b][1]],
            begun[b : b + 1],
            late,
            order,
        )
        for kept, part in zip((grads, mine, other), parts):
            kept.append(part)
    grad, mine, other = (
        kept[0] if blocks == 1 else jnp.concatenate(kept, axis=1) for kept in (grads, mine, other)
    )
    block_grad = block_gradient(grad, weights + late)

    if not fast:
        gradient = lax.psum_scatter(
            contract(grad, block_input, ((1,), (0,))),
            ("line", "core"),
            scatter_dimension=0,
            tiled=True,
        )
        pseudo = global_params - (local_rows - inner_rate * gradient)
        mean_pseudo = lax.psum(pseudo.astype(jnp.bfloat16), "rep").astype(jnp.float32) / replicas
        new_momentum = momentum_decay * momentum + mean_pseudo
        new_params = global_params - outer_rate * (mean_pseudo + momentum_decay * new_momentum)
        return (block_grad, new_params, new_momentum)

    tokens = blocks * block
    other = send(other, "core", 1)
    other, pieces = lax.optimization_barrier((other, pieces))
    both = jnp.concatenate([mine, other], axis=0)
    plane = [both] + send_each([both] * (replicas - 1), "rep")
    twin = send(jnp.concatenate([p[:tokens] for p in pieces], axis=0), "core", 1)
    sums = gradient_slice(where, plane, pieces, twin, chips)
    sums = [sums[0]] + send_each(sums[1:], "line")
    sums, block_grad = lax.optimization_barrier((sums, block_grad))
    stepped = stepped_slice(sums, pieces)
    stepped = [stepped] + send_each([stepped] * (replicas - 1), "rep")
    new_params, new_momentum = outer_step(where, global_params, momentum, stepped)
    return (block_grad, new_params, new_momentum)


def solution(mesh):
    replicas, shards = mesh.shape["rep"], mesh.shape["fsdp"]
    cores = 2 if shards % 2 == 0 else 1
    sizes = (replicas, shards // cores, cores)
    apart = jax.sharding.Mesh(mesh.devices.reshape(sizes), ("rep", "line", "core"))
    fsdp = ("line", "core")
    rows = P(("rep", "line", "core"), None)
    placed = (
        rows,
        rows,
        rows,
        P(("rep", "line", "core"), None, None),
        P(),
        P(),
        P("rep", fsdp, None),
        P(fsdp, None),
        P(fsdp, None),
    )
    return jax.shard_map(
        functools.partial(on_device, sizes),
        mesh=apart,
        in_specs=placed,
        out_specs=(rows, P(fsdp, None), P(fsdp, None)),
        check_vma=False,
    )
```

```python
import functools

import jax
import jax.numpy as jnp
from jax import lax
from jax.experimental import pallas as pl
from jax.experimental.pallas import tpu as pltpu
from jax.sharding import PartitionSpec as P

STATE = 64
LOG2E = 1.4426950408889634

inner_rate = 0.002
outer_rate = 0.7
momentum_decay = 0.9

VMEM_LIMIT = 20 * 1024 * 1024


def params(**more):
    return pltpu.CompilerParams(vmem_limit_bytes=VMEM_LIMIT, **more)


def whole_vmem(count):
    return [pl.BlockSpec(memory_space=pltpu.VMEM)] * count


def contract(left, right, dims):
    return lax.dot_general(left, right, (dims, ((), ())), preferred_element_type=jnp.float32)


def terms(value, count):
    out = []
    for _ in range(count):
        out.append(value.astype(jnp.bfloat16))
        value = value - out[-1].astype(jnp.float32)
    return out


def round_kernel(wide_ref, out_ref):
    out_ref[...] = wide_ref[...].astype(out_ref.dtype)


def rounded(wide):
    return pl.pallas_call(
        round_kernel,
        in_specs=whole_vmem(1),
        out_specs=pl.BlockSpec(memory_space=pltpu.VMEM),
        out_shape=jax.ShapeDtypeStruct(wide.shape, jnp.bfloat16),
        compiler_params=params(),
        name="rounded",
    )(wide)


def early_kernel(cot_ref, val_ref, state_ref, cross_ref, enter_ref):
    block = cot_ref.shape[0]
    lanes = lax.broadcasted_iota(jnp.int32, (block, 2 * STATE), 1)
    rows = lax.broadcasted_iota(jnp.int32, (block, block), 0)
    cols = lax.broadcasted_iota(jnp.int32, (block, block), 1)
    causal = rows >= cols
    low = lanes < STATE
    square = (2 * STATE, 2 * STATE)
    same_head = (lax.broadcasted_iota(jnp.int32, square, 0) < STATE) == (
        lax.broadcasted_iota(jnp.int32, square, 1) < STATE
    )
    for pair in range(cot_ref.shape[1] // (2 * STATE)):
        span = slice(pair * 2 * STATE, (pair + 1) * 2 * STATE)
        cot = cot_ref[:, span]
        val = val_ref[:, span]
        zero = jnp.zeros_like(cot)
        for odd in range(2):
            one = jnp.where(low, zero, cot) if odd else jnp.where(low, cot, zero)
            cross = contract(one, val, ((1,), (1,)))
            cross_ref[2 * pair + odd] = jnp.where(causal, cross, 0.0).astype(cross_ref.dtype)
        state = state_ref[span, :]
        wide = jnp.concatenate([state, state], axis=1)
        wide = jnp.where(same_head, wide, jnp.zeros_like(wide))
        enter_ref[:, span] = contract(cot, wide, ((1,), (0,)))


def early_products(out_grad, ssd_input, state, part, width):
    block = out_grad.shape[0]
    heads = width // STATE
    steps = 4
    piece = width // steps
    return pl.pallas_call(
        early_kernel,
        grid=(steps,),
        in_specs=[
            pl.BlockSpec((block, piece), lambda i: (0, part * steps + i)),
            pl.BlockSpec((block, piece), lambda i: (0, part * steps + i)),
            pl.BlockSpec((piece, STATE), lambda i: (part * steps + i, 0)),
        ],
        out_specs=[
            pl.BlockSpec((heads // steps, block, block), lambda i: (i, 0, 0)),
            pl.BlockSpec((block, piece), lambda i: (0, i)),
        ],
        out_shape=[
            jax.ShapeDtypeStruct((heads, block, block), jnp.bfloat16),
            jax.ShapeDtypeStruct((block, width), jnp.float32),
        ],
        compiler_params=params(),
        cost_estimate=pl.CostEstimate(flops=1, bytes_accessed=1, transcendentals=0),
        name="early_products",
    )(out_grad, ssd_input, state)


def stacked(refs):
    if len(refs) == 1:
        return refs[0][...]
    return jnp.concatenate([r[...].astype(jnp.float32) for r in refs], axis=0).astype(jnp.bfloat16)


def own_place(cores):
    return lax.axis_index("rep"), lax.axis_index("line") * cores + lax.axis_index("core")


def shard_rows(index, k, rows):
    return pl.ds(pl.multiple_of((index ^ k) * rows, 8), rows)


def first_kernel(rows_ref, *refs):
    refs[-1][...] = contract(stacked(refs[:-1]), rows_ref[...], ((1,), (1,)))


def first_projection(rows_in, weights):
    rows = sum(w.shape[0] for w in weights)
    return pl.pallas_call(
        first_kernel,
        in_specs=whole_vmem(1 + len(weights)),
        out_specs=pl.BlockSpec(memory_space=pltpu.VMEM),
        out_shape=jax.ShapeDtypeStruct((rows, rows_in.shape[0]), jnp.float32),
        compiler_params=params(),
        cost_estimate=pl.CostEstimate(flops=1, bytes_accessed=1, transcendentals=0),
        name="first_projection",
    )(rows_in, *weights)


def ssd_kernel(order, first, rows_ref, bias_ref, decay_ref, *rest):
    shards = len(order)
    cross_refs, enter_refs, rest = rest[:2], rest[2:4], rest[4:]
    _, spot = own_place(2) if shards > 1 else (0, 0)
    first_ref, rest = (rest[0], rest[1:]) if first else (None, rest)
    weight_refs, rest = rest[: shards - first], rest[shards - first :]
    grad_ref, mine_ref, other_ref, proj_ref, col_ref, out_ref = rest
    block = rows_ref.shape[0]
    heads = bias_ref.shape[1]
    per = weight_refs[0].shape[0]
    arrived = contract(stacked(weight_refs), rows_ref[...], ((1,), (1,)))
    if shards == 1:
        proj_ref[...] = arrived
    else:
        for at, k in enumerate(order):
            source, line = (first_ref, at) if at < first else (arrived, at - first)
            proj_ref[shard_rows(spot, k, per), :] = source[line * per : (line + 1) * per]
    key_t = proj_ref[:STATE, :]
    query_t = proj_ref[STATE : 2 * STATE, :]
    bias_t = jnp.broadcast_to(bias_ref[...], (block, heads)).T
    rate = jnp.exp(jnp.broadcast_to(decay_ref[...], (block, heads)).T)
    raw = proj_ref[2 * STATE :, :] + bias_t
    step_t = jnp.maximum(raw, 0.0) + jnp.log1p(jnp.exp(-jnp.abs(raw)))
    up = lax.broadcasted_iota(jnp.int32, (block, block), 0)
    across = lax.broadcasted_iota(jnp.int32, (block, block), 1)
    before = jnp.where(up <= across, 1.0, 0.0).astype(jnp.bfloat16)
    after = jnp.where(up >= across, 1.0, 0.0).astype(jnp.bfloat16)
    cum_t = LOG2E * contract(
        jnp.concatenate(terms(-step_t * rate, 3), axis=1),
        jnp.concatenate([before] * 3, axis=0),
        ((1,), (0,)),
    )
    cum = cum_t.T
    step = step_t.T
    query = query_t.T
    query_high, query_low = terms(query, 2)
    key_high, key_low = terms(key_t, 2)
    scores = contract(
        jnp.concatenate([query_high, query_high, query_low], axis=1),
        jnp.concatenate([key_high, key_low, key_high], axis=0),
        ((1,), (0,)),
    )
    entered = jnp.exp2(cum)
    query_twice = jnp.concatenate([query, query], axis=1)
    low = lax.broadcasted_iota(jnp.int32, (block, 2 * STATE), 1) < STATE
    head_of = lax.broadcasted_iota(jnp.int32, (block, heads), 1)
    below = lax.broadcasted_iota(jnp.int32, (block, heads), 0) < STATE

    score_grad = jnp.zeros((block, block), jnp.float32)
    query_grad = jnp.zeros((block, 2 * STATE), jnp.float32)
    row_sums = jnp.zeros((block, heads), jnp.float32)
    for h0 in range(0, heads, 4):
        left, right = [], []
        for h in range(h0, h0 + 4):
            span = cum[:, h : h + 1] - cum_t[h : h + 1, :]
            cross = cross_refs[2 * h // heads][h % (heads // 2)]
            weight = cross.astype(jnp.float32) * jnp.exp2(jnp.minimum(span, 0.0))
            score_grad = score_grad + weight * step_t[h : h + 1, :]
            mixed = weight * scores
            col_ref[h : h + 1, :] = jnp.sum(mixed, axis=0, keepdims=True)
            left.append(mixed.astype(jnp.bfloat16))
            right.append(jnp.where(head_of == h, step, 0.0).astype(jnp.bfloat16))
        for h in range(h0, h0 + 4, 2):
            gain = jnp.where(low, entered[:, h : h + 1], entered[:, h + 1 : h + 2])
            at = h % (heads // 2) * STATE
            part = enter_refs[2 * h // heads][:, at : at + 2 * STATE] * gain
            query_grad = query_grad + part
            left.append((part * query_twice).astype(jnp.bfloat16))
            right.append(
                jnp.where(head_of == jnp.where(below, h, h + 1), 1.0, 0.0).astype(jnp.bfloat16)
            )
        row_sums = row_sums + contract(
            jnp.concatenate(left, axis=1), jnp.concatenate(right, axis=0), ((1,), (0,))
        )

    cols_t = col_ref[...]
    cum_grad = row_sums.T - step_t * cols_t
    later = contract(
        jnp.concatenate(terms(cum_grad, 2), axis=1),
        jnp.concatenate([after] * 2, axis=0),
        ((1,), (0,)),
    )
    step_grad = cols_t - rate * later
    raw_grad = step_grad / (1.0 + jnp.exp(-raw))
    score_grad = score_grad.astype(jnp.bfloat16)
    out_ref[:STATE, :] = contract(query_t.astype(jnp.bfloat16), score_grad, ((1,), (0,)))
    query_all = (query_grad[:, :STATE] + query_grad[:, STATE:]).T
    out_ref[STATE : 2 * STATE, :] = query_all + contract(key_high, score_grad, ((1,), (1,)))
    out_ref[2 * STATE :, :] = raw_grad
    if shards == 1:
        grad_ref[...] = out_ref[...].astype(jnp.bfloat16)
        mine_ref[...] = jnp.zeros_like(mine_ref)
        other_ref[...] = jnp.zeros_like(other_ref)
        return
    core = spot % 2
    for part, ref in ((core, mine_ref), (1 - core, other_ref)):
        of_core = [out_ref[shard_rows(f + part, 0, per), :] for f in range(0, shards, 2)]
        ref[...] = jnp.concatenate(of_core, axis=0).astype(jnp.bfloat16)
    for at, k in enumerate(order):
        proj_ref[at * per : (at + 1) * per, :] = out_ref[shard_rows(spot, k, per), :]
    grad_ref[...] = proj_ref[...].astype(jnp.bfloat16)


def ssd_backward(rows_in, step_bias, decay_log, cross, enter, first, weights, order):
    block = rows_in.shape[0]
    heads = step_bias.shape[0]
    cols = len(order) * weights[0].shape[0]
    half = (cols // 2, block)
    return pl.pallas_call(
        functools.partial(ssd_kernel, order, len(order) - len(weights)),
        in_specs=whole_vmem(7 + len(first) + len(weights)),
        out_specs=whole_vmem(3),
        out_shape=[
            jax.ShapeDtypeStruct((cols, block), jnp.bfloat16),
            jax.ShapeDtypeStruct(half, jnp.bfloat16),
            jax.ShapeDtypeStruct(half, jnp.bfloat16),
        ],
        scratch_shapes=[
            pltpu.VMEM((cols, block), jnp.float32),
            pltpu.VMEM((heads, block), jnp.float32),
            pltpu.VMEM((cols, block), jnp.float32),
        ],
        compiler_params=params(),
        cost_estimate=pl.CostEstimate(flops=1, bytes_accessed=1, transcendentals=0),
        name="ssd_backward",
    )(rows_in, step_bias.reshape(1, -1), decay_log.reshape(1, -1), *cross, *enter, *first, *weights)


def block_grad_kernel(grad_ref, *refs):
    out_ref = refs[-1]
    weights = stacked(refs[:-1])
    out_ref[...] = contract(grad_ref[...].T, weights, ((1,), (0,))).astype(out_ref.dtype)


def block_gradient(grad, weights):
    depth = weights[0].shape[1]
    cols, block = grad.shape
    return pl.pallas_call(
        block_grad_kernel,
        in_specs=whole_vmem(1 + len(weights)),
        out_specs=pl.BlockSpec(memory_space=pltpu.VMEM),
        out_shape=jax.ShapeDtypeStruct((block, depth), jnp.bfloat16),
        compiler_params=params(),
        cost_estimate=pl.CostEstimate(
            flops=2 * block * cols * depth, bytes_accessed=4 * cols * depth, transcendentals=0
        ),
        name="block_gradient",
    )(grad, *weights)


def pieces_kernel(rows_ref, own_ref, *outs):
    block = rows_ref.shape[0]
    rep, _ = own_place(2)
    width = outs[0].shape[1]
    for k, out in enumerate(outs):
        cols = pl.ds(pl.multiple_of((rep ^ k) * width, 128), width)
        out[:block, :] = rows_ref[:, cols]
        out[block:, :] = own_ref[:, cols]


def column_pieces(rows_in, own, replicas):
    tokens, depth = rows_in.shape
    shape = (tokens + own.shape[0], depth // replicas)
    return pl.pallas_call(
        pieces_kernel,
        in_specs=whole_vmem(2),
        out_specs=whole_vmem(replicas),
        out_shape=[jax.ShapeDtypeStruct(shape, jnp.bfloat16)] * replicas,
        compiler_params=params(),
        name="column_pieces",
    )(rows_in, own)


def slice_kernel(replicas, *refs):
    grads, pieces, refs = refs[:replicas], refs[replicas : 2 * replicas], refs[2 * replicas :]
    twin, outs, total = refs[0], refs[1:-1], refs[-1]
    tokens = twin.shape[0] // replicas
    rows = total.shape[0]
    left, right = [], []
    for other in range(2):
        for k in range(replicas):
            left.append(grads[k][other * rows : (other + 1) * rows, :])
            right.append(
                twin[k * tokens : (k + 1) * tokens, :] if other else pieces[k][:tokens, :]
            )
    total[...] = contract(
        jnp.concatenate(left, axis=1), jnp.concatenate(right, axis=0), ((1,), (0,))
    )
    per = outs[0].shape[0]
    chip = lax.axis_index("line")
    for k, out in enumerate(outs):
        out[...] = total[shard_rows(chip, k, per), :].astype(jnp.bfloat16)


def gradient_slice(grads, pieces, twin, chips):
    rows = grads[0].shape[0] // (2 * chips)
    width = twin.shape[1]
    return pl.pallas_call(
        functools.partial(slice_kernel, len(pieces)),
        in_specs=whole_vmem(1 + 2 * len(pieces)),
        out_specs=whole_vmem(chips),
        out_shape=[jax.ShapeDtypeStruct((rows, width), jnp.bfloat16)] * chips,
        scratch_shapes=[pltpu.VMEM((rows * chips, width), jnp.float32)],
        compiler_params=params(),
        name="gradient_slice",
    )(*grads, *pieces, twin)


def stepped_kernel(chips, *refs):
    sums, pieces, out_ref = refs[:chips], refs[chips:-1], refs[-1]
    rows = out_ref.shape[0]
    total = sums[0][...].astype(jnp.float32)
    for part in sums[1:]:
        total = total + part[...].astype(jnp.float32)
    level = pieces[0][-rows:, :].astype(jnp.float32)
    for piece in pieces[1:]:
        level = level + piece[-rows:, :].astype(jnp.float32)
    mean = (level - inner_rate * total) * (1.0 / len(pieces))
    out_ref[...] = mean.astype(jnp.bfloat16)


def stepped_slice(sums, pieces):
    return pl.pallas_call(
        functools.partial(stepped_kernel, len(sums)),
        in_specs=whole_vmem(len(sums) + len(pieces)),
        out_specs=pl.BlockSpec(memory_space=pltpu.VMEM),
        out_shape=jax.ShapeDtypeStruct(sums[0].shape, jnp.bfloat16),
        compiler_params=params(),
        name="stepped_slice",
    )(*sums, *pieces)


def outer_kernel(par_ref, mom_ref, *refs):
    stepped, (new_par, new_mom, all_ref) = refs[:-3], refs[-3:]
    width = stepped[0].shape[1]
    for k, part in enumerate(stepped):
        all_ref[lax.axis_index("rep") ^ k] = part[...].astype(jnp.float32)
    for r in range(len(stepped)):
        cols = slice(r * width, (r + 1) * width)
        old = par_ref[:, cols]
        pseudo = old - all_ref[r]
        fresh = momentum_decay * mom_ref[:, cols] + pseudo
        new_mom[:, cols] = fresh
        new_par[:, cols] = old - outer_rate * (pseudo + momentum_decay * fresh)


def outer_step(global_params, momentum, stepped):
    return pl.pallas_call(
        outer_kernel,
        in_specs=whole_vmem(2 + len(stepped)),
        out_specs=whole_vmem(2),
        out_shape=[jax.ShapeDtypeStruct(global_params.shape, jnp.float32)] * 2,
        scratch_shapes=[pltpu.VMEM((len(stepped),) + stepped[0].shape, jnp.float32)],
        compiler_params=params(),
        name="outer_step",
    )(global_params, momentum, *stepped)


def on_device(
    sizes,
    block_input,
    ssd_input,
    out_grad,
    start_state,
    step_bias,
    decay_log,
    local_params,
    global_params,
    momentum,
):
    replicas, chips, cores = sizes
    local_rows = local_params[0]
    rows, depth = local_rows.shape
    own = rounded(local_rows)
    seq_width = ssd_input.shape[1]
    blocks = start_state.shape[0]
    block = block_input.shape[0] // blocks
    fast = (
        cores == 2
        and chips == 4
        and rows % 8 == 0
        and replicas & (replicas - 1) == 0
        and depth % (128 * replicas) == 0
    )

    def send(value, axis, k):
        count = dict(rep=replicas, line=chips, core=cores)[axis]
        return lax.ppermute(value, axis, [(i, i ^ k) for i in range(count)])

    def send_each(values, axis):
        values = [(k, v) for k, v in enumerate(values, 1)]
        return [sent for sent in reversed([send(v, axis, k) for k, v in reversed(values)])]

    if fast:
        far = send(own, "line", 3)
        near = send(own, "line", 1)
        order = (0, 2, 6, 1, 3, 7, 4, 5)
    else:
        late = [lax.all_gather(own, ("line", "core"), axis=0, tiled=True)]
        weights = []
        order = (0,)

    early = [[], []]
    states = [start_state[b].reshape(seq_width, STATE) for b in range(blocks)]
    states, own_late = lax.optimization_barrier((states, own))
    for b in range(blocks):
        seq = slice(b * block, (b + 1) * block)
        for half in range(2):
            early[half].append(
                early_products(out_grad[seq], ssd_input[seq], states[b], half, seq_width // 2)
            )
    if fast:
        pieces = column_pieces(block_input, own_late, replicas)
        far, _ = lax.optimization_barrier((far, pieces))
        pieces = [pieces[0]] + send_each(pieces[1:], "rep")
        far, near, early = lax.optimization_barrier((far, near, early))
        middle = send(far, "line", 1)
        middle, pieces[-1] = lax.optimization_barrier((middle, pieces[-1]))
        late_near, pieces[-1] = lax.optimization_barrier((near, pieces[-1]))
        pair = send(jnp.concatenate([own, late_near], axis=0), "core", 1)
        weights = [own, near, far, pair, send(far, "core", 1)]
        middle, weights = lax.optimization_barrier((middle, weights))
        late = [middle, send(middle, "core", 1)]

    begun = []
    if fast:
        begun = [
            first_projection(block_input[b * block : (b + 1) * block], weights)
            for b in range(blocks)
        ]

    grads, mine, other = [], [], []
    for b in range(blocks):
        seq = slice(b * block, (b + 1) * block)
        parts = ssd_backward(
            block_input[seq],
            step_bias,
            decay_log,
            [early[0][b][0], early[1][b][0]],
            [early[0][b][1], early[1][b][1]],
            begun[b : b + 1],
            late,
            order,
        )
        for kept, part in zip((grads, mine, other), parts):
            kept.append(part)
    grad, mine, other = (
        kept[0] if blocks == 1 else jnp.concatenate(kept, axis=1) for kept in (grads, mine, other)
    )
    block_grad = block_gradient(grad, weights + late)

    if not fast:
        gradient = lax.psum_scatter(
            contract(grad, block_input, ((1,), (0,))),
            ("line", "core"),
            scatter_dimension=0,
            tiled=True,
        )
        pseudo = global_params - (local_rows - inner_rate * gradient)
        mean_pseudo = lax.psum(pseudo.astype(jnp.bfloat16), "rep").astype(jnp.float32) / replicas
        new_momentum = momentum_decay * momentum + mean_pseudo
        new_params = global_params - outer_rate * (mean_pseudo + momentum_decay * new_momentum)
        return (block_grad, new_params, new_momentum)

    tokens = blocks * block
    other = send(other, "core", 1)
    other, pieces = lax.optimization_barrier((other, pieces))
    both = jnp.concatenate([mine, other], axis=0)
    plane = [both] + send_each([both] * (replicas - 1), "rep")
    twin = send(jnp.concatenate([p[:tokens] for p in pieces], axis=0), "core", 1)
    sums = gradient_slice(plane, pieces, twin, chips)
    sums = [sums[0]] + send_each(sums[1:], "line")
    sums, block_grad = lax.optimization_barrier((sums, block_grad))
    stepped = stepped_slice(sums, pieces)
    stepped = [stepped] + send_each([stepped] * (replicas - 1), "rep")
    new_params, new_momentum = outer_step(global_params, momentum, stepped)
    return (block_grad, new_params, new_momentum)


def solution(mesh):
    replicas, shards = mesh.shape["rep"], mesh.shape["fsdp"]
    cores = 2 if shards % 2 == 0 else 1
    sizes = (replicas, shards // cores, cores)
    apart = jax.sharding.Mesh(mesh.devices.reshape(sizes), ("rep", "line", "core"))
    fsdp = ("line", "core")
    rows = P(("rep", "line", "core"), None)
    placed = (
        rows,
        rows,
        rows,
        P(("rep", "line", "core"), None, None),
        P(),
        P(),
        P("rep", fsdp, None),
        P(fsdp, None),
        P(fsdp, None),
    )
    return jax.shard_map(
        functools.partial(on_device, sizes),
        mesh=apart,
        in_specs=placed,
        out_specs=(rows, P(fsdp, None), P(fsdp, None)),
        check_vma=False,
    )
```

```python
import functools

import jax
import jax.numpy as jnp
from jax import lax
from jax.experimental import pallas as pl
from jax.experimental.pallas import tpu as pltpu
from jax.sharding import PartitionSpec as P

STATE = 64
LOG2E = 1.4426950408889634

inner_rate = 0.002
outer_rate = 0.7
momentum_decay = 0.9

VMEM_LIMIT = 20 * 1024 * 1024


def params(**more):
    return pltpu.CompilerParams(vmem_limit_bytes=VMEM_LIMIT, **more)


def whole_vmem(count):
    return [pl.BlockSpec(memory_space=pltpu.VMEM)] * count


def contract(left, right, dims):
    return lax.dot_general(left, right, (dims, ((), ())), preferred_element_type=jnp.float32)


def terms(value, count):
    out = []
    for _ in range(count):
        out.append(value.astype(jnp.bfloat16))
        value = value - out[-1].astype(jnp.float32)
    return out


def round_kernel(wide_ref, out_ref):
    out_ref[...] = wide_ref[...].astype(out_ref.dtype)


def rounded(wide):
    return pl.pallas_call(
        round_kernel,
        in_specs=whole_vmem(1),
        out_specs=pl.BlockSpec(memory_space=pltpu.VMEM),
        out_shape=jax.ShapeDtypeStruct(wide.shape, jnp.bfloat16),
        compiler_params=params(),
        name="rounded",
    )(wide)


def early_kernel(cot_ref, val_ref, state_ref, cross_ref, enter_ref):
    block = cot_ref.shape[0]
    lanes = lax.broadcasted_iota(jnp.int32, (block, 2 * STATE), 1)
    rows = lax.broadcasted_iota(jnp.int32, (block, block), 0)
    cols = lax.broadcasted_iota(jnp.int32, (block, block), 1)
    causal = rows >= cols
    low = lanes < STATE
    square = (2 * STATE, 2 * STATE)
    same_head = (lax.broadcasted_iota(jnp.int32, square, 0) < STATE) == (
        lax.broadcasted_iota(jnp.int32, square, 1) < STATE
    )
    for pair in range(cot_ref.shape[1] // (2 * STATE)):
        span = slice(pair * 2 * STATE, (pair + 1) * 2 * STATE)
        cot = cot_ref[:, span]
        val = val_ref[:, span]
        zero = jnp.zeros_like(cot)
        for odd in range(2):
            one = jnp.where(low, zero, cot) if odd else jnp.where(low, cot, zero)
            cross = contract(one, val, ((1,), (1,)))
            cross_ref[2 * pair + odd] = jnp.where(causal, cross, 0.0).astype(cross_ref.dtype)
        state = state_ref[span, :]
        wide = jnp.concatenate([state, state], axis=1)
        wide = jnp.where(same_head, wide, jnp.zeros_like(wide))
        enter_ref[:, span] = contract(cot, wide, ((1,), (0,)))


def early_products(out_grad, ssd_input, state, part, width):
    block = out_grad.shape[0]
    heads = width // STATE
    steps = 4
    piece = width // steps
    return pl.pallas_call(
        early_kernel,
        grid=(steps,),
        in_specs=[
            pl.BlockSpec((block, piece), lambda i: (0, part * steps + i)),
            pl.BlockSpec((block, piece), lambda i: (0, part * steps + i)),
            pl.BlockSpec((piece, STATE), lambda i: (part * steps + i, 0)),
        ],
        out_specs=[
            pl.BlockSpec((heads // steps, block, block), lambda i: (i, 0, 0)),
            pl.BlockSpec((block, piece), lambda i: (0, i)),
        ],
        out_shape=[
            jax.ShapeDtypeStruct((heads, block, block), jnp.bfloat16),
            jax.ShapeDtypeStruct((block, width), jnp.float32),
        ],
        compiler_params=params(),
        cost_estimate=pl.CostEstimate(flops=1, bytes_accessed=1, transcendentals=0),
        name="early_products",
    )(out_grad, ssd_input, state)


def stacked(refs):
    if len(refs) == 1:
        return refs[0][...]
    return jnp.concatenate([r[...].astype(jnp.float32) for r in refs], axis=0).astype(jnp.bfloat16)


def own_place(cores):
    return lax.axis_index("rep"), lax.axis_index("line") * cores + lax.axis_index("core")


def shard_rows(index, k, rows):
    return pl.ds(pl.multiple_of((index ^ k) * rows, 8), rows)


def first_kernel(rows_ref, *refs):
    refs[-1][...] = contract(stacked(refs[:-1]), rows_ref[...], ((1,), (1,)))


def first_projection(rows_in, weights):
    rows = sum(w.shape[0] for w in weights)
    return pl.pallas_call(
        first_kernel,
        in_specs=whole_vmem(1 + len(weights)),
        out_specs=pl.BlockSpec(memory_space=pltpu.VMEM),
        out_shape=jax.ShapeDtypeStruct((rows, rows_in.shape[0]), jnp.float32),
        compiler_params=params(),
        cost_estimate=pl.CostEstimate(flops=1, bytes_accessed=1, transcendentals=0),
        name="first_projection",
    )(rows_in, *weights)


def ssd_kernel(order, first, rows_ref, bias_ref, decay_ref, *rest):
    shards = len(order)
    cross_refs, enter_refs, rest = rest[:2], rest[2:4], rest[4:]
    _, spot = own_place(2) if shards > 1 else (0, 0)
    first_ref, rest = (rest[0], rest[1:]) if first else (None, rest)
    weight_refs, rest = rest[: shards - first], rest[shards - first :]
    grad_ref, mine_ref, other_ref, proj_ref, col_ref, out_ref = rest
    block = rows_ref.shape[0]
    heads = bias_ref.shape[1]
    per = weight_refs[0].shape[0]
    arrived = contract(stacked(weight_refs), rows_ref[...], ((1,), (1,)))
    if shards == 1:
        proj_ref[...] = arrived
    else:
        for at, k in enumerate(order):
            source, line = (first_ref, at) if at < first else (arrived, at - first)
            proj_ref[shard_rows(spot, k, per), :] = source[line * per : (line + 1) * per]
    key_t = proj_ref[:STATE, :]
    query_t = proj_ref[STATE : 2 * STATE, :]
    bias_t = jnp.broadcast_to(bias_ref[...], (block, heads)).T
    rate = jnp.exp(jnp.broadcast_to(decay_ref[...], (block, heads)).T)
    raw = proj_ref[2 * STATE :, :] + bias_t
    step_t = jnp.maximum(raw, 0.0) + jnp.log1p(jnp.exp(-jnp.abs(raw)))
    up = lax.broadcasted_iota(jnp.int32, (block, block), 0)
    across = lax.broadcasted_iota(jnp.int32, (block, block), 1)
    before = jnp.where(up <= across, 1.0, 0.0).astype(jnp.bfloat16)
    after = jnp.where(up >= across, 1.0, 0.0).astype(jnp.bfloat16)
    cum_t = LOG2E * contract(
        jnp.concatenate(terms(-step_t * rate, 3), axis=1),
        jnp.concatenate([before] * 3, axis=0),
        ((1,), (0,)),
    )
    cum = cum_t.T
    step = step_t.T
    query = query_t.T
    query_high, query_low = terms(query, 2)
    key_high, key_low = terms(key_t, 2)
    scores = contract(
        jnp.concatenate([query_high, query_high, query_low], axis=1),
        jnp.concatenate([key_high, key_low, key_high], axis=0),
        ((1,), (0,)),
    )
    entered = jnp.exp2(cum)
    query_twice = jnp.concatenate([query, query], axis=1)
    low = lax.broadcasted_iota(jnp.int32, (block, 2 * STATE), 1) < STATE
    head_of = lax.broadcasted_iota(jnp.int32, (block, heads), 1)
    below = lax.broadcasted_iota(jnp.int32, (block, heads), 0) < STATE

    score_grad = jnp.zeros((block, block), jnp.float32)
    query_grad = jnp.zeros((block, 2 * STATE), jnp.float32)
    row_sums = jnp.zeros((block, heads), jnp.float32)
    for h0 in range(0, heads, 4):
        left, right = [], []
        for h in range(h0, h0 + 4):
            span = cum[:, h : h + 1] - cum_t[h : h + 1, :]
            cross = cross_refs[2 * h // heads][h % (heads // 2)]
            weight = cross.astype(jnp.float32) * jnp.exp2(jnp.minimum(span, 0.0))
            score_grad = score_grad + weight * step_t[h : h + 1, :]
            mixed = weight * scores
            col_ref[h : h + 1, :] = jnp.sum(mixed, axis=0, keepdims=True)
            left.append(mixed.astype(jnp.bfloat16))
            right.append(jnp.where(head_of == h, step, 0.0).astype(jnp.bfloat16))
        for h in range(h0, h0 + 4, 2):
            gain = jnp.where(low, entered[:, h : h + 1], entered[:, h + 1 : h + 2])
            at = h % (heads // 2) * STATE
            part = enter_refs[2 * h // heads][:, at : at + 2 * STATE] * gain
            query_grad = query_grad + part
            left.append((part * query_twice).astype(jnp.bfloat16))
            right.append(
                jnp.where(head_of == jnp.where(below, h, h + 1), 1.0, 0.0).astype(jnp.bfloat16)
            )
        row_sums = row_sums + contract(
            jnp.concatenate(left, axis=1), jnp.concatenate(right, axis=0), ((1,), (0,))
        )

    cols_t = col_ref[...]
    cum_grad = row_sums.T - step_t * cols_t
    later = contract(
        jnp.concatenate(terms(cum_grad, 2), axis=1),
        jnp.concatenate([after] * 2, axis=0),
        ((1,), (0,)),
    )
    step_grad = cols_t - rate * later
    raw_grad = step_grad / (1.0 + jnp.exp(-raw))
    score_grad = score_grad.astype(jnp.bfloat16)
    out_ref[:STATE, :] = contract(query_t.astype(jnp.bfloat16), score_grad, ((1,), (0,)))
    query_all = (query_grad[:, :STATE] + query_grad[:, STATE:]).T
    out_ref[STATE : 2 * STATE, :] = query_all + contract(key_high, score_grad, ((1,), (1,)))
    out_ref[2 * STATE :, :] = raw_grad
    if shards == 1:
        grad_ref[...] = out_ref[...].astype(jnp.bfloat16)
        mine_ref[...] = jnp.zeros_like(mine_ref)
        other_ref[...] = jnp.zeros_like(other_ref)
        return
    core = spot % 2
    for part, ref in ((core, mine_ref), (1 - core, other_ref)):
        of_core = [out_ref[shard_rows(f + part, 0, per), :] for f in range(0, shards, 2)]
        ref[...] = jnp.concatenate(of_core, axis=0).astype(jnp.bfloat16)
    for at, k in enumerate(order):
        proj_ref[at * per : (at + 1) * per, :] = out_ref[shard_rows(spot, k, per), :]
    grad_ref[...] = proj_ref[...].astype(jnp.bfloat16)


def ssd_backward(rows_in, step_bias, decay_log, cross, enter, first, weights, order):
    block = rows_in.shape[0]
    heads = step_bias.shape[0]
    cols = len(order) * weights[0].shape[0]
    half = (cols // 2, block)
    return pl.pallas_call(
        functools.partial(ssd_kernel, order, len(order) - len(weights)),
        in_specs=whole_vmem(7 + len(first) + len(weights)),
        out_specs=whole_vmem(3),
        out_shape=[
            jax.ShapeDtypeStruct((cols, block), jnp.bfloat16),
            jax.ShapeDtypeStruct(half, jnp.bfloat16),
            jax.ShapeDtypeStruct(half, jnp.bfloat16),
        ],
        scratch_shapes=[
            pltpu.VMEM((cols, block), jnp.float32),
            pltpu.VMEM((heads, block), jnp.float32),
            pltpu.VMEM((cols, block), jnp.float32),
        ],
        compiler_params=params(),
        cost_estimate=pl.CostEstimate(flops=1, bytes_accessed=1, transcendentals=0),
        name="ssd_backward",
    )(rows_in, step_bias.reshape(1, -1), decay_log.reshape(1, -1), *cross, *enter, *first, *weights)


def block_grad_kernel(grad_ref, *refs):
    out_ref = refs[-1]
    weights = stacked(refs[:-1])
    out_ref[...] = contract(grad_ref[...].T, weights, ((1,), (0,))).astype(out_ref.dtype)


def block_gradient(grad, weights):
    depth = weights[0].shape[1]
    cols, block = grad.shape
    return pl.pallas_call(
        block_grad_kernel,
        in_specs=whole_vmem(1 + len(weights)),
        out_specs=pl.BlockSpec(memory_space=pltpu.VMEM),
        out_shape=jax.ShapeDtypeStruct((block, depth), jnp.bfloat16),
        compiler_params=params(),
        cost_estimate=pl.CostEstimate(
            flops=2 * block * cols * depth, bytes_accessed=4 * cols * depth, transcendentals=0
        ),
        name="block_gradient",
    )(grad, *weights)


def pieces_kernel(rows_ref, own_ref, *outs):
    block = rows_ref.shape[0]
    rep, _ = own_place(2)
    width = outs[0].shape[1]
    for k, out in enumerate(outs):
        cols = pl.ds(pl.multiple_of((rep ^ k) * width, 128), width)
        out[:block, :] = rows_ref[:, cols]
        out[block:, :] = own_ref[:, cols]


def column_pieces(rows_in, own, replicas):
    tokens, depth = rows_in.shape
    shape = (tokens + own.shape[0], depth // replicas)
    return pl.pallas_call(
        pieces_kernel,
        in_specs=whole_vmem(2),
        out_specs=whole_vmem(replicas),
        out_shape=[jax.ShapeDtypeStruct(shape, jnp.bfloat16)] * replicas,
        compiler_params=params(),
        name="column_pieces",
    )(rows_in, own)


def slice_kernel(replicas, *refs):
    grads, pieces, refs = refs[:replicas], refs[replicas : 2 * replicas], refs[2 * replicas :]
    twin, outs, total = refs[0], refs[1:-1], refs[-1]
    tokens = twin.shape[0] // replicas
    rows = total.shape[0]
    left, right = [], []
    for other in range(2):
        for k in range(replicas):
            left.append(grads[k][other * rows : (other + 1) * rows, :])
            right.append(
                twin[k * tokens : (k + 1) * tokens, :] if other else pieces[k][:tokens, :]
            )
    total[...] = contract(
        jnp.concatenate(left, axis=1), jnp.concatenate(right, axis=0), ((1,), (0,))
    )
    per = outs[0].shape[0]
    chip = lax.axis_index("line")
    for k, out in enumerate(outs):
        out[...] = total[shard_rows(chip, k, per), :].astype(jnp.bfloat16)


def gradient_slice(grads, pieces, twin, chips):
    rows = grads[0].shape[0] // (2 * chips)
    width = twin.shape[1]
    return pl.pallas_call(
        functools.partial(slice_kernel, len(pieces)),
        in_specs=whole_vmem(1 + 2 * len(pieces)),
        out_specs=whole_vmem(chips),
        out_shape=[jax.ShapeDtypeStruct((rows, width), jnp.bfloat16)] * chips,
        scratch_shapes=[pltpu.VMEM((rows * chips, width), jnp.float32)],
        compiler_params=params(),
        name="gradient_slice",
    )(*grads, *pieces, twin)


def stepped_kernel(chips, *refs):
    sums, pieces, out_ref = refs[:chips], refs[chips:-1], refs[-1]
    rows = out_ref.shape[0]
    total = sums[0][...].astype(jnp.float32)
    for part in sums[1:]:
        total = total + part[...].astype(jnp.float32)
    level = pieces[0][-rows:, :].astype(jnp.float32)
    for piece in pieces[1:]:
        level = level + piece[-rows:, :].astype(jnp.float32)
    mean = (level - inner_rate * total) * (1.0 / len(pieces))
    out_ref[...] = mean.astype(jnp.bfloat16)


def stepped_slice(sums, pieces):
    return pl.pallas_call(
        functools.partial(stepped_kernel, len(sums)),
        in_specs=whole_vmem(len(sums) + len(pieces)),
        out_specs=pl.BlockSpec(memory_space=pltpu.VMEM),
        out_shape=jax.ShapeDtypeStruct(sums[0].shape, jnp.bfloat16),
        compiler_params=params(),
        name="stepped_slice",
    )(*sums, *pieces)


def outer_kernel(par_ref, mom_ref, *refs):
    stepped, (new_par, new_mom, all_ref) = refs[:-3], refs[-3:]
    width = stepped[0].shape[1]
    for k, part in enumerate(stepped):
        all_ref[lax.axis_index("rep") ^ k] = part[...].astype(jnp.float32)
    for r in range(len(stepped)):
        cols = slice(r * width, (r + 1) * width)
        old = par_ref[:, cols]
        pseudo = old - all_ref[r]
        fresh = momentum_decay * mom_ref[:, cols] + pseudo
        new_mom[:, cols] = fresh
        new_par[:, cols] = old - outer_rate * (pseudo + momentum_decay * fresh)


def outer_step(global_params, momentum, stepped):
    return pl.pallas_call(
        outer_kernel,
        in_specs=whole_vmem(2 + len(stepped)),
        out_specs=whole_vmem(2),
        out_shape=[jax.ShapeDtypeStruct(global_params.shape, jnp.float32)] * 2,
        scratch_shapes=[pltpu.VMEM((len(stepped),) + stepped[0].shape, jnp.float32)],
        compiler_params=params(),
        name="outer_step",
    )(global_params, momentum, *stepped)


def on_device(
    sizes,
    block_input,
    ssd_input,
    out_grad,
    start_state,
    step_bias,
    decay_log,
    local_params,
    global_params,
    momentum,
):
    replicas, chips, cores = sizes
    local_rows = local_params[0]
    rows, depth = local_rows.shape
    own = rounded(local_rows)
    seq_width = ssd_input.shape[1]
    blocks = start_state.shape[0]
    block = block_input.shape[0] // blocks
    fast = (
        cores == 2
        and chips == 4
        and rows % 8 == 0
        and replicas & (replicas - 1) == 0
        and depth % (128 * replicas) == 0
    )

    def send(value, axis, k):
        count = dict(rep=replicas, line=chips, core=cores)[axis]
        return lax.ppermute(value, axis, [(i, i ^ k) for i in range(count)])

    def send_each(values, axis):
        values = [(k, v) for k, v in enumerate(values, 1)]
        return [sent for sent in reversed([send(v, axis, k) for k, v in reversed(values)])]

    if fast:
        far = send(own, "line", 3)
        near = send(own, "line", 1)
        order = (0, 2, 6, 1, 3, 7, 4, 5)
    else:
        late = [lax.all_gather(own, ("line", "core"), axis=0, tiled=True)]
        weights = []
        order = (0,)

    early = [[], []]
    states = [start_state[b].reshape(seq_width, STATE) for b in range(blocks)]
    states, own_late = lax.optimization_barrier((states, own))
    for b in range(blocks):
        seq = slice(b * block, (b + 1) * block)
        for half in range(2):
            early[half].append(
                early_products(out_grad[seq], ssd_input[seq], states[b], half, seq_width // 2)
            )
    if fast:
        pieces = column_pieces(block_input, own_late, replicas)
        far, _ = lax.optimization_barrier((far, pieces))
        pieces = [pieces[0]] + send_each(pieces[1:], "rep")
        far, near, early = lax.optimization_barrier((far, near, early))
        middle = send(far, "line", 1)
        middle, pieces[-1] = lax.optimization_barrier((middle, pieces[-1]))
        pair = send(jnp.concatenate([own, near], axis=0), "core", 1)
        weights = [own, near, far, pair, send(far, "core", 1)]
        middle, weights = lax.optimization_barrier((middle, weights))
        late = [middle, send(middle, "core", 1)]

    begun = []
    if fast:
        begun = [
            first_projection(block_input[b * block : (b + 1) * block], weights)
            for b in range(blocks)
        ]

    grads, mine, other = [], [], []
    for b in range(blocks):
        seq = slice(b * block, (b + 1) * block)
        parts = ssd_backward(
            block_input[seq],
            step_bias,
            decay_log,
            [early[0][b][0], early[1][b][0]],
            [early[0][b][1], early[1][b][1]],
            begun[b : b + 1],
            late,
            order,
        )
        for kept, part in zip((grads, mine, other), parts):
            kept.append(part)
    grad, mine, other = (
        kept[0] if blocks == 1 else jnp.concatenate(kept, axis=1) for kept in (grads, mine, other)
    )
    block_grad = block_gradient(grad, weights + late)

    if not fast:
        gradient = lax.psum_scatter(
            contract(grad, block_input, ((1,), (0,))),
            ("line", "core"),
            scatter_dimension=0,
            tiled=True,
        )
        pseudo = global_params - (local_rows - inner_rate * gradient)
        mean_pseudo = lax.psum(pseudo.astype(jnp.bfloat16), "rep").astype(jnp.float32) / replicas
        new_momentum = momentum_decay * momentum + mean_pseudo
        new_params = global_params - outer_rate * (mean_pseudo + momentum_decay * new_momentum)
        return (block_grad, new_params, new_momentum)

    tokens = blocks * block
    other = send(other, "core", 1)
    other, pieces = lax.optimization_barrier((other, pieces))
    both = jnp.concatenate([mine, other], axis=0)
    plane = [both] + send_each([both] * (replicas - 1), "rep")
    twin = send(jnp.concatenate([p[:tokens] for p in pieces], axis=0), "core", 1)
    sums = gradient_slice(plane, pieces, twin, chips)
    sums = [sums[0]] + send_each(sums[1:], "line")
    sums, block_grad = lax.optimization_barrier((sums, block_grad))
    stepped = stepped_slice(sums, pieces)
    stepped = [stepped] + send_each([stepped] * (replicas - 1), "rep")
    new_params, new_momentum = outer_step(global_params, momentum, stepped)
    return (block_grad, new_params, new_momentum)


def solution(mesh):
    replicas, shards = mesh.shape["rep"], mesh.shape["fsdp"]
    cores = 2 if shards % 2 == 0 else 1
    sizes = (replicas, shards // cores, cores)
    apart = jax.sharding.Mesh(mesh.devices.reshape(sizes), ("rep", "line", "core"))
    fsdp = ("line", "core")
    rows = P(("rep", "line", "core"), None)
    placed = (
        rows,
        rows,
        rows,
        P(("rep", "line", "core"), None, None),
        P(),
        P(),
        P("rep", fsdp, None),
        P(fsdp, None),
        P(fsdp, None),
    )
    return jax.shard_map(
        functools.partial(on_device, sizes),
        mesh=apart,
        in_specs=placed,
        out_specs=(rows, P(fsdp, None), P(fsdp, None)),
        check_vma=False,
    )
```

```python
import functools

import jax
import jax.numpy as jnp
from jax import lax
from jax.experimental import pallas as pl
from jax.experimental.pallas import tpu as pltpu
from jax.sharding import PartitionSpec as P

STATE = 64
LOG2E = 1.4426950408889634

inner_rate = 0.002
outer_rate = 0.7
momentum_decay = 0.9

VMEM_LIMIT = 20 * 1024 * 1024


def params(**more):
    return pltpu.CompilerParams(vmem_limit_bytes=VMEM_LIMIT, **more)


def whole_vmem(count):
    return [pl.BlockSpec(memory_space=pltpu.VMEM)] * count


def contract(left, right, dims):
    return lax.dot_general(left, right, (dims, ((), ())), preferred_element_type=jnp.float32)


def terms(value, count):
    out = []
    for _ in range(count):
        out.append(value.astype(jnp.bfloat16))
        value = value - out[-1].astype(jnp.float32)
    return out


def round_kernel(wide_ref, out_ref):
    out_ref[...] = wide_ref[...].astype(out_ref.dtype)


def rounded(wide):
    return pl.pallas_call(
        round_kernel,
        in_specs=whole_vmem(1),
        out_specs=pl.BlockSpec(memory_space=pltpu.VMEM),
        out_shape=jax.ShapeDtypeStruct(wide.shape, jnp.bfloat16),
        compiler_params=params(),
        name="rounded",
    )(wide)


def early_kernel(cot_ref, val_ref, state_ref, cross_ref, enter_ref):
    block = cot_ref.shape[0]
    lanes = lax.broadcasted_iota(jnp.int32, (block, 2 * STATE), 1)
    rows = lax.broadcasted_iota(jnp.int32, (block, block), 0)
    cols = lax.broadcasted_iota(jnp.int32, (block, block), 1)
    causal = rows >= cols
    low = lanes < STATE
    square = (2 * STATE, 2 * STATE)
    same_head = (lax.broadcasted_iota(jnp.int32, square, 0) < STATE) == (
        lax.broadcasted_iota(jnp.int32, square, 1) < STATE
    )
    for pair in range(cot_ref.shape[1] // (2 * STATE)):
        span = slice(pair * 2 * STATE, (pair + 1) * 2 * STATE)
        cot = cot_ref[:, span]
        val = val_ref[:, span]
        zero = jnp.zeros_like(cot)
        for odd in range(2):
            one = jnp.where(low, zero, cot) if odd else jnp.where(low, cot, zero)
            cross = contract(one, val, ((1,), (1,)))
            cross_ref[2 * pair + odd] = jnp.where(causal, cross, 0.0).astype(cross_ref.dtype)
        state = state_ref[span, :]
        wide = jnp.concatenate([state, state], axis=1)
        wide = jnp.where(same_head, wide, jnp.zeros_like(wide))
        enter_ref[:, span] = contract(cot, wide, ((1,), (0,)))


def early_products(out_grad, ssd_input, state, part, width):
    block = out_grad.shape[0]
    heads = width // STATE
    steps = 4
    piece = width // steps
    return pl.pallas_call(
        early_kernel,
        grid=(steps,),
        in_specs=[
            pl.BlockSpec((block, piece), lambda i: (0, part * steps + i)),
            pl.BlockSpec((block, piece), lambda i: (0, part * steps + i)),
            pl.BlockSpec((piece, STATE), lambda i: (part * steps + i, 0)),
        ],
        out_specs=[
            pl.BlockSpec((heads // steps, block, block), lambda i: (i, 0, 0)),
            pl.BlockSpec((block, piece), lambda i: (0, i)),
        ],
        out_shape=[
            jax.ShapeDtypeStruct((heads, block, block), jnp.bfloat16),
            jax.ShapeDtypeStruct((block, width), jnp.float32),
        ],
        compiler_params=params(),
        cost_estimate=pl.CostEstimate(flops=1, bytes_accessed=1, transcendentals=0),
        name="early_products",
    )(out_grad, ssd_input, state)


def stacked(refs):
    if len(refs) == 1:
        return refs[0][...]
    return jnp.concatenate([r[...].astype(jnp.float32) for r in refs], axis=0).astype(jnp.bfloat16)


def own_place(cores):
    return lax.axis_index("rep"), lax.axis_index("line") * cores + lax.axis_index("core")


def shard_rows(index, k, rows):
    return pl.ds(pl.multiple_of((index ^ k) * rows, 8), rows)


def first_kernel(rows_ref, *refs):
    refs[-1][...] = contract(stacked(refs[:-1]), rows_ref[...], ((1,), (1,)))


def first_projection(rows_in, weights):
    rows = sum(w.shape[0] for w in weights)
    return pl.pallas_call(
        first_kernel,
        in_specs=whole_vmem(1 + len(weights)),
        out_specs=pl.BlockSpec(memory_space=pltpu.VMEM),
        out_shape=jax.ShapeDtypeStruct((rows, rows_in.shape[0]), jnp.float32),
        compiler_params=params(),
        cost_estimate=pl.CostEstimate(flops=1, bytes_accessed=1, transcendentals=0),
        name="first_projection",
    )(rows_in, *weights)


def ssd_kernel(order, first, rows_ref, bias_ref, decay_ref, *rest):
    shards = len(order)
    cross_refs, enter_refs, rest = rest[:2], rest[2:4], rest[4:]
    _, spot = own_place(2) if shards > 1 else (0, 0)
    first_ref, rest = (rest[0], rest[1:]) if first else (None, rest)
    weight_refs, rest = rest[: shards - first], rest[shards - first :]
    grad_ref, send_ref, proj_ref, col_ref, out_ref = rest
    block = rows_ref.shape[0]
    heads = bias_ref.shape[1]
    per = weight_refs[0].shape[0]
    arrived = contract(stacked(weight_refs), rows_ref[...], ((1,), (1,)))
    if shards == 1:
        proj_ref[...] = arrived
    else:
        for at, k in enumerate(order):
            source, line = (first_ref, at) if at < first else (arrived, at - first)
            proj_ref[shard_rows(spot, k, per), :] = source[line * per : (line + 1) * per]
    key_t = proj_ref[:STATE, :]
    query_t = proj_ref[STATE : 2 * STATE, :]
    bias_t = jnp.broadcast_to(bias_ref[...], (block, heads)).T
    rate = jnp.exp(jnp.broadcast_to(decay_ref[...], (block, heads)).T)
    raw = proj_ref[2 * STATE :, :] + bias_t
    step_t = jnp.maximum(raw, 0.0) + jnp.log1p(jnp.exp(-jnp.abs(raw)))
    up = lax.broadcasted_iota(jnp.int32, (block, block), 0)
    across = lax.broadcasted_iota(jnp.int32, (block, block), 1)
    before = jnp.where(up <= across, 1.0, 0.0).astype(jnp.bfloat16)
    after = jnp.where(up >= across, 1.0, 0.0).astype(jnp.bfloat16)
    cum_t = LOG2E * contract(
        jnp.concatenate(terms(-step_t * rate, 3), axis=1),
        jnp.concatenate([before] * 3, axis=0),
        ((1,), (0,)),
    )
    cum = cum_t.T
    step = step_t.T
    query = query_t.T
    query_high, query_low = terms(query, 2)
    key_high, key_low = terms(key_t, 2)
    scores = contract(
        jnp.concatenate([query_high, query_high, query_low], axis=1),
        jnp.concatenate([key_high, key_low, key_high], axis=0),
        ((1,), (0,)),
    )
    entered = jnp.exp2(cum)
    query_twice = jnp.concatenate([query, query], axis=1)
    low = lax.broadcasted_iota(jnp.int32, (block, 2 * STATE), 1) < STATE
    head_of = lax.broadcasted_iota(jnp.int32, (block, heads), 1)
    below = lax.broadcasted_iota(jnp.int32, (block, heads), 0) < STATE

    score_grad = jnp.zeros((block, block), jnp.float32)
    query_grad = jnp.zeros((block, 2 * STATE), jnp.float32)
    row_sums = jnp.zeros((block, heads), jnp.float32)
    for h0 in range(0, heads, 4):
        left, right = [], []
        for h in range(h0, h0 + 4):
            span = cum[:, h : h + 1] - cum_t[h : h + 1, :]
            cross = cross_refs[2 * h // heads][h % (heads // 2)]
            weight = cross.astype(jnp.float32) * jnp.exp2(jnp.minimum(span, 0.0))
            score_grad = score_grad + weight * step_t[h : h + 1, :]
            mixed = weight * scores
            col_ref[h : h + 1, :] = jnp.sum(mixed, axis=0, keepdims=True)
            left.append(mixed.astype(jnp.bfloat16))
            right.append(jnp.where(head_of == h, step, 0.0).astype(jnp.bfloat16))
        for h in range(h0, h0 + 4, 2):
            gain = jnp.where(low, entered[:, h : h + 1], entered[:, h + 1 : h + 2])
            at = h % (heads // 2) * STATE
            part = enter_refs[2 * h // heads][:, at : at + 2 * STATE] * gain
            query_grad = query_grad + part
            left.append((part * query_twice).astype(jnp.bfloat16))
            right.append(
                jnp.where(head_of == jnp.where(below, h, h + 1), 1.0, 0.0).astype(jnp.bfloat16)
            )
        row_sums = row_sums + contract(
            jnp.concatenate(left, axis=1), jnp.concatenate(right, axis=0), ((1,), (0,))
        )

    cols_t = col_ref[...]
    cum_grad = row_sums.T - step_t * cols_t
    later = contract(
        jnp.concatenate(terms(cum_grad, 2), axis=1),
        jnp.concatenate([after] * 2, axis=0),
        ((1,), (0,)),
    )
    step_grad = cols_t - rate * later
    raw_grad = step_grad / (1.0 + jnp.exp(-raw))
    score_grad = score_grad.astype(jnp.bfloat16)
    out_ref[:STATE, :] = contract(query_t.astype(jnp.bfloat16), score_grad, ((1,), (0,)))
    query_all = (query_grad[:, :STATE] + query_grad[:, STATE:]).T
    out_ref[STATE : 2 * STATE, :] = query_all + contract(key_high, score_grad, ((1,), (1,)))
    out_ref[2 * STATE :, :] = raw_grad
    if shards == 1:
        grad_ref[...] = out_ref[...].astype(jnp.bfloat16)
        send_ref[...] = jnp.zeros_like(send_ref)
        return
    for core in range(2):
        of_core = [out_ref[f * per : (f + 1) * per, :] for f in range(core, shards, 2)]
        of_core = jnp.concatenate(of_core, axis=0).astype(jnp.bfloat16)
        for r in range(send_ref.shape[0] // 2):
            send_ref[2 * r + core] = of_core
    for at, k in enumerate(order):
        proj_ref[at * per : (at + 1) * per, :] = out_ref[shard_rows(spot, k, per), :]
    grad_ref[...] = proj_ref[...].astype(jnp.bfloat16)


def ssd_backward(
    rows_in, step_bias, decay_log, cross, enter, first, weights, order, replicas
):
    block = rows_in.shape[0]
    heads = step_bias.shape[0]
    cols = len(order) * weights[0].shape[0]
    apart = (2 * replicas, cols // 2, block) if len(order) > 1 else (1, 16, 128)
    return pl.pallas_call(
        functools.partial(ssd_kernel, order, len(order) - len(weights)),
        in_specs=whole_vmem(7 + len(first) + len(weights)),
        out_specs=whole_vmem(2),
        out_shape=[
            jax.ShapeDtypeStruct((cols, block), jnp.bfloat16),
            jax.ShapeDtypeStruct(apart, jnp.bfloat16),
        ],
        scratch_shapes=[
            pltpu.VMEM((cols, block), jnp.float32),
            pltpu.VMEM((heads, block), jnp.float32),
            pltpu.VMEM((cols, block), jnp.float32),
        ],
        compiler_params=params(),
        cost_estimate=pl.CostEstimate(flops=1, bytes_accessed=1, transcendentals=0),
        name="ssd_backward",
    )(rows_in, step_bias.reshape(1, -1), decay_log.reshape(1, -1), *cross, *enter, *first, *weights)


def block_grad_kernel(grad_ref, *refs):
    out_ref = refs[-1]
    weights = stacked(refs[:-1])
    out_ref[...] = contract(grad_ref[...].T, weights, ((1,), (0,))).astype(out_ref.dtype)


def block_gradient(grad, weights):
    depth = weights[0].shape[1]
    cols, block = grad.shape
    return pl.pallas_call(
        block_grad_kernel,
        in_specs=whole_vmem(1 + len(weights)),
        out_specs=pl.BlockSpec(memory_space=pltpu.VMEM),
        out_shape=jax.ShapeDtypeStruct((block, depth), jnp.bfloat16),
        compiler_params=params(),
        cost_estimate=pl.CostEstimate(
            flops=2 * block * cols * depth, bytes_accessed=4 * cols * depth, transcendentals=0
        ),
        name="block_gradient",
    )(grad, *weights)


def pieces_kernel(rows_ref, own_ref, *outs):
    block = rows_ref.shape[0]
    rep, _ = own_place(2)
    width = outs[0].shape[1]
    for k, out in enumerate(outs):
        cols = pl.ds(pl.multiple_of((rep ^ k) * width, 128), width)
        out[:block, :] = rows_ref[:, cols]
        out[block:, :] = own_ref[:, cols]


def column_pieces(rows_in, own, replicas):
    tokens, depth = rows_in.shape
    shape = (tokens + own.shape[0], depth // replicas)
    return pl.pallas_call(
        pieces_kernel,
        in_specs=whole_vmem(2),
        out_specs=whole_vmem(replicas),
        out_shape=[jax.ShapeDtypeStruct(shape, jnp.bfloat16)] * replicas,
        compiler_params=params(),
        name="column_pieces",
    )(rows_in, own)


def slice_kernel(replicas, grads_ref, *refs):
    pieces, refs = refs[:replicas], refs[replicas:]
    early, late, outs, total = refs[0], refs[1], refs[2:-1], refs[-1]
    tokens = early.shape[0] // 2
    rep, core = lax.axis_index("rep"), lax.axis_index("core")
    left = [grads_ref[(rep ^ k) * 2 + (core ^ j)] for j in range(2) for k in range(replicas)]
    right = [piece[:tokens, :] for piece in pieces]
    right += [early[:tokens, :], late[...], early[tokens:, :]]
    total[...] = contract(
        jnp.concatenate(left, axis=1), jnp.concatenate(right, axis=0), ((1,), (0,))
    )
    per = outs[0].shape[0]
    chip = lax.axis_index("line")
    for k, out in enumerate(outs):
        out[...] = total[shard_rows(chip, k, per), :].astype(jnp.bfloat16)


def gradient_slice(grads, pieces, twins, chips):
    rows = grads.shape[1] // chips
    width = twins[0].shape[1]
    return pl.pallas_call(
        functools.partial(slice_kernel, len(pieces)),
        in_specs=whole_vmem(1 + len(pieces) + len(twins)),
        out_specs=whole_vmem(chips),
        out_shape=[jax.ShapeDtypeStruct((rows, width), jnp.bfloat16)] * chips,
        scratch_shapes=[pltpu.VMEM((rows * chips, width), jnp.float32)],
        compiler_params=params(),
        name="gradient_slice",
    )(grads, *pieces, *twins)


def stepped_kernel(chips, *refs):
    sums, pieces, out_ref = refs[:chips], refs[chips:-1], refs[-1]
    rows = out_ref.shape[0]
    total = sums[0][...].astype(jnp.float32)
    for part in sums[1:]:
        total = total + part[...].astype(jnp.float32)
    level = pieces[0][-rows:, :].astype(jnp.float32)
    for piece in pieces[1:]:
        level = level + piece[-rows:, :].astype(jnp.float32)
    mean = (level - inner_rate * total) * (1.0 / len(pieces))
    out_ref[...] = mean.astype(jnp.bfloat16)


def stepped_slice(sums, pieces):
    return pl.pallas_call(
        functools.partial(stepped_kernel, len(sums)),
        in_specs=whole_vmem(len(sums) + len(pieces)),
        out_specs=pl.BlockSpec(memory_space=pltpu.VMEM),
        out_shape=jax.ShapeDtypeStruct(sums[0].shape, jnp.bfloat16),
        compiler_params=params(),
        name="stepped_slice",
    )(*sums, *pieces)


def outer_kernel(par_ref, mom_ref, *refs):
    stepped, (new_par, new_mom, all_ref) = refs[:-3], refs[-3:]
    width = stepped[0].shape[1]
    for k, part in enumerate(stepped):
        all_ref[lax.axis_index("rep") ^ k] = part[...].astype(jnp.float32)
    for r in range(len(stepped)):
        cols = slice(r * width, (r + 1) * width)
        old = par_ref[:, cols]
        pseudo = old - all_ref[r]
        fresh = momentum_decay * mom_ref[:, cols] + pseudo
        new_mom[:, cols] = fresh
        new_par[:, cols] = old - outer_rate * (pseudo + momentum_decay * fresh)


def outer_step(global_params, momentum, stepped):
    return pl.pallas_call(
        outer_kernel,
        in_specs=whole_vmem(2 + len(stepped)),
        out_specs=whole_vmem(2),
        out_shape=[jax.ShapeDtypeStruct(global_params.shape, jnp.float32)] * 2,
        scratch_shapes=[pltpu.VMEM((len(stepped),) + stepped[0].shape, jnp.float32)],
        compiler_params=params(),
        name="outer_step",
    )(global_params, momentum, *stepped)


def on_device(
    sizes,
    block_input,
    ssd_input,
    out_grad,
    start_state,
    step_bias,
    decay_log,
    local_params,
    global_params,
    momentum,
):
    replicas, chips, cores = sizes
    local_rows = local_params[0]
    rows, depth = local_rows.shape
    own = rounded(local_rows)
    seq_width = ssd_input.shape[1]
    blocks = start_state.shape[0]
    block = block_input.shape[0] // blocks
    tokens = blocks * block
    fast = (
        cores == 2
        and chips == 4
        and rows % 8 == 0
        and replicas >= 4
        and replicas & (replicas - 1) == 0
        and depth % (128 * replicas) == 0
    )

    def send(value, axis, k):
        count = dict(rep=replicas, line=chips, core=cores)[axis]
        return lax.ppermute(value, axis, [(i, i ^ k) for i in range(count)])

    def send_each(values, axis):
        values = [(k, v) for k, v in enumerate(values, 1)]
        return [sent for sent in reversed([send(v, axis, k) for k, v in reversed(values)])]

    if fast:
        far = send(own, "line", 3)
        near = send(own, "line", 1)
        order = (0, 2, 6, 1, 3, 7, 4, 5)
    else:
        late = [lax.all_gather(own, ("line", "core"), axis=0, tiled=True)]
        weights = []
        order = (0,)

    early = [[], []]
    states = [start_state[b].reshape(seq_width, STATE) for b in range(blocks)]
    states, own_late = lax.optimization_barrier((states, own))
    for b in range(blocks):
        seq = slice(b * block, (b + 1) * block)
        for half in range(2):
            early[half].append(
                early_products(out_grad[seq], ssd_input[seq], states[b], half, seq_width // 2)
            )
    if fast:
        pieces = column_pieces(block_input, own_late, replicas)
        far, _ = lax.optimization_barrier((far, pieces))
        pieces = [pieces[0]] + send_each(pieces[1:], "rep")
        far, near, early = lax.optimization_barrier((far, near, early))
        middle = send(far, "line", 1)
        middle, pieces[-1] = lax.optimization_barrier((middle, pieces[-1]))
        pair = send(jnp.concatenate([own, near], axis=0), "core", 1)
        weights = [own, near, far, pair, send(far, "core", 1)]
        middle, weights = lax.optimization_barrier((middle, weights))
        late = [middle, send(middle, "core", 1)]

    begun = []
    if fast:
        begun = [
            first_projection(block_input[b * block : (b + 1) * block], weights)
            for b in range(blocks)
        ]

    if fast:
        outer = jnp.concatenate([pieces[0][:tokens], pieces[-1][:tokens]], axis=0)
        begun, outer = lax.optimization_barrier((begun, outer))
        twin = send(outer, "core", 1)

    grads, apart = [], []
    for b in range(blocks):
        seq = slice(b * block, (b + 1) * block)
        parts = ssd_backward(
            block_input[seq],
            step_bias,
            decay_log,
            [early[0][b][0], early[1][b][0]],
            [early[0][b][1], early[1][b][1]],
            begun[b : b + 1],
            late,
            order,
            replicas,
        )
        for kept, part in zip((grads, apart), parts):
            kept.append(part)
    grad = grads[0] if blocks == 1 else jnp.concatenate(grads, axis=1)
    apart = apart[0] if blocks == 1 else jnp.concatenate(apart, axis=2)
    block_grad = block_gradient(grad, weights + late)

    if not fast:
        gradient = lax.psum_scatter(
            contract(grad, block_input, ((1,), (0,))),
            ("line", "core"),
            scatter_dimension=0,
            tiled=True,
        )
        pseudo = global_params - (local_rows - inner_rate * gradient)
        mean_pseudo = lax.psum(pseudo.astype(jnp.bfloat16), "rep").astype(jnp.float32) / replicas
        new_momentum = momentum_decay * momentum + mean_pseudo
        new_params = global_params - outer_rate * (mean_pseudo + momentum_decay * new_momentum)
        return (block_grad, new_params, new_momentum)

    apart, pieces[1:-1] = lax.optimization_barrier((apart, pieces[1:-1]))
    twins = [twin, send(jnp.concatenate([p[:tokens] for p in pieces[1:-1]], axis=0), "core", 1)]
    plane = lax.all_to_all(apart, ("rep", "core"), split_axis=0, concat_axis=0, tiled=True)
    sums = gradient_slice(plane, pieces, twins, chips)
    sums = [sums[0]] + send_each(sums[1:], "line")
    sums, block_grad = lax.optimization_barrier((sums, block_grad))
    stepped = stepped_slice(sums, pieces)
    stepped = [stepped] + send_each([stepped] * (replicas - 1), "rep")
    new_params, new_momentum = outer_step(global_params, momentum, stepped)
    return (block_grad, new_params, new_momentum)


def solution(mesh):
    replicas, shards = mesh.shape["rep"], mesh.shape["fsdp"]
    cores = 2 if shards % 2 == 0 else 1
    sizes = (replicas, shards // cores, cores)
    apart = jax.sharding.Mesh(mesh.devices.reshape(sizes), ("rep", "line", "core"))
    fsdp = ("line", "core")
    rows = P(("rep", "line", "core"), None)
    placed = (
        rows,
        rows,
        rows,
        P(("rep", "line", "core"), None, None),
        P(),
        P(),
        P("rep", fsdp, None),
        P(fsdp, None),
        P(fsdp, None),
    )
    return jax.shard_map(
        functools.partial(on_device, sizes),
        mesh=apart,
        in_specs=placed,
        out_specs=(rows, P(fsdp, None), P(fsdp, None)),
        check_vma=False,
    )
```

```python
import functools

import jax
import jax.numpy as jnp
from jax import lax
from jax.experimental import pallas as pl
from jax.experimental.pallas import tpu as pltpu
from jax.sharding import PartitionSpec as P

STATE = 64
LOG2E = 1.4426950408889634

inner_rate = 0.002
outer_rate = 0.7
momentum_decay = 0.9

VMEM_LIMIT = 20 * 1024 * 1024


def params(**more):
    return pltpu.CompilerParams(vmem_limit_bytes=VMEM_LIMIT, **more)


def whole_vmem(count):
    return [pl.BlockSpec(memory_space=pltpu.VMEM)] * count


def contract(left, right, dims):
    return lax.dot_general(left, right, (dims, ((), ())), preferred_element_type=jnp.float32)


def terms(value, count):
    out = []
    for _ in range(count):
        out.append(value.astype(jnp.bfloat16))
        value = value - out[-1].astype(jnp.float32)
    return out


def round_kernel(wide_ref, out_ref):
    out_ref[...] = wide_ref[...].astype(out_ref.dtype)


def rounded(wide):
    return pl.pallas_call(
        round_kernel,
        in_specs=whole_vmem(1),
        out_specs=pl.BlockSpec(memory_space=pltpu.VMEM),
        out_shape=jax.ShapeDtypeStruct(wide.shape, jnp.bfloat16),
        compiler_params=params(),
        name="rounded",
    )(wide)


def early_kernel(cot_ref, val_ref, state_ref, cross_ref, enter_ref):
    block = cot_ref.shape[0]
    lanes = lax.broadcasted_iota(jnp.int32, (block, 2 * STATE), 1)
    rows = lax.broadcasted_iota(jnp.int32, (block, block), 0)
    cols = lax.broadcasted_iota(jnp.int32, (block, block), 1)
    causal = rows >= cols
    low = lanes < STATE
    square = (2 * STATE, 2 * STATE)
    same_head = (lax.broadcasted_iota(jnp.int32, square, 0) < STATE) == (
        lax.broadcasted_iota(jnp.int32, square, 1) < STATE
    )
    for pair in range(cot_ref.shape[1] // (2 * STATE)):
        span = slice(pair * 2 * STATE, (pair + 1) * 2 * STATE)
        cot = cot_ref[:, span]
        val = val_ref[:, span]
        zero = jnp.zeros_like(cot)
        for odd in range(2):
            one = jnp.where(low, zero, cot) if odd else jnp.where(low, cot, zero)
            cross = contract(one, val, ((1,), (1,)))
            cross_ref[2 * pair + odd] = jnp.where(causal, cross, 0.0).astype(cross_ref.dtype)
        state = state_ref[span, :]
        wide = jnp.concatenate([state, state], axis=1)
        wide = jnp.where(same_head, wide, jnp.zeros_like(wide))
        enter_ref[:, span] = contract(cot, wide, ((1,), (0,)))


def early_products(out_grad, ssd_input, state, part, width):
    block = out_grad.shape[0]
    heads = width // STATE
    steps = 4
    piece = width // steps
    return pl.pallas_call(
        early_kernel,
        grid=(steps,),
        in_specs=[
            pl.BlockSpec((block, piece), lambda i: (0, part * steps + i)),
            pl.BlockSpec((block, piece), lambda i: (0, part * steps + i)),
            pl.BlockSpec((piece, STATE), lambda i: (part * steps + i, 0)),
        ],
        out_specs=[
            pl.BlockSpec((heads // steps, block, block), lambda i: (i, 0, 0)),
            pl.BlockSpec((block, piece), lambda i: (0, i)),
        ],
        out_shape=[
            jax.ShapeDtypeStruct((heads, block, block), jnp.bfloat16),
            jax.ShapeDtypeStruct((block, width), jnp.float32),
        ],
        compiler_params=params(),
        cost_estimate=pl.CostEstimate(flops=1, bytes_accessed=1, transcendentals=0),
        name="early_products",
    )(out_grad, ssd_input, state)


def stacked(refs):
    if len(refs) == 1:
        return refs[0][...]
    return jnp.concatenate([r[...].astype(jnp.float32) for r in refs], axis=0).astype(jnp.bfloat16)


def own_place(cores):
    return lax.axis_index("rep"), lax.axis_index("line") * cores + lax.axis_index("core")


def shard_rows(index, k, rows):
    return pl.ds(pl.multiple_of((index ^ k) * rows, 8), rows)


def first_kernel(rows_ref, *refs):
    refs[-1][...] = contract(stacked(refs[:-1]), rows_ref[...], ((1,), (1,)))


def first_projection(rows_in, weights):
    rows = sum(w.shape[0] for w in weights)
    return pl.pallas_call(
        first_kernel,
        in_specs=whole_vmem(1 + len(weights)),
        out_specs=pl.BlockSpec(memory_space=pltpu.VMEM),
        out_shape=jax.ShapeDtypeStruct((rows, rows_in.shape[0]), jnp.float32),
        compiler_params=params(),
        cost_estimate=pl.CostEstimate(flops=1, bytes_accessed=1, transcendentals=0),
        name="first_projection",
    )(rows_in, *weights)


def ssd_kernel(order, first, rows_ref, bias_ref, decay_ref, *rest):
    shards = len(order)
    cross_refs, enter_refs, rest = rest[:2], rest[2:4], rest[4:]
    _, spot = own_place(2) if shards > 1 else (0, 0)
    first_ref, rest = (rest[0], rest[1:]) if first else (None, rest)
    weight_refs, rest = rest[: shards - first], rest[shards - first :]
    grad_ref, mine_ref, other_ref, proj_ref, col_ref, out_ref = rest
    block = rows_ref.shape[0]
    heads = bias_ref.shape[1]
    per = weight_refs[0].shape[0]
    arrived = contract(stacked(weight_refs), rows_ref[...], ((1,), (1,)))
    if shards == 1:
        proj_ref[...] = arrived
    else:
        for at, k in enumerate(order):
            source, line = (first_ref, at) if at < first else (arrived, at - first)
            proj_ref[shard_rows(spot, k, per), :] = source[line * per : (line + 1) * per]
    key_t = proj_ref[:STATE, :]
    query_t = proj_ref[STATE : 2 * STATE, :]
    bias_t = jnp.broadcast_to(bias_ref[...], (block, heads)).T
    rate = jnp.exp(jnp.broadcast_to(decay_ref[...], (block, heads)).T)
    raw = proj_ref[2 * STATE :, :] + bias_t
    step_t = jnp.maximum(raw, 0.0) + jnp.log1p(jnp.exp(-jnp.abs(raw)))
    up = lax.broadcasted_iota(jnp.int32, (block, block), 0)
    across = lax.broadcasted_iota(jnp.int32, (block, block), 1)
    before = jnp.where(up <= across, 1.0, 0.0).astype(jnp.bfloat16)
    after = jnp.where(up >= across, 1.0, 0.0).astype(jnp.bfloat16)
    cum_t = LOG2E * contract(
        jnp.concatenate(terms(-step_t * rate, 3), axis=1),
        jnp.concatenate([before] * 3, axis=0),
        ((1,), (0,)),
    )
    cum = cum_t.T
    step = step_t.T
    query = query_t.T
    query_high, query_low = terms(query, 2)
    key_high, key_low = terms(key_t, 2)
    scores = contract(
        jnp.concatenate([query_high, query_high, query_low], axis=1),
        jnp.concatenate([key_high, key_low, key_high], axis=0),
        ((1,), (0,)),
    )
    entered = jnp.exp2(cum)
    query_twice = jnp.concatenate([query, query], axis=1)
    low = lax.broadcasted_iota(jnp.int32, (block, 2 * STATE), 1) < STATE
    head_of = lax.broadcasted_iota(jnp.int32, (block, heads), 1)
    below = lax.broadcasted_iota(jnp.int32, (block, heads), 0) < STATE

    score_grad = jnp.zeros((block, block), jnp.float32)
    query_grad = jnp.zeros((block, 2 * STATE), jnp.float32)
    row_sums = jnp.zeros((block, heads), jnp.float32)
    for h0 in range(0, heads, 4):
        left, right = [], []
        for h in range(h0, h0 + 4):
            span = cum[:, h : h + 1] - cum_t[h : h + 1, :]
            cross = cross_refs[2 * h // heads][h % (heads // 2)]
            weight = cross.astype(jnp.float32) * jnp.exp2(jnp.minimum(span, 0.0))
            score_grad = score_grad + weight * step_t[h : h + 1, :]
            mixed = weight * scores
            col_ref[h : h + 1, :] = jnp.sum(mixed, axis=0, keepdims=True)
            left.append(mixed.astype(jnp.bfloat16))
            right.append(jnp.where(head_of == h, step, 0.0).astype(jnp.bfloat16))
        for h in range(h0, h0 + 4, 2):
            gain = jnp.where(low, entered[:, h : h + 1], entered[:, h + 1 : h + 2])
            at = h % (heads // 2) * STATE
            part = enter_refs[2 * h // heads][:, at : at + 2 * STATE] * gain
            query_grad = query_grad + part
            left.append((part * query_twice).astype(jnp.bfloat16))
            right.append(
                jnp.where(head_of == jnp.where(below, h, h + 1), 1.0, 0.0).astype(jnp.bfloat16)
            )
        row_sums = row_sums + contract(
            jnp.concatenate(left, axis=1), jnp.concatenate(right, axis=0), ((1,), (0,))
        )

    cols_t = col_ref[...]
    cum_grad = row_sums.T - step_t * cols_t
    later = contract(
        jnp.concatenate(terms(cum_grad, 2), axis=1),
        jnp.concatenate([after] * 2, axis=0),
        ((1,), (0,)),
    )
    step_grad = cols_t - rate * later
    raw_grad = step_grad / (1.0 + jnp.exp(-raw))
    score_grad = score_grad.astype(jnp.bfloat16)
    out_ref[:STATE, :] = contract(query_t.astype(jnp.bfloat16), score_grad, ((1,), (0,)))
    query_all = (query_grad[:, :STATE] + query_grad[:, STATE:]).T
    out_ref[STATE : 2 * STATE, :] = query_all + contract(key_high, score_grad, ((1,), (1,)))
    out_ref[2 * STATE :, :] = raw_grad
    if shards == 1:
        grad_ref[...] = out_ref[...].astype(jnp.bfloat16)
        mine_ref[...] = jnp.zeros_like(mine_ref)
        other_ref[...] = jnp.zeros_like(other_ref)
        return
    core = spot % 2
    for part, ref in ((core, mine_ref), (1 - core, other_ref)):
        of_core = [out_ref[shard_rows(f + part, 0, per), :] for f in range(0, shards, 2)]
        ref[...] = jnp.concatenate(of_core, axis=0).astype(jnp.bfloat16)
    for at, k in enumerate(order):
        proj_ref[at * per : (at + 1) * per, :] = out_ref[shard_rows(spot, k, per), :]
    grad_ref[...] = proj_ref[...].astype(jnp.bfloat16)


def ssd_backward(rows_in, step_bias, decay_log, cross, enter, first, weights, order):
    block = rows_in.shape[0]
    heads = step_bias.shape[0]
    cols = len(order) * weights[0].shape[0]
    half = (cols // 2, block)
    return pl.pallas_call(
        functools.partial(ssd_kernel, order, len(order) - len(weights)),
        in_specs=whole_vmem(7 + len(first) + len(weights)),
        out_specs=whole_vmem(3),
        out_shape=[
            jax.ShapeDtypeStruct((cols, block), jnp.bfloat16),
            jax.ShapeDtypeStruct(half, jnp.bfloat16),
            jax.ShapeDtypeStruct(half, jnp.bfloat16),
        ],
        scratch_shapes=[
            pltpu.VMEM((cols, block), jnp.float32),
            pltpu.VMEM((heads, block), jnp.float32),
            pltpu.VMEM((cols, block), jnp.float32),
        ],
        compiler_params=params(),
        cost_estimate=pl.CostEstimate(flops=1, bytes_accessed=1, transcendentals=0),
        name="ssd_backward",
    )(rows_in, step_bias.reshape(1, -1), decay_log.reshape(1, -1), *cross, *enter, *first, *weights)


def block_grad_kernel(grad_ref, *refs):
    out_ref = refs[-1]
    weights = stacked(refs[:-1])
    out_ref[...] = contract(grad_ref[...].T, weights, ((1,), (0,))).astype(out_ref.dtype)


def block_gradient(grad, weights):
    depth = weights[0].shape[1]
    cols, block = grad.shape
    return pl.pallas_call(
        block_grad_kernel,
        in_specs=whole_vmem(1 + len(weights)),
        out_specs=pl.BlockSpec(memory_space=pltpu.VMEM),
        out_shape=jax.ShapeDtypeStruct((block, depth), jnp.bfloat16),
        compiler_params=params(),
        cost_estimate=pl.CostEstimate(
            flops=2 * block * cols * depth, bytes_accessed=4 * cols * depth, transcendentals=0
        ),
        name="block_gradient",
    )(grad, *weights)


def pieces_kernel(rows_ref, own_ref, *outs):
    block = rows_ref.shape[0]
    rep, _ = own_place(2)
    width = outs[0].shape[1]
    for k, out in enumerate(outs):
        cols = pl.ds(pl.multiple_of((rep ^ k) * width, 128), width)
        out[:block, :] = rows_ref[:, cols]
        out[block:, :] = own_ref[:, cols]


def column_pieces(rows_in, own, replicas):
    tokens, depth = rows_in.shape
    shape = (tokens + own.shape[0], depth // replicas)
    return pl.pallas_call(
        pieces_kernel,
        in_specs=whole_vmem(2),
        out_specs=whole_vmem(replicas),
        out_shape=[jax.ShapeDtypeStruct(shape, jnp.bfloat16)] * replicas,
        compiler_params=params(),
        name="column_pieces",
    )(rows_in, own)


def slice_kernel(parts, replicas, *refs):
    held, pieces, refs = refs[:parts], refs[parts : parts + replicas], refs[parts + replicas :]
    twin, outs, total = refs[0], refs[1:-1], refs[-1]
    tokens = twin.shape[0] // replicas
    rows = total.shape[0]
    grads = [
        part[at : at + rows, :] for part in held for at in range(0, part.shape[0], rows)
    ]
    right = [piece[:tokens, :] for piece in pieces] + [twin[...]]
    left = grads[::2] + grads[1::2]
    total[...] = contract(
        jnp.concatenate(left, axis=1), jnp.concatenate(right, axis=0), ((1,), (0,))
    )
    per = outs[0].shape[0]
    chip = lax.axis_index("line")
    for k, out in enumerate(outs):
        out[...] = total[shard_rows(chip, k, per), :].astype(jnp.bfloat16)


def gradient_slice(grads, pieces, twin, chips):
    rows = grads[0].shape[0] // (2 * chips)
    width = twin.shape[1]
    return pl.pallas_call(
        functools.partial(slice_kernel, len(grads), len(pieces)),
        in_specs=whole_vmem(1 + len(grads) + len(pieces)),
        out_specs=whole_vmem(chips),
        out_shape=[jax.ShapeDtypeStruct((rows, width), jnp.bfloat16)] * chips,
        scratch_shapes=[pltpu.VMEM((rows * chips, width), jnp.float32)],
        compiler_params=params(),
        name="gradient_slice",
    )(*grads, *pieces, twin)


def stepped_kernel(chips, *refs):
    sums, pieces, out_ref = refs[:chips], refs[chips:-1], refs[-1]
    rows = out_ref.shape[0]
    total = sums[0][...].astype(jnp.float32)
    for part in sums[1:]:
        total = total + part[...].astype(jnp.float32)
    level = pieces[0][-rows:, :].astype(jnp.float32)
    for piece in pieces[1:]:
        level = level + piece[-rows:, :].astype(jnp.float32)
    mean = (level - inner_rate * total) * (1.0 / len(pieces))
    out_ref[...] = mean.astype(jnp.bfloat16)


def stepped_slice(sums, pieces):
    return pl.pallas_call(
        functools.partial(stepped_kernel, len(sums)),
        in_specs=whole_vmem(len(sums) + len(pieces)),
        out_specs=pl.BlockSpec(memory_space=pltpu.VMEM),
        out_shape=jax.ShapeDtypeStruct(sums[0].shape, jnp.bfloat16),
        compiler_params=params(),
        name="stepped_slice",
    )(*sums, *pieces)


def outer_kernel(par_ref, mom_ref, *refs):
    stepped, (new_par, new_mom, all_ref) = refs[:-3], refs[-3:]
    width = stepped[0].shape[1]
    rep, k = lax.axis_index("rep"), 0
    for part in stepped:
        for at in range(0, part.shape[1], width):
            all_ref[rep ^ k] = part[:, at : at + width].astype(jnp.float32)
            k += 1
    for r in range(all_ref.shape[0]):
        cols = slice(r * width, (r + 1) * width)
        old = par_ref[:, cols]
        pseudo = old - all_ref[r]
        fresh = momentum_decay * mom_ref[:, cols] + pseudo
        new_mom[:, cols] = fresh
        new_par[:, cols] = old - outer_rate * (pseudo + momentum_decay * fresh)


def outer_step(global_params, momentum, stepped):
    return pl.pallas_call(
        outer_kernel,
        in_specs=whole_vmem(2 + len(stepped)),
        out_specs=whole_vmem(2),
        out_shape=[jax.ShapeDtypeStruct(global_params.shape, jnp.float32)] * 2,
        scratch_shapes=[
            pltpu.VMEM((global_params.shape[1] // stepped[0].shape[1],) + stepped[0].shape, jnp.float32)
        ],
        compiler_params=params(),
        name="outer_step",
    )(global_params, momentum, *stepped)


def on_device(
    sizes,
    block_input,
    ssd_input,
    out_grad,
    start_state,
    step_bias,
    decay_log,
    local_params,
    global_params,
    momentum,
):
    replicas, chips, cores = sizes
    local_rows = local_params[0]
    rows, depth = local_rows.shape
    own = rounded(local_rows)
    seq_width = ssd_input.shape[1]
    blocks = start_state.shape[0]
    block = block_input.shape[0] // blocks
    fast = (
        cores == 2
        and chips == 4
        and rows % 8 == 0
        and replicas & (replicas - 1) == 0
        and depth % (128 * replicas) == 0
    )

    def send(value, axis, k):
        count = dict(rep=replicas, line=chips, core=cores)[axis]
        return lax.ppermute(value, axis, [(i, i ^ k) for i in range(count)])

    def from_replicas(value, axis):
        parts, count = [value], 1
        while count < replicas:
            held = parts[0] if count == 1 else jnp.concatenate(parts, axis=axis)
            parts.append(send(held, "rep", count))
            count *= 2
        return parts

    def send_each(values, axis):
        values = [(k, v) for k, v in enumerate(values, 1)]
        return [sent for sent in reversed([send(v, axis, k) for k, v in reversed(values)])]

    if fast:
        far = send(own, "line", 3)
        near = send(own, "line", 1)
        order = (0, 2, 6, 1, 3, 7, 4, 5)
    else:
        late = [lax.all_gather(own, ("line", "core"), axis=0, tiled=True)]
        weights = []
        order = (0,)

    early = [[], []]
    states = [start_state[b].reshape(seq_width, STATE) for b in range(blocks)]
    states, own_late = lax.optimization_barrier((states, own))
    for b in range(blocks):
        seq = slice(b * block, (b + 1) * block)
        for half in range(2):
            early[half].append(
                early_products(out_grad[seq], ssd_input[seq], states[b], half, seq_width // 2)
            )
    if fast:
        pieces = column_pieces(block_input, own_late, replicas)
        far, _ = lax.optimization_barrier((far, pieces))
        pieces = [pieces[0]] + send_each(pieces[1:], "rep")
        far, near, early = lax.optimization_barrier((far, near, early))
        middle = send(far, "line", 1)
        middle, pieces[-1] = lax.optimization_barrier((middle, pieces[-1]))
        pair = send(jnp.concatenate([own, near], axis=0), "core", 1)
        weights = [own, near, far, pair, send(far, "core", 1)]
        middle, weights = lax.optimization_barrier((middle, weights))
        late = [middle, send(middle, "core", 1)]

    begun = []
    if fast:
        begun = [
            first_projection(block_input[b * block : (b + 1) * block], weights)
            for b in range(blocks)
        ]

    grads, mine, other = [], [], []
    for b in range(blocks):
        seq = slice(b * block, (b + 1) * block)
        parts = ssd_backward(
            block_input[seq],
            step_bias,
            decay_log,
            [early[0][b][0], early[1][b][0]],
            [early[0][b][1], early[1][b][1]],
            begun[b : b + 1],
            late,
            order,
        )
        for kept, part in zip((grads, mine, other), parts):
            kept.append(part)
    grad, mine, other = (
        kept[0] if blocks == 1 else jnp.concatenate(kept, axis=1) for kept in (grads, mine, other)
    )
    block_grad = block_gradient(grad, weights + late)

    if not fast:
        gradient = lax.psum_scatter(
            contract(grad, block_input, ((1,), (0,))),
            ("line", "core"),
            scatter_dimension=0,
            tiled=True,
        )
        pseudo = global_params - (local_rows - inner_rate * gradient)
        mean_pseudo = lax.psum(pseudo.astype(jnp.bfloat16), "rep").astype(jnp.float32) / replicas
        new_momentum = momentum_decay * momentum + mean_pseudo
        new_params = global_params - outer_rate * (mean_pseudo + momentum_decay * new_momentum)
        return (block_grad, new_params, new_momentum)

    tokens = blocks * block
    other = send(other, "core", 1)
    other, pieces = lax.optimization_barrier((other, pieces))
    both = jnp.concatenate([mine, other], axis=0)
    plane = from_replicas(both, 0)
    twin = send(jnp.concatenate([p[:tokens] for p in pieces], axis=0), "core", 1)
    sums = gradient_slice(plane, pieces, twin, chips)
    sums = [sums[0]] + send_each(sums[1:], "line")
    sums, block_grad = lax.optimization_barrier((sums, block_grad))
    stepped = stepped_slice(sums, pieces)
    stepped = from_replicas(stepped, 1)
    new_params, new_momentum = outer_step(global_params, momentum, stepped)
    return (block_grad, new_params, new_momentum)


def solution(mesh):
    replicas, shards = mesh.shape["rep"], mesh.shape["fsdp"]
    cores = 2 if shards % 2 == 0 else 1
    sizes = (replicas, shards // cores, cores)
    apart = jax.sharding.Mesh(mesh.devices.reshape(sizes), ("rep", "line", "core"))
    fsdp = ("line", "core")
    rows = P(("rep", "line", "core"), None)
    placed = (
        rows,
        rows,
        rows,
        P(("rep", "line", "core"), None, None),
        P(),
        P(),
        P("rep", fsdp, None),
        P(fsdp, None),
        P(fsdp, None),
    )
    return jax.shard_map(
        functools.partial(on_device, sizes),
        mesh=apart,
        in_specs=placed,
        out_specs=(rows, P(fsdp, None), P(fsdp, None)),
        check_vma=False,
    )
```

```python
import functools

import jax
import jax.numpy as jnp
from jax import lax
from jax.experimental import pallas as pl
from jax.experimental.pallas import tpu as pltpu
from jax.sharding import PartitionSpec as P

STATE = 64
LOG2E = 1.4426950408889634

inner_rate = 0.002
outer_rate = 0.7
momentum_decay = 0.9

VMEM_LIMIT = 20 * 1024 * 1024


def params(**more):
    return pltpu.CompilerParams(vmem_limit_bytes=VMEM_LIMIT, **more)


def whole_vmem(count):
    return [pl.BlockSpec(memory_space=pltpu.VMEM)] * count


def contract(left, right, dims):
    return lax.dot_general(left, right, (dims, ((), ())), preferred_element_type=jnp.float32)


def terms(value, count):
    out = []
    for _ in range(count):
        out.append(value.astype(jnp.bfloat16))
        value = value - out[-1].astype(jnp.float32)
    return out


def round_kernel(wide_ref, out_ref):
    out_ref[...] = wide_ref[...].astype(out_ref.dtype)


def rounded(wide):
    return pl.pallas_call(
        round_kernel,
        in_specs=whole_vmem(1),
        out_specs=pl.BlockSpec(memory_space=pltpu.VMEM),
        out_shape=jax.ShapeDtypeStruct(wide.shape, jnp.bfloat16),
        compiler_params=params(),
        name="rounded",
    )(wide)


def early_kernel(cot_ref, val_ref, state_ref, cross_ref, enter_ref):
    block = cot_ref.shape[0]
    lanes = lax.broadcasted_iota(jnp.int32, (block, 2 * STATE), 1)
    rows = lax.broadcasted_iota(jnp.int32, (block, block), 0)
    cols = lax.broadcasted_iota(jnp.int32, (block, block), 1)
    causal = rows >= cols
    low = lanes < STATE
    square = (2 * STATE, 2 * STATE)
    same_head = (lax.broadcasted_iota(jnp.int32, square, 0) < STATE) == (
        lax.broadcasted_iota(jnp.int32, square, 1) < STATE
    )
    for pair in range(cot_ref.shape[1] // (2 * STATE)):
        span = slice(pair * 2 * STATE, (pair + 1) * 2 * STATE)
        cot = cot_ref[:, span]
        val = val_ref[:, span]
        zero = jnp.zeros_like(cot)
        for odd in range(2):
            one = jnp.where(low, zero, cot) if odd else jnp.where(low, cot, zero)
            cross = contract(one, val, ((1,), (1,)))
            cross_ref[2 * pair + odd] = jnp.where(causal, cross, 0.0).astype(cross_ref.dtype)
        state = state_ref[span, :]
        wide = jnp.concatenate([state, state], axis=1)
        wide = jnp.where(same_head, wide, jnp.zeros_like(wide))
        enter_ref[:, span] = contract(cot, wide, ((1,), (0,)))


def early_products(out_grad, ssd_input, state, part, width):
    block = out_grad.shape[0]
    heads = width // STATE
    steps = 4
    piece = width // steps
    return pl.pallas_call(
        early_kernel,
        grid=(steps,),
        in_specs=[
            pl.BlockSpec((block, piece), lambda i: (0, part * steps + i)),
            pl.BlockSpec((block, piece), lambda i: (0, part * steps + i)),
            pl.BlockSpec((piece, STATE), lambda i: (part * steps + i, 0)),
        ],
        out_specs=[
            pl.BlockSpec((heads // steps, block, block), lambda i: (i, 0, 0)),
            pl.BlockSpec((block, piece), lambda i: (0, i)),
        ],
        out_shape=[
            jax.ShapeDtypeStruct((heads, block, block), jnp.bfloat16),
            jax.ShapeDtypeStruct((block, width), jnp.float32),
        ],
        compiler_params=params(),
        cost_estimate=pl.CostEstimate(flops=1, bytes_accessed=1, transcendentals=0),
        name="early_products",
    )(out_grad, ssd_input, state)


def stacked(refs):
    if len(refs) == 1:
        return refs[0][...]
    return jnp.concatenate([r[...].astype(jnp.float32) for r in refs], axis=0).astype(jnp.bfloat16)


def own_place(cores):
    return lax.axis_index("rep"), lax.axis_index("line") * cores + lax.axis_index("core")


def shard_rows(index, k, rows):
    return pl.ds(pl.multiple_of((index ^ k) * rows, 8), rows)


def first_kernel(rows_ref, *refs):
    refs[-1][...] = contract(stacked(refs[:-1]), rows_ref[...], ((1,), (1,)))


def first_projection(rows_in, weights):
    rows = sum(w.shape[0] for w in weights)
    return pl.pallas_call(
        first_kernel,
        in_specs=whole_vmem(1 + len(weights)),
        out_specs=pl.BlockSpec(memory_space=pltpu.VMEM),
        out_shape=jax.ShapeDtypeStruct((rows, rows_in.shape[0]), jnp.float32),
        compiler_params=params(),
        cost_estimate=pl.CostEstimate(flops=1, bytes_accessed=1, transcendentals=0),
        name="first_projection",
    )(rows_in, *weights)


def ssd_kernel(order, first, rows_ref, bias_ref, decay_ref, *rest):
    shards = len(order)
    cross_refs, enter_refs, rest = rest[:2], rest[2:4], rest[4:]
    _, spot = own_place(2) if shards > 1 else (0, 0)
    first_ref, rest = (rest[0], rest[1:]) if first else (None, rest)
    weight_refs, rest = rest[: shards - first], rest[shards - first :]
    grad_ref, mine_ref, other_ref, proj_ref, col_ref, out_ref = rest
    block = rows_ref.shape[0]
    heads = bias_ref.shape[1]
    per = weight_refs[0].shape[0]
    arrived = contract(stacked(weight_refs), rows_ref[...], ((1,), (1,)))
    if shards == 1:
        proj_ref[...] = arrived
    else:
        for at, k in enumerate(order):
            source, line = (first_ref, at) if at < first else (arrived, at - first)
            proj_ref[shard_rows(spot, k, per), :] = source[line * per : (line + 1) * per]
    key_t = proj_ref[:STATE, :]
    query_t = proj_ref[STATE : 2 * STATE, :]
    bias_t = jnp.broadcast_to(bias_ref[...], (block, heads)).T
    rate = jnp.exp(jnp.broadcast_to(decay_ref[...], (block, heads)).T)
    raw = proj_ref[2 * STATE :, :] + bias_t
    step_t = jnp.maximum(raw, 0.0) + jnp.log1p(jnp.exp(-jnp.abs(raw)))
    up = lax.broadcasted_iota(jnp.int32, (block, block), 0)
    across = lax.broadcasted_iota(jnp.int32, (block, block), 1)
    before = jnp.where(up <= across, 1.0, 0.0).astype(jnp.bfloat16)
    after = jnp.where(up >= across, 1.0, 0.0).astype(jnp.bfloat16)
    cum_t = LOG2E * contract(
        jnp.concatenate(terms(-step_t * rate, 3), axis=1),
        jnp.concatenate([before] * 3, axis=0),
        ((1,), (0,)),
    )
    cum = cum_t.T
    query = query_t.T
    query_high, query_low = terms(query, 2)
    key_high, key_low = terms(key_t, 2)
    scores = contract(
        jnp.concatenate([query_high, query_high, query_low], axis=1),
        jnp.concatenate([key_high, key_low, key_high], axis=0),
        ((1,), (0,)),
    )
    entered = jnp.exp2(cum)
    query_twice = jnp.concatenate([query, query], axis=1)
    low = lax.broadcasted_iota(jnp.int32, (block, 2 * STATE), 1) < STATE
    head_of = lax.broadcasted_iota(jnp.int32, (block, heads), 1)

    wide = (2 * block + 2 * STATE, heads)
    place = lax.broadcasted_iota(jnp.int32, wide, 0)
    parity = jnp.where(place < 2 * block, place // block, (place - 2 * block) // STATE)
    chooser = jnp.where(lax.broadcasted_iota(jnp.int32, wide, 1) % 2 == parity, 1.0, 0.0)
    chooser = chooser.astype(jnp.bfloat16)

    score_grad = jnp.zeros((block, block), jnp.float32)
    query_grad = jnp.zeros((block, 2 * STATE), jnp.float32)
    row_sums = jnp.zeros((block, heads), jnp.float32)
    for pair in range(heads // 2):
        left = []
        for h in (2 * pair, 2 * pair + 1):
            span = cum[:, h : h + 1] - cum_t[h : h + 1, :]
            cross = cross_refs[2 * h // heads][h % (heads // 2)]
            weight = cross.astype(jnp.float32) * jnp.exp2(jnp.minimum(span, 0.0))
            stepped = weight * step_t[h : h + 1, :]
            score_grad = score_grad + stepped
            col_ref[h : h + 1, :] = jnp.sum(weight * scores, axis=0, keepdims=True)
            left.append((stepped * scores).astype(jnp.bfloat16))
        h = 2 * pair
        gain = jnp.where(low, entered[:, h : h + 1], entered[:, h + 1 : h + 2])
        at = h % (heads // 2) * STATE
        part = enter_refs[2 * h // heads][:, at : at + 2 * STATE] * gain
        query_grad = query_grad + part
        left.append((part * query_twice).astype(jnp.bfloat16))
        sums = contract(jnp.concatenate(left, axis=1), chooser, ((1,), (0,)))
        row_sums = jnp.where(head_of // 2 == pair, sums, row_sums)

    cols_t = col_ref[...]
    cum_grad = row_sums.T - step_t * cols_t
    later = contract(
        jnp.concatenate(terms(cum_grad, 2), axis=1),
        jnp.concatenate([after] * 2, axis=0),
        ((1,), (0,)),
    )
    step_grad = cols_t - rate * later
    raw_grad = step_grad / (1.0 + jnp.exp(-raw))
    score_grad = score_grad.astype(jnp.bfloat16)
    out_ref[:STATE, :] = contract(query_t.astype(jnp.bfloat16), score_grad, ((1,), (0,)))
    query_all = (query_grad[:, :STATE] + query_grad[:, STATE:]).T
    out_ref[STATE : 2 * STATE, :] = query_all + contract(key_high, score_grad, ((1,), (1,)))
    out_ref[2 * STATE :, :] = raw_grad
    if shards == 1:
        grad_ref[...] = out_ref[...].astype(jnp.bfloat16)
        mine_ref[...] = jnp.zeros_like(mine_ref)
        other_ref[...] = jnp.zeros_like(other_ref)
        return
    core = spot % 2
    for part, ref in ((core, mine_ref), (1 - core, other_ref)):
        of_core = [out_ref[shard_rows(f + part, 0, per), :] for f in range(0, shards, 2)]
        ref[...] = jnp.concatenate(of_core, axis=0).astype(jnp.bfloat16)
    for at, k in enumerate(order):
        proj_ref[at * per : (at + 1) * per, :] = out_ref[shard_rows(spot, k, per), :]
    grad_ref[...] = proj_ref[...].astype(jnp.bfloat16)


def ssd_backward(rows_in, step_bias, decay_log, cross, enter, first, weights, order):
    block = rows_in.shape[0]
    heads = step_bias.shape[0]
    cols = len(order) * weights[0].shape[0]
    half = (cols // 2, block)
    return pl.pallas_call(
        functools.partial(ssd_kernel, order, len(order) - len(weights)),
        in_specs=whole_vmem(7 + len(first) + len(weights)),
        out_specs=whole_vmem(3),
        out_shape=[
            jax.ShapeDtypeStruct((cols, block), jnp.bfloat16),
            jax.ShapeDtypeStruct(half, jnp.bfloat16),
            jax.ShapeDtypeStruct(half, jnp.bfloat16),
        ],
        scratch_shapes=[
            pltpu.VMEM((cols, block), jnp.float32),
            pltpu.VMEM((heads, block), jnp.float32),
            pltpu.VMEM((cols, block), jnp.float32),
        ],
        compiler_params=params(),
        cost_estimate=pl.CostEstimate(flops=1, bytes_accessed=1, transcendentals=0),
        name="ssd_backward",
    )(rows_in, step_bias.reshape(1, -1), decay_log.reshape(1, -1), *cross, *enter, *first, *weights)


def block_grad_kernel(grad_ref, *refs):
    out_ref = refs[-1]
    weights = stacked(refs[:-1])
    out_ref[...] = contract(grad_ref[...].T, weights, ((1,), (0,))).astype(out_ref.dtype)


def block_gradient(grad, weights):
    depth = weights[0].shape[1]
    cols, block = grad.shape
    return pl.pallas_call(
        block_grad_kernel,
        in_specs=whole_vmem(1 + len(weights)),
        out_specs=pl.BlockSpec(memory_space=pltpu.VMEM),
        out_shape=jax.ShapeDtypeStruct((block, depth), jnp.bfloat16),
        compiler_params=params(),
        cost_estimate=pl.CostEstimate(
            flops=2 * block * cols * depth, bytes_accessed=4 * cols * depth, transcendentals=0
        ),
        name="block_gradient",
    )(grad, *weights)


def pieces_kernel(rows_ref, own_ref, *outs):
    block = rows_ref.shape[0]
    rep, _ = own_place(2)
    width = outs[0].shape[1]
    for k, out in enumerate(outs):
        cols = pl.ds(pl.multiple_of((rep ^ k) * width, 128), width)
        out[:block, :] = rows_ref[:, cols]
        out[block:, :] = own_ref[:, cols]


def column_pieces(rows_in, own, replicas):
    tokens, depth = rows_in.shape
    shape = (tokens + own.shape[0], depth // replicas)
    return pl.pallas_call(
        pieces_kernel,
        in_specs=whole_vmem(2),
        out_specs=whole_vmem(replicas),
        out_shape=[jax.ShapeDtypeStruct(shape, jnp.bfloat16)] * replicas,
        compiler_params=params(),
        name="column_pieces",
    )(rows_in, own)


def slice_kernel(replicas, *refs):
    grads, pieces, refs = refs[:replicas], refs[replicas : 2 * replicas], refs[2 * replicas :]
    twin, outs, total = refs[0], refs[1:-1], refs[-1]
    tokens = twin.shape[0] // replicas
    rows = total.shape[0]
    left, right = [], []
    for other in range(2):
        for k in range(replicas):
            left.append(grads[k][other * rows : (other + 1) * rows, :])
            right.append(
                twin[k * tokens : (k + 1) * tokens, :] if other else pieces[k][:tokens, :]
            )
    total[...] = contract(
        jnp.concatenate(left, axis=1), jnp.concatenate(right, axis=0), ((1,), (0,))
    )
    per = outs[0].shape[0]
    chip = lax.axis_index("line")
    for k, out in enumerate(outs):
        out[...] = total[shard_rows(chip, k, per), :].astype(jnp.bfloat16)


def gradient_slice(grads, pieces, twin, chips):
    rows = grads[0].shape[0] // (2 * chips)
    width = twin.shape[1]
    return pl.pallas_call(
        functools.partial(slice_kernel, len(pieces)),
        in_specs=whole_vmem(1 + 2 * len(pieces)),
        out_specs=whole_vmem(chips),
        out_shape=[jax.ShapeDtypeStruct((rows, width), jnp.bfloat16)] * chips,
        scratch_shapes=[pltpu.VMEM((rows * chips, width), jnp.float32)],
        compiler_params=params(),
        name="gradient_slice",
    )(*grads, *pieces, twin)


def stepped_kernel(chips, *refs):
    sums, pieces, out_ref = refs[:chips], refs[chips:-1], refs[-1]
    rows = out_ref.shape[0]
    total = sums[0][...].astype(jnp.float32)
    for part in sums[1:]:
        total = total + part[...].astype(jnp.float32)
    level = pieces[0][-rows:, :].astype(jnp.float32)
    for piece in pieces[1:]:
        level = level + piece[-rows:, :].astype(jnp.float32)
    mean = (level - inner_rate * total) * (1.0 / len(pieces))
    out_ref[...] = mean.astype(jnp.bfloat16)


def stepped_slice(sums, pieces):
    return pl.pallas_call(
        functools.partial(stepped_kernel, len(sums)),
        in_specs=whole_vmem(len(sums) + len(pieces)),
        out_specs=pl.BlockSpec(memory_space=pltpu.VMEM),
        out_shape=jax.ShapeDtypeStruct(sums[0].shape, jnp.bfloat16),
        compiler_params=params(),
        name="stepped_slice",
    )(*sums, *pieces)


def outer_kernel(par_ref, mom_ref, *refs):
    stepped, (new_par, new_mom, all_ref) = refs[:-3], refs[-3:]
    width = stepped[0].shape[1]
    for k, part in enumerate(stepped):
        all_ref[lax.axis_index("rep") ^ k] = part[...].astype(jnp.float32)
    for r in range(len(stepped)):
        cols = slice(r * width, (r + 1) * width)
        old = par_ref[:, cols]
        pseudo = old - all_ref[r]
        fresh = momentum_decay * mom_ref[:, cols] + pseudo
        new_mom[:, cols] = fresh
        new_par[:, cols] = old - outer_rate * (pseudo + momentum_decay * fresh)


def outer_step(global_params, momentum, stepped):
    return pl.pallas_call(
        outer_kernel,
        in_specs=whole_vmem(2 + len(stepped)),
        out_specs=whole_vmem(2),
        out_shape=[jax.ShapeDtypeStruct(global_params.shape, jnp.float32)] * 2,
        scratch_shapes=[pltpu.VMEM((len(stepped),) + stepped[0].shape, jnp.float32)],
        compiler_params=params(),
        name="outer_step",
    )(global_params, momentum, *stepped)


def on_device(
    sizes,
    block_input,
    ssd_input,
    out_grad,
    start_state,
    step_bias,
    decay_log,
    local_params,
    global_params,
    momentum,
):
    replicas, chips, cores = sizes
    local_rows = local_params[0]
    rows, depth = local_rows.shape
    own = rounded(local_rows)
    seq_width = ssd_input.shape[1]
    blocks = start_state.shape[0]
    block = block_input.shape[0] // blocks
    fast = (
        cores == 2
        and chips == 4
        and rows % 8 == 0
        and replicas & (replicas - 1) == 0
        and depth % (128 * replicas) == 0
    )

    def send(value, axis, k):
        count = dict(rep=replicas, line=chips, core=cores)[axis]
        return lax.ppermute(value, axis, [(i, i ^ k) for i in range(count)])

    def send_each(values, axis):
        values = [(k, v) for k, v in enumerate(values, 1)]
        return [sent for sent in reversed([send(v, axis, k) for k, v in reversed(values)])]

    if fast:
        far = send(own, "line", 3)
        near = send(own, "line", 1)
        order = (0, 2, 6, 1, 7, 3, 4, 5)
    else:
        late = [lax.all_gather(own, ("line", "core"), axis=0, tiled=True)]
        weights = []
        order = (0,)

    early = [[], []]
    states = [start_state[b].reshape(seq_width, STATE) for b in range(blocks)]
    states, own_late = lax.optimization_barrier((states, own))
    for b in range(blocks):
        seq = slice(b * block, (b + 1) * block)
        for half in range(2):
            early[half].append(
                early_products(out_grad[seq], ssd_input[seq], states[b], half, seq_width // 2)
            )
    if fast:
        pieces = column_pieces(block_input, own_late, replicas)
        far, _ = lax.optimization_barrier((far, pieces))
        pieces = [pieces[0]] + send_each(pieces[1:], "rep")
        far, early = lax.optimization_barrier((far, early))
        middle = send(far, "line", 1)
        middle, pieces[-1] = lax.optimization_barrier((middle, pieces[-1]))
        pair = send(jnp.concatenate([own, far], axis=0), "core", 1)
        weights = [own, near, far, pair, send(near, "core", 1)]
        middle, weights = lax.optimization_barrier((middle, weights))
        late = [middle, send(middle, "core", 1)]

    begun = []
    if fast:
        begun = [
            first_projection(block_input[b * block : (b + 1) * block], weights)
            for b in range(blocks)
        ]

    grads, mine, other = [], [], []
    for b in range(blocks):
        seq = slice(b * block, (b + 1) * block)
        parts = ssd_backward(
            block_input[seq],
            step_bias,
            decay_log,
            [early[0][b][0], early[1][b][0]],
            [early[0][b][1], early[1][b][1]],
            begun[b : b + 1],
            late,
            order,
        )
        for kept, part in zip((grads, mine, other), parts):
            kept.append(part)
    grad, mine, other = (
        kept[0] if blocks == 1 else jnp.concatenate(kept, axis=1) for kept in (grads, mine, other)
    )
    block_grad = block_gradient(grad, weights + late)

    if not fast:
        gradient = lax.psum_scatter(
            contract(grad, block_input, ((1,), (0,))),
            ("line", "core"),
            scatter_dimension=0,
            tiled=True,
        )
        pseudo = global_params - (local_rows - inner_rate * gradient)
        mean_pseudo = lax.psum(pseudo.astype(jnp.bfloat16), "rep").astype(jnp.float32) / replicas
        new_momentum = momentum_decay * momentum + mean_pseudo
        new_params = global_params - outer_rate * (mean_pseudo + momentum_decay * new_momentum)
        return (block_grad, new_params, new_momentum)

    tokens = blocks * block
    other = send(other, "core", 1)
    other, pieces = lax.optimization_barrier((other, pieces))
    both = jnp.concatenate([mine, other], axis=0)
    plane = [both] + send_each([both] * (replicas - 1), "rep")
    twin = send(jnp.concatenate([p[:tokens] for p in pieces], axis=0), "core", 1)
    sums = gradient_slice(plane, pieces, twin, chips)
    sums = [sums[0]] + send_each(sums[1:], "line")
    sums, block_grad = lax.optimization_barrier((sums, block_grad))
    stepped = stepped_slice(sums, pieces)
    stepped = [stepped] + send_each([stepped] * (replicas - 1), "rep")
    new_params, new_momentum = outer_step(global_params, momentum, stepped)
    return (block_grad, new_params, new_momentum)


def solution(mesh):
    replicas, shards = mesh.shape["rep"], mesh.shape["fsdp"]
    cores = 2 if shards % 2 == 0 else 1
    sizes = (replicas, shards // cores, cores)
    apart = jax.sharding.Mesh(mesh.devices.reshape(sizes), ("rep", "line", "core"))
    fsdp = ("line", "core")
    rows = P(("rep", "line", "core"), None)
    placed = (
        rows,
        rows,
        rows,
        P(("rep", "line", "core"), None, None),
        P(),
        P(),
        P("rep", fsdp, None),
        P(fsdp, None),
        P(fsdp, None),
    )
    return jax.shard_map(
        functools.partial(on_device, sizes),
        mesh=apart,
        in_specs=placed,
        out_specs=(rows, P(fsdp, None), P(fsdp, None)),
        check_vma=False,
    )
```

```python
import functools

import jax
import jax.numpy as jnp
from jax import lax
from jax.experimental import pallas as pl
from jax.experimental.pallas import tpu as pltpu
from jax.sharding import PartitionSpec as P

STATE = 64
LOG2E = 1.4426950408889634

inner_rate = 0.002
outer_rate = 0.7
momentum_decay = 0.9

VMEM_LIMIT = 20 * 1024 * 1024


def params(**more):
    return pltpu.CompilerParams(vmem_limit_bytes=VMEM_LIMIT, **more)


def whole_vmem(count):
    return [pl.BlockSpec(memory_space=pltpu.VMEM)] * count


def contract(left, right, dims):
    return lax.dot_general(left, right, (dims, ((), ())), preferred_element_type=jnp.float32)


def terms(value, count):
    out = []
    for _ in range(count):
        out.append(value.astype(jnp.bfloat16))
        value = value - out[-1].astype(jnp.float32)
    return out


def round_kernel(wide_ref, out_ref, held_ref, sems):
    width = wide_ref.shape[1] // sems.shape[0]
    copies = []
    for i in range(sems.shape[0]):
        cols = pl.ds(i * width, width)
        copy = pltpu.make_async_copy(wide_ref.at[:, cols], held_ref.at[:, cols], sems.at[i])
        copy.start()
        copies.append((cols, copy))
    for cols, copy in copies:
        copy.wait()
        out_ref[:, cols] = held_ref[:, cols].astype(out_ref.dtype)


def rounded(wide):
    return pl.pallas_call(
        round_kernel,
        in_specs=[pl.BlockSpec(memory_space=pltpu.HBM)],
        out_specs=pl.BlockSpec(memory_space=pltpu.VMEM),
        out_shape=jax.ShapeDtypeStruct(wide.shape, jnp.bfloat16),
        scratch_shapes=[pltpu.VMEM(wide.shape, wide.dtype), pltpu.SemaphoreType.DMA((8,))],
        compiler_params=params(),
        name="rounded",
    )(wide)


def early_kernel(cot_ref, val_ref, state_ref, cross_ref, enter_ref):
    block = cot_ref.shape[0]
    lanes = lax.broadcasted_iota(jnp.int32, (block, 2 * STATE), 1)
    rows = lax.broadcasted_iota(jnp.int32, (block, block), 0)
    cols = lax.broadcasted_iota(jnp.int32, (block, block), 1)
    causal = rows >= cols
    low = lanes < STATE
    square = (2 * STATE, 2 * STATE)
    same_head = (lax.broadcasted_iota(jnp.int32, square, 0) < STATE) == (
        lax.broadcasted_iota(jnp.int32, square, 1) < STATE
    )
    for pair in range(cot_ref.shape[1] // (2 * STATE)):
        span = slice(pair * 2 * STATE, (pair + 1) * 2 * STATE)
        cot = cot_ref[:, span]
        val = val_ref[:, span]
        zero = jnp.zeros_like(cot)
        for odd in range(2):
            one = jnp.where(low, zero, cot) if odd else jnp.where(low, cot, zero)
            cross = contract(one, val, ((1,), (1,)))
            cross_ref[2 * pair + odd] = jnp.where(causal, cross, 0.0).astype(cross_ref.dtype)
        state = state_ref[span, :]
        wide = jnp.concatenate([state, state], axis=1)
        wide = jnp.where(same_head, wide, jnp.zeros_like(wide))
        enter_ref[:, span] = contract(cot, wide, ((1,), (0,)))


def early_products(out_grad, ssd_input, state, part, width):
    block = out_grad.shape[0]
    heads = width // STATE
    steps = 4
    piece = width // steps
    return pl.pallas_call(
        early_kernel,
        grid=(steps,),
        in_specs=[
            pl.BlockSpec((block, piece), lambda i: (0, part * steps + i)),
            pl.BlockSpec((block, piece), lambda i: (0, part * steps + i)),
            pl.BlockSpec((piece, STATE), lambda i: (part * steps + i, 0)),
        ],
        out_specs=[
            pl.BlockSpec((heads // steps, block, block), lambda i: (i, 0, 0)),
            pl.BlockSpec((block, piece), lambda i: (0, i)),
        ],
        out_shape=[
            jax.ShapeDtypeStruct((heads, block, block), jnp.bfloat16),
            jax.ShapeDtypeStruct((block, width), jnp.float32),
        ],
        compiler_params=params(),
        cost_estimate=pl.CostEstimate(flops=1, bytes_accessed=1, transcendentals=0),
        name="early_products",
    )(out_grad, ssd_input, state)


def stacked(refs):
    if len(refs) == 1:
        return refs[0][...]
    return jnp.concatenate([r[...].astype(jnp.float32) for r in refs], axis=0).astype(jnp.bfloat16)


def own_place(cores):
    return lax.axis_index("rep"), lax.axis_index("line") * cores + lax.axis_index("core")


def shard_rows(index, k, rows):
    return pl.ds(pl.multiple_of((index ^ k) * rows, 8), rows)


def first_kernel(rows_ref, *refs):
    refs[-1][...] = contract(stacked(refs[:-1]), rows_ref[...], ((1,), (1,)))


def first_projection(rows_in, weights):
    rows = sum(w.shape[0] for w in weights)
    return pl.pallas_call(
        first_kernel,
        in_specs=whole_vmem(1 + len(weights)),
        out_specs=pl.BlockSpec(memory_space=pltpu.VMEM),
        out_shape=jax.ShapeDtypeStruct((rows, rows_in.shape[0]), jnp.float32),
        compiler_params=params(),
        cost_estimate=pl.CostEstimate(flops=1, bytes_accessed=1, transcendentals=0),
        name="first_projection",
    )(rows_in, *weights)


def ssd_kernel(order, first, rows_ref, bias_ref, decay_ref, *rest):
    shards = len(order)
    cross_refs, enter_refs, rest = rest[:2], rest[2:4], rest[4:]
    _, spot = own_place(2) if shards > 1 else (0, 0)
    first_ref, rest = (rest[0], rest[1:]) if first else (None, rest)
    weight_refs, rest = rest[: shards - first], rest[shards - first :]
    grad_ref, mine_ref, other_ref, proj_ref, col_ref, out_ref = rest
    block = rows_ref.shape[0]
    heads = bias_ref.shape[1]
    per = weight_refs[0].shape[0]
    arrived = contract(stacked(weight_refs), rows_ref[...], ((1,), (1,)))
    if shards == 1:
        proj_ref[...] = arrived
    else:
        for at, k in enumerate(order):
            source, line = (first_ref, at) if at < first else (arrived, at - first)
            proj_ref[shard_rows(spot, k, per), :] = source[line * per : (line + 1) * per]
    key_t = proj_ref[:STATE, :]
    query_t = proj_ref[STATE : 2 * STATE, :]
    bias_t = jnp.broadcast_to(bias_ref[...], (block, heads)).T
    rate = jnp.exp(jnp.broadcast_to(decay_ref[...], (block, heads)).T)
    raw = proj_ref[2 * STATE :, :] + bias_t
    step_t = jnp.maximum(raw, 0.0) + jnp.log1p(jnp.exp(-jnp.abs(raw)))
    up = lax.broadcasted_iota(jnp.int32, (block, block), 0)
    across = lax.broadcasted_iota(jnp.int32, (block, block), 1)
    before = jnp.where(up <= across, 1.0, 0.0).astype(jnp.bfloat16)
    after = jnp.where(up >= across, 1.0, 0.0).astype(jnp.bfloat16)
    cum_t = LOG2E * contract(
        jnp.concatenate(terms(-step_t * rate, 3), axis=1),
        jnp.concatenate([before] * 3, axis=0),
        ((1,), (0,)),
    )
    cum = cum_t.T
    step = step_t.T
    query = query_t.T
    query_high, query_low = terms(query, 2)
    key_high, key_low = terms(key_t, 2)
    scores = contract(
        jnp.concatenate([query_high, query_high, query_low], axis=1),
        jnp.concatenate([key_high, key_low, key_high], axis=0),
        ((1,), (0,)),
    )
    entered = jnp.exp2(cum)
    query_twice = jnp.concatenate([query, query], axis=1)
    low = lax.broadcasted_iota(jnp.int32, (block, 2 * STATE), 1) < STATE
    head_of = lax.broadcasted_iota(jnp.int32, (block, heads), 1)
    below = lax.broadcasted_iota(jnp.int32, (block, heads), 0) < STATE

    score_grad = jnp.zeros((block, block), jnp.float32)
    query_grad = jnp.zeros((block, 2 * STATE), jnp.float32)
    row_sums = jnp.zeros((block, heads), jnp.float32)
    for h0 in range(0, heads, 4):
        left, right = [], []
        for h in range(h0, h0 + 4):
            span = cum[:, h : h + 1] - cum_t[h : h + 1, :]
            cross = cross_refs[2 * h // heads][h % (heads // 2)]
            weight = cross.astype(jnp.float32) * jnp.exp2(jnp.minimum(span, 0.0))
            score_grad = score_grad + weight * step_t[h : h + 1, :]
            mixed = weight * scores
            col_ref[h : h + 1, :] = jnp.sum(mixed, axis=0, keepdims=True)
            left.append(mixed.astype(jnp.bfloat16))
            right.append(jnp.where(head_of == h, step, 0.0).astype(jnp.bfloat16))
        for h in range(h0, h0 + 4, 2):
            gain = jnp.where(low, entered[:, h : h + 1], entered[:, h + 1 : h + 2])
            at = h % (heads // 2) * STATE
            part = enter_refs[2 * h // heads][:, at : at + 2 * STATE] * gain
            query_grad = query_grad + part
            left.append((part * query_twice).astype(jnp.bfloat16))
            right.append(
                jnp.where(head_of == jnp.where(below, h, h + 1), 1.0, 0.0).astype(jnp.bfloat16)
            )
        row_sums = row_sums + contract(
            jnp.concatenate(left, axis=1), jnp.concatenate(right, axis=0), ((1,), (0,))
        )

    cols_t = col_ref[...]
    cum_grad = row_sums.T - step_t * cols_t
    later = contract(
        jnp.concatenate(terms(cum_grad, 2), axis=1),
        jnp.concatenate([after] * 2, axis=0),
        ((1,), (0,)),
    )
    step_grad = cols_t - rate * later
    raw_grad = step_grad / (1.0 + jnp.exp(-raw))
    score_grad = score_grad.astype(jnp.bfloat16)
    out_ref[:STATE, :] = contract(query_t.astype(jnp.bfloat16), score_grad, ((1,), (0,)))
    query_all = (query_grad[:, :STATE] + query_grad[:, STATE:]).T
    out_ref[STATE : 2 * STATE, :] = query_all + contract(key_high, score_grad, ((1,), (1,)))
    out_ref[2 * STATE :, :] = raw_grad
    if shards == 1:
        grad_ref[...] = out_ref[...].astype(jnp.bfloat16)
        mine_ref[...] = jnp.zeros_like(mine_ref)
        other_ref[...] = jnp.zeros_like(other_ref)
        return
    core = spot % 2
    for part, ref in ((core, mine_ref), (1 - core, other_ref)):
        of_core = [out_ref[shard_rows(f + part, 0, per), :] for f in range(0, shards, 2)]
        ref[...] = jnp.concatenate(of_core, axis=0).astype(jnp.bfloat16)
    for at, k in enumerate(order):
        proj_ref[at * per : (at + 1) * per, :] = out_ref[shard_rows(spot, k, per), :]
    grad_ref[...] = proj_ref[...].astype(jnp.bfloat16)


def ssd_backward(rows_in, step_bias, decay_log, cross, enter, first, weights, order):
    block = rows_in.shape[0]
    heads = step_bias.shape[0]
    cols = len(order) * weights[0].shape[0]
    half = (cols // 2, block)
    return pl.pallas_call(
        functools.partial(ssd_kernel, order, len(order) - len(weights)),
        in_specs=whole_vmem(7 + len(first) + len(weights)),
        out_specs=whole_vmem(3),
        out_shape=[
            jax.ShapeDtypeStruct((cols, block), jnp.bfloat16),
            jax.ShapeDtypeStruct(half, jnp.bfloat16),
            jax.ShapeDtypeStruct(half, jnp.bfloat16),
        ],
        scratch_shapes=[
            pltpu.VMEM((cols, block), jnp.float32),
            pltpu.VMEM((heads, block), jnp.float32),
            pltpu.VMEM((cols, block), jnp.float32),
        ],
        compiler_params=params(),
        cost_estimate=pl.CostEstimate(flops=1, bytes_accessed=1, transcendentals=0),
        name="ssd_backward",
    )(rows_in, step_bias.reshape(1, -1), decay_log.reshape(1, -1), *cross, *enter, *first, *weights)


def block_grad_kernel(grad_ref, *refs):
    out_ref = refs[-1]
    weights = stacked(refs[:-1])
    out_ref[...] = contract(grad_ref[...].T, weights, ((1,), (0,))).astype(out_ref.dtype)


def block_gradient(grad, weights):
    depth = weights[0].shape[1]
    cols, block = grad.shape
    return pl.pallas_call(
        block_grad_kernel,
        in_specs=whole_vmem(1 + len(weights)),
        out_specs=pl.BlockSpec(memory_space=pltpu.VMEM),
        out_shape=jax.ShapeDtypeStruct((block, depth), jnp.bfloat16),
        compiler_params=params(),
        cost_estimate=pl.CostEstimate(
            flops=2 * block * cols * depth, bytes_accessed=4 * cols * depth, transcendentals=0
        ),
        name="block_gradient",
    )(grad, *weights)


def pieces_kernel(rows_ref, own_ref, *outs):
    block = rows_ref.shape[0]
    rep, _ = own_place(2)
    width = outs[0].shape[1]
    for k, out in enumerate(outs):
        cols = pl.ds(pl.multiple_of((rep ^ k) * width, 128), width)
        out[:block, :] = rows_ref[:, cols]
        out[block:, :] = own_ref[:, cols]


def column_pieces(rows_in, own, replicas):
    tokens, depth = rows_in.shape
    shape = (tokens + own.shape[0], depth // replicas)
    return pl.pallas_call(
        pieces_kernel,
        in_specs=whole_vmem(2),
        out_specs=whole_vmem(replicas),
        out_shape=[jax.ShapeDtypeStruct(shape, jnp.bfloat16)] * replicas,
        compiler_params=params(),
        name="column_pieces",
    )(rows_in, own)


def slice_kernel(replicas, *refs):
    grads, pieces, refs = refs[:replicas], refs[replicas : 2 * replicas], refs[2 * replicas :]
    twin, outs, total = refs[0], refs[1:-1], refs[-1]
    tokens = twin.shape[0] // replicas
    rows = total.shape[0]
    left, right = [], []
    for other in range(2):
        for k in range(replicas):
            left.append(grads[k][other * rows : (other + 1) * rows, :])
            right.append(
                twin[k * tokens : (k + 1) * tokens, :] if other else pieces[k][:tokens, :]
            )
    total[...] = contract(
        jnp.concatenate(left, axis=1), jnp.concatenate(right, axis=0), ((1,), (0,))
    )
    per = outs[0].shape[0]
    chip = lax.axis_index("line")
    for k, out in enumerate(outs):
        out[...] = total[shard_rows(chip, k, per), :].astype(jnp.bfloat16)


def gradient_slice(grads, pieces, twin, chips):
    rows = grads[0].shape[0] // (2 * chips)
    width = twin.shape[1]
    return pl.pallas_call(
        functools.partial(slice_kernel, len(pieces)),
        in_specs=whole_vmem(1 + 2 * len(pieces)),
        out_specs=whole_vmem(chips),
        out_shape=[jax.ShapeDtypeStruct((rows, width), jnp.bfloat16)] * chips,
        scratch_shapes=[pltpu.VMEM((rows * chips, width), jnp.float32)],
        compiler_params=params(),
        name="gradient_slice",
    )(*grads, *pieces, twin)


def stepped_kernel(chips, *refs):
    sums, pieces, out_ref = refs[:chips], refs[chips:-1], refs[-1]
    rows = out_ref.shape[0]
    total = sums[0][...].astype(jnp.float32)
    for part in sums[1:]:
        total = total + part[...].astype(jnp.float32)
    level = pieces[0][-rows:, :].astype(jnp.float32)
    for piece in pieces[1:]:
        level = level + piece[-rows:, :].astype(jnp.float32)
    mean = (level - inner_rate * total) * (1.0 / len(pieces))
    out_ref[...] = mean.astype(jnp.bfloat16)


def stepped_slice(sums, pieces):
    return pl.pallas_call(
        functools.partial(stepped_kernel, len(sums)),
        in_specs=whole_vmem(len(sums) + len(pieces)),
        out_specs=pl.BlockSpec(memory_space=pltpu.VMEM),
        out_shape=jax.ShapeDtypeStruct(sums[0].shape, jnp.bfloat16),
        compiler_params=params(),
        name="stepped_slice",
    )(*sums, *pieces)


def outer_kernel(par_ref, mom_ref, *refs):
    stepped, (new_par, new_mom, all_ref) = refs[:-3], refs[-3:]
    width = stepped[0].shape[1]
    for k, part in enumerate(stepped):
        all_ref[lax.axis_index("rep") ^ k] = part[...].astype(jnp.float32)
    for r in range(len(stepped)):
        cols = slice(r * width, (r + 1) * width)
        old = par_ref[:, cols]
        pseudo = old - all_ref[r]
        fresh = momentum_decay * mom_ref[:, cols] + pseudo
        new_mom[:, cols] = fresh
        new_par[:, cols] = old - outer_rate * (pseudo + momentum_decay * fresh)


def outer_step(global_params, momentum, stepped):
    return pl.pallas_call(
        outer_kernel,
        in_specs=whole_vmem(2 + len(stepped)),
        out_specs=whole_vmem(2),
        out_shape=[jax.ShapeDtypeStruct(global_params.shape, jnp.float32)] * 2,
        scratch_shapes=[pltpu.VMEM((len(stepped),) + stepped[0].shape, jnp.float32)],
        compiler_params=params(),
        name="outer_step",
    )(global_params, momentum, *stepped)


def on_device(
    sizes,
    block_input,
    ssd_input,
    out_grad,
    start_state,
    step_bias,
    decay_log,
    local_params,
    global_params,
    momentum,
):
    replicas, chips, cores = sizes
    local_rows = local_params[0]
    rows, depth = local_rows.shape
    own = rounded(local_rows)
    seq_width = ssd_input.shape[1]
    blocks = start_state.shape[0]
    block = block_input.shape[0] // blocks
    fast = (
        cores == 2
        and chips == 4
        and rows % 8 == 0
        and replicas & (replicas - 1) == 0
        and depth % (128 * replicas) == 0
    )

    def send(value, axis, k):
        count = dict(rep=replicas, line=chips, core=cores)[axis]
        return lax.ppermute(value, axis, [(i, i ^ k) for i in range(count)])

    def send_each(values, axis):
        values = [(k, v) for k, v in enumerate(values, 1)]
        return [sent for sent in reversed([send(v, axis, k) for k, v in reversed(values)])]

    if fast:
        far = send(own, "line", 3)
        near = send(own, "line", 1)
        order = (0, 2, 6, 1, 7, 3, 4, 5)
    else:
        late = [lax.all_gather(own, ("line", "core"), axis=0, tiled=True)]
        weights = []
        order = (0,)

    early = [[], []]
    states = [start_state[b].reshape(seq_width, STATE) for b in range(blocks)]
    states, own_late = lax.optimization_barrier((states, own))
    for b in range(blocks):
        seq = slice(b * block, (b + 1) * block)
        for half in range(2):
            early[half].append(
                early_products(out_grad[seq], ssd_input[seq], states[b], half, seq_width // 2)
            )
    if fast:
        pieces = column_pieces(block_input, own_late, replicas)
        far, _ = lax.optimization_barrier((far, pieces))
        pieces = [pieces[0]] + send_each(pieces[1:], "rep")
        far, early[0] = lax.optimization_barrier((far, early[0]))
        middle = send(far, "line", 1)
        middle, early[1], pieces[-1] = lax.optimization_barrier((middle, early[1], pieces[-1]))
        pair = send(jnp.concatenate([own, far], axis=0), "core", 1)
        weights = [own, near, far, pair, send(near, "core", 1)]
        middle, weights = lax.optimization_barrier((middle, weights))
        late = [middle, send(middle, "core", 1)]

    begun = []
    if fast:
        begun = [
            first_projection(block_input[b * block : (b + 1) * block], weights)
            for b in range(blocks)
        ]

    grads, mine, other = [], [], []
    for b in range(blocks):
        seq = slice(b * block, (b + 1) * block)
        parts = ssd_backward(
            block_input[seq],
            step_bias,
            decay_log,
            [early[0][b][0], early[1][b][0]],
            [early[0][b][1], early[1][b][1]],
            begun[b : b + 1],
            late,
            order,
        )
        for kept, part in zip((grads, mine, other), parts):
            kept.append(part)
    grad, mine, other = (
        kept[0] if blocks == 1 else jnp.concatenate(kept, axis=1) for kept in (grads, mine, other)
    )
    block_grad = block_gradient(grad, weights + late)

    if not fast:
        gradient = lax.psum_scatter(
            contract(grad, block_input, ((1,), (0,))),
            ("line", "core"),
            scatter_dimension=0,
            tiled=True,
        )
        pseudo = global_params - (local_rows - inner_rate * gradient)
        mean_pseudo = lax.psum(pseudo.astype(jnp.bfloat16), "rep").astype(jnp.float32) / replicas
        new_momentum = momentum_decay * momentum + mean_pseudo
        new_params = global_params - outer_rate * (mean_pseudo + momentum_decay * new_momentum)
        return (block_grad, new_params, new_momentum)

    tokens = blocks * block
    other = send(other, "core", 1)
    other, pieces = lax.optimization_barrier((other, pieces))
    both = jnp.concatenate([mine, other], axis=0)
    plane = [both] + send_each([both] * (replicas - 1), "rep")
    twin = send(jnp.concatenate([p[:tokens] for p in pieces], axis=0), "core", 1)
    sums = gradient_slice(plane, pieces, twin, chips)
    sums = [sums[0]] + send_each(sums[1:], "line")
    sums, block_grad = lax.optimization_barrier((sums, block_grad))
    stepped = stepped_slice(sums, pieces)
    stepped = [stepped] + send_each([stepped] * (replicas - 1), "rep")
    new_params, new_momentum = outer_step(global_params, momentum, stepped)
    return (block_grad, new_params, new_momentum)


def solution(mesh):
    replicas, shards = mesh.shape["rep"], mesh.shape["fsdp"]
    cores = 2 if shards % 2 == 0 else 1
    sizes = (replicas, shards // cores, cores)
    apart = jax.sharding.Mesh(mesh.devices.reshape(sizes), ("rep", "line", "core"))
    fsdp = ("line", "core")
    rows = P(("rep", "line", "core"), None)
    placed = (
        rows,
        rows,
        rows,
        P(("rep", "line", "core"), None, None),
        P(),
        P(),
        P("rep", fsdp, None),
        P(fsdp, None),
        P(fsdp, None),
    )
    return jax.shard_map(
        functools.partial(on_device, sizes),
        mesh=apart,
        in_specs=placed,
        out_specs=(rows, P(fsdp, None), P(fsdp, None)),
        check_vma=False,
    )
```

```python
import functools

import jax
import jax.numpy as jnp
from jax import lax
from jax.experimental import pallas as pl
from jax.experimental.pallas import tpu as pltpu
from jax.sharding import PartitionSpec as P

STATE = 64
LOG2E = 1.4426950408889634

inner_rate = 0.002
outer_rate = 0.7
momentum_decay = 0.9

VMEM_LIMIT = 20 * 1024 * 1024


def params(**more):
    return pltpu.CompilerParams(vmem_limit_bytes=VMEM_LIMIT, **more)


def whole_vmem(count):
    return [pl.BlockSpec(memory_space=pltpu.VMEM)] * count


def contract(left, right, dims):
    return lax.dot_general(left, right, (dims, ((), ())), preferred_element_type=jnp.float32)


def terms(value, count):
    out = []
    for _ in range(count):
        out.append(value.astype(jnp.bfloat16))
        value = value - out[-1].astype(jnp.float32)
    return out


def round_kernel(wide_ref, out_ref):
    out_ref[...] = wide_ref[...].astype(out_ref.dtype)


def rounded(wide):
    return pl.pallas_call(
        round_kernel,
        in_specs=whole_vmem(1),
        out_specs=pl.BlockSpec(memory_space=pltpu.VMEM),
        out_shape=jax.ShapeDtypeStruct(wide.shape, jnp.bfloat16),
        compiler_params=params(),
        name="rounded",
    )(wide)


def early_kernel(cot_ref, val_ref, state_ref, cross_ref, enter_ref):
    block = cot_ref.shape[0]
    lanes = lax.broadcasted_iota(jnp.int32, (block, 2 * STATE), 1)
    rows = lax.broadcasted_iota(jnp.int32, (block, block), 0)
    cols = lax.broadcasted_iota(jnp.int32, (block, block), 1)
    causal = rows >= cols
    low = lanes < STATE
    square = (2 * STATE, 2 * STATE)
    same_head = (lax.broadcasted_iota(jnp.int32, square, 0) < STATE) == (
        lax.broadcasted_iota(jnp.int32, square, 1) < STATE
    )
    for pair in range(cot_ref.shape[1] // (2 * STATE)):
        span = slice(pair * 2 * STATE, (pair + 1) * 2 * STATE)
        cot = cot_ref[:, span]
        val = val_ref[:, span]
        zero = jnp.zeros_like(cot)
        for odd in range(2):
            one = jnp.where(low, zero, cot) if odd else jnp.where(low, cot, zero)
            cross = contract(one, val, ((1,), (1,)))
            cross_ref[2 * pair + odd] = jnp.where(causal, cross, 0.0).astype(cross_ref.dtype)
        state = state_ref[span, :]
        wide = jnp.concatenate([state, state], axis=1)
        wide = jnp.where(same_head, wide, jnp.zeros_like(wide))
        enter_ref[:, span] = contract(cot, wide, ((1,), (0,)))


def early_products(out_grad, ssd_input, state, first, steps, piece):
    block = out_grad.shape[0]
    width = steps * piece
    heads = width // STATE
    return pl.pallas_call(
        early_kernel,
        grid=(steps,),
        in_specs=[
            pl.BlockSpec((block, piece), lambda i: (0, first + i)),
            pl.BlockSpec((block, piece), lambda i: (0, first + i)),
            pl.BlockSpec((piece, STATE), lambda i: (first + i, 0)),
        ],
        out_specs=[
            pl.BlockSpec((heads // steps, block, block), lambda i: (i, 0, 0)),
            pl.BlockSpec((block, piece), lambda i: (0, i)),
        ],
        out_shape=[
            jax.ShapeDtypeStruct((heads, block, block), jnp.bfloat16),
            jax.ShapeDtypeStruct((block, width), jnp.float32),
        ],
        compiler_params=params(),
        cost_estimate=pl.CostEstimate(flops=1, bytes_accessed=1, transcendentals=0),
        name="early_products",
    )(out_grad, ssd_input, state)


def stacked(refs):
    if len(refs) == 1:
        return refs[0][...]
    return jnp.concatenate([r[...].astype(jnp.float32) for r in refs], axis=0).astype(jnp.bfloat16)


def own_place(cores):
    return lax.axis_index("rep"), lax.axis_index("line") * cores + lax.axis_index("core")


def shard_rows(index, k, rows):
    return pl.ds(pl.multiple_of((index ^ k) * rows, 8), rows)


def first_kernel(rows_ref, *refs):
    refs[-1][...] = contract(stacked(refs[:-1]), rows_ref[...], ((1,), (1,)))


def first_projection(rows_in, weights):
    rows = sum(w.shape[0] for w in weights)
    return pl.pallas_call(
        first_kernel,
        in_specs=whole_vmem(1 + len(weights)),
        out_specs=pl.BlockSpec(memory_space=pltpu.VMEM),
        out_shape=jax.ShapeDtypeStruct((rows, rows_in.shape[0]), jnp.float32),
        compiler_params=params(),
        cost_estimate=pl.CostEstimate(flops=1, bytes_accessed=1, transcendentals=0),
        name="first_projection",
    )(rows_in, *weights)


def ssd_kernel(order, first, rows_ref, bias_ref, decay_ref, *rest):
    shards = len(order)
    cross_refs, enter_refs, rest = rest[:2], rest[2:4], rest[4:]
    _, spot = own_place(2) if shards > 1 else (0, 0)
    ahead = cross_refs[0].shape[0]
    first_ref, rest = (rest[0], rest[1:]) if first else (None, rest)
    weight_refs, rest = rest[: shards - first], rest[shards - first :]
    grad_ref, mine_ref, other_ref, proj_ref, col_ref, out_ref = rest
    block = rows_ref.shape[0]
    heads = bias_ref.shape[1]
    per = weight_refs[0].shape[0]
    arrived = contract(stacked(weight_refs), rows_ref[...], ((1,), (1,)))
    if shards == 1:
        proj_ref[...] = arrived
    else:
        for at, k in enumerate(order):
            source, line = (first_ref, at) if at < first else (arrived, at - first)
            proj_ref[shard_rows(spot, k, per), :] = source[line * per : (line + 1) * per]
    key_t = proj_ref[:STATE, :]
    query_t = proj_ref[STATE : 2 * STATE, :]
    bias_t = jnp.broadcast_to(bias_ref[...], (block, heads)).T
    rate = jnp.exp(jnp.broadcast_to(decay_ref[...], (block, heads)).T)
    raw = proj_ref[2 * STATE :, :] + bias_t
    step_t = jnp.maximum(raw, 0.0) + jnp.log1p(jnp.exp(-jnp.abs(raw)))
    up = lax.broadcasted_iota(jnp.int32, (block, block), 0)
    across = lax.broadcasted_iota(jnp.int32, (block, block), 1)
    before = jnp.where(up <= across, 1.0, 0.0).astype(jnp.bfloat16)
    after = jnp.where(up >= across, 1.0, 0.0).astype(jnp.bfloat16)
    cum_t = LOG2E * contract(
        jnp.concatenate(terms(-step_t * rate, 3), axis=1),
        jnp.concatenate([before] * 3, axis=0),
        ((1,), (0,)),
    )
    cum = cum_t.T
    step = step_t.T
    query = query_t.T
    query_high, query_low = terms(query, 2)
    key_high, key_low = terms(key_t, 2)
    scores = contract(
        jnp.concatenate([query_high, query_high, query_low], axis=1),
        jnp.concatenate([key_high, key_low, key_high], axis=0),
        ((1,), (0,)),
    )
    entered = jnp.exp2(cum)
    query_twice = jnp.concatenate([query, query], axis=1)
    low = lax.broadcasted_iota(jnp.int32, (block, 2 * STATE), 1) < STATE
    head_of = lax.broadcasted_iota(jnp.int32, (block, heads), 1)
    below = lax.broadcasted_iota(jnp.int32, (block, heads), 0) < STATE

    score_grad = jnp.zeros((block, block), jnp.float32)
    query_grad = jnp.zeros((block, 2 * STATE), jnp.float32)
    row_sums = jnp.zeros((block, heads), jnp.float32)
    for h0 in range(0, heads, 4):
        left, right = [], []
        for h in range(h0, h0 + 4):
            span = cum[:, h : h + 1] - cum_t[h : h + 1, :]
            cross = cross_refs[0][h] if h < ahead else cross_refs[1][h - ahead]
            weight = cross.astype(jnp.float32) * jnp.exp2(jnp.minimum(span, 0.0))
            score_grad = score_grad + weight * step_t[h : h + 1, :]
            mixed = weight * scores
            col_ref[h : h + 1, :] = jnp.sum(mixed, axis=0, keepdims=True)
            left.append(mixed.astype(jnp.bfloat16))
            right.append(jnp.where(head_of == h, step, 0.0).astype(jnp.bfloat16))
        for h in range(h0, h0 + 4, 2):
            gain = jnp.where(low, entered[:, h : h + 1], entered[:, h + 1 : h + 2])
            at = (h if h < ahead else h - ahead) * STATE
            part = enter_refs[int(h >= ahead)][:, at : at + 2 * STATE] * gain
            query_grad = query_grad + part
            left.append((part * query_twice).astype(jnp.bfloat16))
            right.append(
                jnp.where(head_of == jnp.where(below, h, h + 1), 1.0, 0.0).astype(jnp.bfloat16)
            )
        row_sums = row_sums + contract(
            jnp.concatenate(left, axis=1), jnp.concatenate(right, axis=0), ((1,), (0,))
        )

    cols_t = col_ref[...]
    cum_grad = row_sums.T - step_t * cols_t
    later = contract(
        jnp.concatenate(terms(cum_grad, 2), axis=1),
        jnp.concatenate([after] * 2, axis=0),
        ((1,), (0,)),
    )
    step_grad = cols_t - rate * later
    raw_grad = step_grad / (1.0 + jnp.exp(-raw))
    score_grad = score_grad.astype(jnp.bfloat16)
    out_ref[:STATE, :] = contract(query_t.astype(jnp.bfloat16), score_grad, ((1,), (0,)))
    query_all = (query_grad[:, :STATE] + query_grad[:, STATE:]).T
    out_ref[STATE : 2 * STATE, :] = query_all + contract(key_high, score_grad, ((1,), (1,)))
    out_ref[2 * STATE :, :] = raw_grad
    if shards == 1:
        grad_ref[...] = out_ref[...].astype(jnp.bfloat16)
        mine_ref[...] = jnp.zeros_like(mine_ref)
        other_ref[...] = jnp.zeros_like(other_ref)
        return
    core = spot % 2
    for part, ref in ((core, mine_ref), (1 - core, other_ref)):
        of_core = [out_ref[shard_rows(f + part, 0, per), :] for f in range(0, shards, 2)]
        ref[...] = jnp.concatenate(of_core, axis=0).astype(jnp.bfloat16)
    for at, k in enumerate(order):
        proj_ref[at * per : (at + 1) * per, :] = out_ref[shard_rows(spot, k, per), :]
    grad_ref[...] = proj_ref[...].astype(jnp.bfloat16)


def ssd_backward(rows_in, step_bias, decay_log, cross, enter, first, weights, order):
    block = rows_in.shape[0]
    heads = step_bias.shape[0]
    cols = len(order) * weights[0].shape[0]
    half = (cols // 2, block)
    return pl.pallas_call(
        functools.partial(ssd_kernel, order, len(order) - len(weights)),
        in_specs=whole_vmem(7 + len(first) + len(weights)),
        out_specs=whole_vmem(3),
        out_shape=[
            jax.ShapeDtypeStruct((cols, block), jnp.bfloat16),
            jax.ShapeDtypeStruct(half, jnp.bfloat16),
            jax.ShapeDtypeStruct(half, jnp.bfloat16),
        ],
        scratch_shapes=[
            pltpu.VMEM((cols, block), jnp.float32),
            pltpu.VMEM((heads, block), jnp.float32),
            pltpu.VMEM((cols, block), jnp.float32),
        ],
        compiler_params=params(),
        cost_estimate=pl.CostEstimate(flops=1, bytes_accessed=1, transcendentals=0),
        name="ssd_backward",
    )(rows_in, step_bias.reshape(1, -1), decay_log.reshape(1, -1), *cross, *enter, *first, *weights)


def block_grad_kernel(grad_ref, *refs):
    out_ref = refs[-1]
    weights = stacked(refs[:-1])
    out_ref[...] = contract(grad_ref[...].T, weights, ((1,), (0,))).astype(out_ref.dtype)


def block_gradient(grad, weights):
    depth = weights[0].shape[1]
    cols, block = grad.shape
    return pl.pallas_call(
        block_grad_kernel,
        in_specs=whole_vmem(1 + len(weights)),
        out_specs=pl.BlockSpec(memory_space=pltpu.VMEM),
        out_shape=jax.ShapeDtypeStruct((block, depth), jnp.bfloat16),
        compiler_params=params(),
        cost_estimate=pl.CostEstimate(
            flops=2 * block * cols * depth, bytes_accessed=4 * cols * depth, transcendentals=0
        ),
        name="block_gradient",
    )(grad, *weights)


def pieces_kernel(rows_ref, own_ref, *outs):
    block = rows_ref.shape[0]
    rep, _ = own_place(2)
    width = outs[0].shape[1]
    for k, out in enumerate(outs):
        cols = pl.ds(pl.multiple_of((rep ^ k) * width, 128), width)
        out[:block, :] = rows_ref[:, cols]
        out[block:, :] = own_ref[:, cols]


def column_pieces(rows_in, own, replicas):
    tokens, depth = rows_in.shape
    shape = (tokens + own.shape[0], depth // replicas)
    return pl.pallas_call(
        pieces_kernel,
        in_specs=whole_vmem(2),
        out_specs=whole_vmem(replicas),
        out_shape=[jax.ShapeDtypeStruct(shape, jnp.bfloat16)] * replicas,
        compiler_params=params(),
        name="column_pieces",
    )(rows_in, own)


def slice_kernel(replicas, *refs):
    grads, pieces, refs = refs[:replicas], refs[replicas : 2 * replicas], refs[2 * replicas :]
    twin, outs, total = refs[0], refs[1:-1], refs[-1]
    tokens = twin.shape[0] // replicas
    rows = total.shape[0]
    left, right = [], []
    for other in range(2):
        for k in range(replicas):
            left.append(grads[k][other * rows : (other + 1) * rows, :])
            right.append(
                twin[k * tokens : (k + 1) * tokens, :] if other else pieces[k][:tokens, :]
            )
    total[...] = contract(
        jnp.concatenate(left, axis=1), jnp.concatenate(right, axis=0), ((1,), (0,))
    )
    per = outs[0].shape[0]
    chip = lax.axis_index("line")
    for k, out in enumerate(outs):
        out[...] = total[shard_rows(chip, k, per), :].astype(jnp.bfloat16)


def gradient_slice(grads, pieces, twin, chips):
    rows = grads[0].shape[0] // (2 * chips)
    width = twin.shape[1]
    return pl.pallas_call(
        functools.partial(slice_kernel, len(pieces)),
        in_specs=whole_vmem(1 + 2 * len(pieces)),
        out_specs=whole_vmem(chips),
        out_shape=[jax.ShapeDtypeStruct((rows, width), jnp.bfloat16)] * chips,
        scratch_shapes=[pltpu.VMEM((rows * chips, width), jnp.float32)],
        compiler_params=params(),
        name="gradient_slice",
    )(*grads, *pieces, twin)


def stepped_kernel(chips, *refs):
    sums, pieces, out_ref = refs[:chips], refs[chips:-1], refs[-1]
    rows = out_ref.shape[0]
    total = sums[0][...].astype(jnp.float32)
    for part in sums[1:]:
        total = total + part[...].astype(jnp.float32)
    level = pieces[0][-rows:, :].astype(jnp.float32)
    for piece in pieces[1:]:
        level = level + piece[-rows:, :].astype(jnp.float32)
    mean = (level - inner_rate * total) * (1.0 / len(pieces))
    out_ref[...] = mean.astype(jnp.bfloat16)


def stepped_slice(sums, pieces):
    return pl.pallas_call(
        functools.partial(stepped_kernel, len(sums)),
        in_specs=whole_vmem(len(sums) + len(pieces)),
        out_specs=pl.BlockSpec(memory_space=pltpu.VMEM),
        out_shape=jax.ShapeDtypeStruct(sums[0].shape, jnp.bfloat16),
        compiler_params=params(),
        name="stepped_slice",
    )(*sums, *pieces)


def outer_kernel(par_ref, mom_ref, *refs):
    stepped, (new_par, new_mom, all_ref) = refs[:-3], refs[-3:]
    width = stepped[0].shape[1]
    for k, part in enumerate(stepped):
        all_ref[lax.axis_index("rep") ^ k] = part[...].astype(jnp.float32)
    for r in range(len(stepped)):
        cols = slice(r * width, (r + 1) * width)
        old = par_ref[:, cols]
        pseudo = old - all_ref[r]
        fresh = momentum_decay * mom_ref[:, cols] + pseudo
        new_mom[:, cols] = fresh
        new_par[:, cols] = old - outer_rate * (pseudo + momentum_decay * fresh)


def outer_step(global_params, momentum, stepped):
    return pl.pallas_call(
        outer_kernel,
        in_specs=whole_vmem(2 + len(stepped)),
        out_specs=whole_vmem(2),
        out_shape=[jax.ShapeDtypeStruct(global_params.shape, jnp.float32)] * 2,
        scratch_shapes=[pltpu.VMEM((len(stepped),) + stepped[0].shape, jnp.float32)],
        compiler_params=params(),
        name="outer_step",
    )(global_params, momentum, *stepped)


def on_device(
    sizes,
    block_input,
    ssd_input,
    out_grad,
    start_state,
    step_bias,
    decay_log,
    local_params,
    global_params,
    momentum,
):
    replicas, chips, cores = sizes
    local_rows = local_params[0]
    rows, depth = local_rows.shape
    own = rounded(local_rows)
    seq_width = ssd_input.shape[1]
    blocks = start_state.shape[0]
    block = block_input.shape[0] // blocks
    fast = (
        cores == 2
        and chips == 4
        and rows % 8 == 0
        and replicas & (replicas - 1) == 0
        and depth % (128 * replicas) == 0
    )

    def send(value, axis, k):
        count = dict(rep=replicas, line=chips, core=cores)[axis]
        return lax.ppermute(value, axis, [(i, i ^ k) for i in range(count)])

    def send_each(values, axis):
        values = [(k, v) for k, v in enumerate(values, 1)]
        return [sent for sent in reversed([send(v, axis, k) for k, v in reversed(values)])]

    if fast:
        far = send(own, "line", 3)
        near = send(own, "line", 1)
        order = (0, 2, 6, 1, 7, 3, 4, 5)
    else:
        late = [lax.all_gather(own, ("line", "core"), axis=0, tiled=True)]
        weights = []
        order = (0,)

    early = [[], []]
    states = [start_state[b].reshape(seq_width, STATE) for b in range(blocks)]
    states, own_late = lax.optimization_barrier((states, own))
    for b in range(blocks):
        seq = slice(b * block, (b + 1) * block)
        for part, (at, steps) in enumerate(((0, 6), (6, 2))):
            early[part].append(
                early_products(
                    out_grad[seq], ssd_input[seq], states[b], at, steps, seq_width // 8
                )
            )
    if fast:
        pieces = column_pieces(block_input, own_late, replicas)
        far, _ = lax.optimization_barrier((far, pieces))
        pieces = [pieces[0]] + send_each(pieces[1:], "rep")
        far, early[0] = lax.optimization_barrier((far, early[0]))
        middle = send(far, "line", 1)
        middle, early[1], pieces[-1] = lax.optimization_barrier((middle, early[1], pieces[-1]))
        pair = send(jnp.concatenate([own, far], axis=0), "core", 1)
        weights = [own, near, far, pair, send(near, "core", 1)]
        middle, weights = lax.optimization_barrier((middle, weights))
        late = [middle, send(middle, "core", 1)]

    begun = []
    if fast:
        begun = [
            first_projection(block_input[b * block : (b + 1) * block], weights)
            for b in range(blocks)
        ]

    grads, mine, other = [], [], []
    for b in range(blocks):
        seq = slice(b * block, (b + 1) * block)
        parts = ssd_backward(
            block_input[seq],
            step_bias,
            decay_log,
            [early[0][b][0], early[1][b][0]],
            [early[0][b][1], early[1][b][1]],
            begun[b : b + 1],
            late,
            order,
        )
        for kept, part in zip((grads, mine, other), parts):
            kept.append(part)
    grad, mine, other = (
        kept[0] if blocks == 1 else jnp.concatenate(kept, axis=1) for kept in (grads, mine, other)
    )
    block_grad = block_gradient(grad, weights + late)

    if not fast:
        gradient = lax.psum_scatter(
            contract(grad, block_input, ((1,), (0,))),
            ("line", "core"),
            scatter_dimension=0,
            tiled=True,
        )
        pseudo = global_params - (local_rows - inner_rate * gradient)
        mean_pseudo = lax.psum(pseudo.astype(jnp.bfloat16), "rep").astype(jnp.float32) / replicas
        new_momentum = momentum_decay * momentum + mean_pseudo
        new_params = global_params - outer_rate * (mean_pseudo + momentum_decay * new_momentum)
        return (block_grad, new_params, new_momentum)

    tokens = blocks * block
    other = send(other, "core", 1)
    other, pieces = lax.optimization_barrier((other, pieces))
    both = jnp.concatenate([mine, other], axis=0)
    plane = [both] + send_each([both] * (replicas - 1), "rep")
    twin = send(jnp.concatenate([p[:tokens] for p in pieces], axis=0), "core", 1)
    sums = gradient_slice(plane, pieces, twin, chips)
    sums = [sums[0]] + send_each(sums[1:], "line")
    sums, block_grad = lax.optimization_barrier((sums, block_grad))
    stepped = stepped_slice(sums, pieces)
    stepped = [stepped] + send_each([stepped] * (replicas - 1), "rep")
    new_params, new_momentum = outer_step(global_params, momentum, stepped)
    return (block_grad, new_params, new_momentum)


def solution(mesh):
    replicas, shards = mesh.shape["rep"], mesh.shape["fsdp"]
    cores = 2 if shards % 2 == 0 else 1
    sizes = (replicas, shards // cores, cores)
    apart = jax.sharding.Mesh(mesh.devices.reshape(sizes), ("rep", "line", "core"))
    fsdp = ("line", "core")
    rows = P(("rep", "line", "core"), None)
    placed = (
        rows,
        rows,
        rows,
        P(("rep", "line", "core"), None, None),
        P(),
        P(),
        P("rep", fsdp, None),
        P(fsdp, None),
        P(fsdp, None),
    )
    return jax.shard_map(
        functools.partial(on_device, sizes),
        mesh=apart,
        in_specs=placed,
        out_specs=(rows, P(fsdp, None), P(fsdp, None)),
        check_vma=False,
    )
```

```python
import functools

import jax
import jax.numpy as jnp
from jax import lax
from jax.experimental import pallas as pl
from jax.experimental.pallas import tpu as pltpu
from jax.sharding import PartitionSpec as P

STATE = 64
LOG2E = 1.4426950408889634

inner_rate = 0.002
outer_rate = 0.7
momentum_decay = 0.9

VMEM_LIMIT = 20 * 1024 * 1024


def params(**more):
    return pltpu.CompilerParams(vmem_limit_bytes=VMEM_LIMIT, **more)


def whole_vmem(count):
    return [pl.BlockSpec(memory_space=pltpu.VMEM)] * count


def contract(left, right, dims):
    return lax.dot_general(left, right, (dims, ((), ())), preferred_element_type=jnp.float32)


def terms(value, count):
    out = []
    for _ in range(count):
        out.append(value.astype(jnp.bfloat16))
        value = value - out[-1].astype(jnp.float32)
    return out


def round_kernel(wide_ref, out_ref):
    out_ref[...] = wide_ref[...].astype(out_ref.dtype)


def rounded(wide):
    return pl.pallas_call(
        round_kernel,
        in_specs=whole_vmem(1),
        out_specs=pl.BlockSpec(memory_space=pltpu.VMEM),
        out_shape=jax.ShapeDtypeStruct(wide.shape, jnp.bfloat16),
        compiler_params=params(),
        name="rounded",
    )(wide)


def early_kernel(cot_ref, val_ref, state_ref, cross_ref, enter_ref):
    block = cot_ref.shape[0]
    lanes = lax.broadcasted_iota(jnp.int32, (block, 2 * STATE), 1)
    rows = lax.broadcasted_iota(jnp.int32, (block, block), 0)
    cols = lax.broadcasted_iota(jnp.int32, (block, block), 1)
    causal = rows >= cols
    low = lanes < STATE
    square = (2 * STATE, 2 * STATE)
    same_head = (lax.broadcasted_iota(jnp.int32, square, 0) < STATE) == (
        lax.broadcasted_iota(jnp.int32, square, 1) < STATE
    )
    for pair in range(cot_ref.shape[1] // (2 * STATE)):
        span = slice(pair * 2 * STATE, (pair + 1) * 2 * STATE)
        cot = cot_ref[:, span]
        val = val_ref[:, span]
        zero = jnp.zeros_like(cot)
        for odd in range(2):
            one = jnp.where(low, zero, cot) if odd else jnp.where(low, cot, zero)
            cross = contract(one, val, ((1,), (1,)))
            cross_ref[2 * pair + odd] = jnp.where(causal, cross, 0.0).astype(cross_ref.dtype)
        state = state_ref[span, :]
        wide = jnp.concatenate([state, state], axis=1)
        wide = jnp.where(same_head, wide, jnp.zeros_like(wide))
        enter_ref[:, span] = contract(cot, wide, ((1,), (0,)))


def early_products(out_grad, ssd_input, state, first, steps, piece):
    block = out_grad.shape[0]
    width = steps * piece
    heads = width // STATE
    return pl.pallas_call(
        early_kernel,
        grid=(steps,),
        in_specs=[
            pl.BlockSpec((block, piece), lambda i: (0, first + i)),
            pl.BlockSpec((block, piece), lambda i: (0, first + i)),
            pl.BlockSpec((piece, STATE), lambda i: (first + i, 0)),
        ],
        out_specs=[
            pl.BlockSpec((heads // steps, block, block), lambda i: (i, 0, 0)),
            pl.BlockSpec((block, piece), lambda i: (0, i)),
        ],
        out_shape=[
            jax.ShapeDtypeStruct((heads, block, block), jnp.bfloat16),
            jax.ShapeDtypeStruct((block, width), jnp.float32),
        ],
        compiler_params=params(),
        cost_estimate=pl.CostEstimate(flops=1, bytes_accessed=1, transcendentals=0),
        name="early_products",
    )(out_grad, ssd_input, state)


def stacked(refs):
    if len(refs) == 1:
        return refs[0][...]
    return jnp.concatenate([r[...].astype(jnp.float32) for r in refs], axis=0).astype(jnp.bfloat16)


def own_place(cores):
    return lax.axis_index("rep"), lax.axis_index("line") * cores + lax.axis_index("core")


def shard_rows(index, k, rows):
    return pl.ds(pl.multiple_of((index ^ k) * rows, 8), rows)


def first_kernel(rows_ref, *refs):
    refs[-1][...] = contract(stacked(refs[:-1]), rows_ref[...], ((1,), (1,)))


def first_projection(rows_in, weights):
    rows = sum(w.shape[0] for w in weights)
    return pl.pallas_call(
        first_kernel,
        in_specs=whole_vmem(1 + len(weights)),
        out_specs=pl.BlockSpec(memory_space=pltpu.VMEM),
        out_shape=jax.ShapeDtypeStruct((rows, rows_in.shape[0]), jnp.float32),
        compiler_params=params(),
        cost_estimate=pl.CostEstimate(flops=1, bytes_accessed=1, transcendentals=0),
        name="first_projection",
    )(rows_in, *weights)


def ssd_kernel(order, first, rows_ref, bias_ref, decay_ref, *rest):
    shards = len(order)
    cross_refs, enter_refs, rest = rest[:2], rest[2:4], rest[4:]
    _, spot = own_place(2) if shards > 1 else (0, 0)
    ahead = cross_refs[0].shape[0]
    first_ref, rest = (rest[0], rest[1:]) if first else (None, rest)
    weight_refs, rest = rest[: shards - first], rest[shards - first :]
    grad_ref, mine_ref, other_ref, proj_ref, col_ref, out_ref = rest
    block = rows_ref.shape[0]
    heads = bias_ref.shape[1]
    per = weight_refs[0].shape[0]
    arrived = contract(stacked(weight_refs), rows_ref[...], ((1,), (1,)))
    if shards == 1:
        proj_ref[...] = arrived
    else:
        for at, k in enumerate(order):
            source, line = (first_ref, at) if at < first else (arrived, at - first)
            proj_ref[shard_rows(spot, k, per), :] = source[line * per : (line + 1) * per]
    key_t = proj_ref[:STATE, :]
    query_t = proj_ref[STATE : 2 * STATE, :]
    bias_t = jnp.broadcast_to(bias_ref[...], (block, heads)).T
    rate = jnp.exp(jnp.broadcast_to(decay_ref[...], (block, heads)).T)
    raw = proj_ref[2 * STATE :, :] + bias_t
    step_t = jnp.maximum(raw, 0.0) + jnp.log1p(jnp.exp(-jnp.abs(raw)))
    up = lax.broadcasted_iota(jnp.int32, (block, block), 0)
    across = lax.broadcasted_iota(jnp.int32, (block, block), 1)
    before = jnp.where(up <= across, 1.0, 0.0).astype(jnp.bfloat16)
    after = jnp.where(up >= across, 1.0, 0.0).astype(jnp.bfloat16)
    cum_t = LOG2E * contract(
        jnp.concatenate(terms(-step_t * rate, 3), axis=1),
        jnp.concatenate([before] * 3, axis=0),
        ((1,), (0,)),
    )
    cum = cum_t.T
    step = step_t.T
    query = query_t.T
    query_high, query_low = terms(query, 2)
    key_high, key_low = terms(key_t, 2)
    scores = contract(
        jnp.concatenate([query_high, query_high, query_low], axis=1),
        jnp.concatenate([key_high, key_low, key_high], axis=0),
        ((1,), (0,)),
    )
    entered = jnp.exp2(cum)
    query_twice = jnp.concatenate([query, query], axis=1)
    low = lax.broadcasted_iota(jnp.int32, (block, 2 * STATE), 1) < STATE
    head_of = lax.broadcasted_iota(jnp.int32, (block, heads), 1)
    below = lax.broadcasted_iota(jnp.int32, (block, heads), 0) < STATE

    score_grad = jnp.zeros((block, block), jnp.float32)
    query_grad = jnp.zeros((block, 2 * STATE), jnp.float32)
    row_sums = jnp.zeros((block, heads), jnp.float32)
    for h0 in range(0, heads, 4):
        left, right = [], []
        for h in range(h0, h0 + 4):
            span = cum[:, h : h + 1] - cum_t[h : h + 1, :]
            cross = cross_refs[0][h] if h < ahead else cross_refs[1][h - ahead]
            weight = cross.astype(jnp.float32) * jnp.exp2(jnp.minimum(span, 0.0))
            score_grad = score_grad + weight * step_t[h : h + 1, :]
            mixed = weight * scores
            col_ref[h : h + 1, :] = jnp.sum(mixed, axis=0, keepdims=True)
            left.append(mixed.astype(jnp.bfloat16))
            right.append(jnp.where(head_of == h, step, 0.0).astype(jnp.bfloat16))
        for h in range(h0, h0 + 4, 2):
            gain = jnp.where(low, entered[:, h : h + 1], entered[:, h + 1 : h + 2])
            at = (h if h < ahead else h - ahead) * STATE
            part = enter_refs[int(h >= ahead)][:, at : at + 2 * STATE] * gain
            query_grad = query_grad + part
            left.append((part * query_twice).astype(jnp.bfloat16))
            right.append(
                jnp.where(head_of == jnp.where(below, h, h + 1), 1.0, 0.0).astype(jnp.bfloat16)
            )
        row_sums = row_sums + contract(
            jnp.concatenate(left, axis=1), jnp.concatenate(right, axis=0), ((1,), (0,))
        )

    cols_t = col_ref[...]
    cum_grad = row_sums.T - step_t * cols_t
    later = contract(
        jnp.concatenate(terms(cum_grad, 2), axis=1),
        jnp.concatenate([after] * 2, axis=0),
        ((1,), (0,)),
    )
    step_grad = cols_t - rate * later
    raw_grad = step_grad / (1.0 + jnp.exp(-raw))
    score_grad = score_grad.astype(jnp.bfloat16)
    out_ref[:STATE, :] = contract(query_t.astype(jnp.bfloat16), score_grad, ((1,), (0,)))
    query_all = (query_grad[:, :STATE] + query_grad[:, STATE:]).T
    out_ref[STATE : 2 * STATE, :] = query_all + contract(key_high, score_grad, ((1,), (1,)))
    out_ref[2 * STATE :, :] = raw_grad
    if shards == 1:
        grad_ref[...] = out_ref[...].astype(jnp.bfloat16)
        mine_ref[...] = jnp.zeros_like(mine_ref)
        other_ref[...] = jnp.zeros_like(other_ref)
        return
    core = spot % 2
    for part, ref in ((core, mine_ref), (1 - core, other_ref)):
        of_core = [out_ref[shard_rows(f + part, 0, per), :] for f in range(0, shards, 2)]
        ref[...] = jnp.concatenate(of_core, axis=0).astype(jnp.bfloat16)
    for at, k in enumerate(order):
        proj_ref[at * per : (at + 1) * per, :] = out_ref[shard_rows(spot, k, per), :]
    grad_ref[...] = proj_ref[...].astype(jnp.bfloat16)


def ssd_backward(rows_in, step_bias, decay_log, cross, enter, first, weights, order):
    block = rows_in.shape[0]
    heads = step_bias.shape[0]
    cols = len(order) * weights[0].shape[0]
    half = (cols // 2, block)
    return pl.pallas_call(
        functools.partial(ssd_kernel, order, len(order) - len(weights)),
        in_specs=whole_vmem(7 + len(first) + len(weights)),
        out_specs=whole_vmem(3),
        out_shape=[
            jax.ShapeDtypeStruct((cols, block), jnp.bfloat16),
            jax.ShapeDtypeStruct(half, jnp.bfloat16),
            jax.ShapeDtypeStruct(half, jnp.bfloat16),
        ],
        scratch_shapes=[
            pltpu.VMEM((cols, block), jnp.float32),
            pltpu.VMEM((heads, block), jnp.float32),
            pltpu.VMEM((cols, block), jnp.float32),
        ],
        compiler_params=params(),
        cost_estimate=pl.CostEstimate(flops=1, bytes_accessed=1, transcendentals=0),
        name="ssd_backward",
    )(rows_in, step_bias.reshape(1, -1), decay_log.reshape(1, -1), *cross, *enter, *first, *weights)


def block_grad_kernel(grad_ref, *refs):
    out_ref = refs[-1]
    weights = stacked(refs[:-1])
    out_ref[...] = contract(grad_ref[...].T, weights, ((1,), (0,))).astype(out_ref.dtype)


def block_gradient(grad, weights):
    depth = weights[0].shape[1]
    cols, block = grad.shape
    return pl.pallas_call(
        block_grad_kernel,
        in_specs=whole_vmem(1 + len(weights)),
        out_specs=pl.BlockSpec(memory_space=pltpu.VMEM),
        out_shape=jax.ShapeDtypeStruct((block, depth), jnp.bfloat16),
        compiler_params=params(),
        cost_estimate=pl.CostEstimate(
            flops=2 * block * cols * depth, bytes_accessed=4 * cols * depth, transcendentals=0
        ),
        name="block_gradient",
    )(grad, *weights)


def pieces_kernel(rows_ref, own_ref, *outs):
    block = rows_ref.shape[0]
    rep, _ = own_place(2)
    width = outs[0].shape[1]
    for k, out in enumerate(outs):
        cols = pl.ds(pl.multiple_of((rep ^ k) * width, 128), width)
        out[:block, :] = rows_ref[:, cols]
        out[block:, :] = own_ref[:, cols]


def column_pieces(rows_in, own, replicas):
    tokens, depth = rows_in.shape
    shape = (tokens + own.shape[0], depth // replicas)
    return pl.pallas_call(
        pieces_kernel,
        in_specs=whole_vmem(2),
        out_specs=whole_vmem(replicas),
        out_shape=[jax.ShapeDtypeStruct(shape, jnp.bfloat16)] * replicas,
        compiler_params=params(),
        name="column_pieces",
    )(rows_in, own)


def slice_kernel(replicas, *refs):
    grads, pieces, refs = refs[:replicas], refs[replicas : 2 * replicas], refs[2 * replicas :]
    twin, outs, total = refs[0], refs[1:-1], refs[-1]
    tokens = twin.shape[0] // replicas
    rows = total.shape[0]
    left, right = [], []
    for other in range(2):
        for k in range(replicas):
            left.append(grads[k][other * rows : (other + 1) * rows, :])
            right.append(
                twin[k * tokens : (k + 1) * tokens, :] if other else pieces[k][:tokens, :]
            )
    total[...] = contract(
        jnp.concatenate(left, axis=1), jnp.concatenate(right, axis=0), ((1,), (0,))
    )
    per = outs[0].shape[0]
    chip = lax.axis_index("line")
    for k, out in enumerate(outs):
        out[...] = total[shard_rows(chip, k, per), :].astype(jnp.bfloat16)


def gradient_slice(grads, pieces, twin, chips):
    rows = grads[0].shape[0] // (2 * chips)
    width = twin.shape[1]
    return pl.pallas_call(
        functools.partial(slice_kernel, len(pieces)),
        in_specs=whole_vmem(1 + 2 * len(pieces)),
        out_specs=whole_vmem(chips),
        out_shape=[jax.ShapeDtypeStruct((rows, width), jnp.bfloat16)] * chips,
        scratch_shapes=[pltpu.VMEM((rows * chips, width), jnp.float32)],
        compiler_params=params(),
        name="gradient_slice",
    )(*grads, *pieces, twin)


def stepped_kernel(chips, *refs):
    sums, pieces, out_ref = refs[:chips], refs[chips:-1], refs[-1]
    rows = out_ref.shape[0]
    total = sums[0][...].astype(jnp.float32)
    for part in sums[1:]:
        total = total + part[...].astype(jnp.float32)
    level = pieces[0][-rows:, :].astype(jnp.float32)
    for piece in pieces[1:]:
        level = level + piece[-rows:, :].astype(jnp.float32)
    mean = (level - inner_rate * total) * (1.0 / len(pieces))
    out_ref[...] = mean.astype(jnp.bfloat16)


def stepped_slice(sums, pieces):
    return pl.pallas_call(
        functools.partial(stepped_kernel, len(sums)),
        in_specs=whole_vmem(len(sums) + len(pieces)),
        out_specs=pl.BlockSpec(memory_space=pltpu.VMEM),
        out_shape=jax.ShapeDtypeStruct(sums[0].shape, jnp.bfloat16),
        compiler_params=params(),
        name="stepped_slice",
    )(*sums, *pieces)


def outer_kernel(par_ref, mom_ref, *refs):
    stepped, (new_par, new_mom, all_ref) = refs[:-3], refs[-3:]
    width = stepped[0].shape[1]
    for k, part in enumerate(stepped):
        all_ref[lax.axis_index("rep") ^ k] = part[...].astype(jnp.float32)
    for r in range(len(stepped)):
        cols = slice(r * width, (r + 1) * width)
        old = par_ref[:, cols]
        pseudo = old - all_ref[r]
        fresh = momentum_decay * mom_ref[:, cols] + pseudo
        new_mom[:, cols] = fresh
        new_par[:, cols] = old - outer_rate * (pseudo + momentum_decay * fresh)


def outer_step(global_params, momentum, stepped):
    return pl.pallas_call(
        outer_kernel,
        in_specs=whole_vmem(2 + len(stepped)),
        out_specs=whole_vmem(2),
        out_shape=[jax.ShapeDtypeStruct(global_params.shape, jnp.float32)] * 2,
        scratch_shapes=[pltpu.VMEM((len(stepped),) + stepped[0].shape, jnp.float32)],
        compiler_params=params(),
        name="outer_step",
    )(global_params, momentum, *stepped)


def on_device(
    sizes,
    block_input,
    ssd_input,
    out_grad,
    start_state,
    step_bias,
    decay_log,
    local_params,
    global_params,
    momentum,
):
    replicas, chips, cores = sizes
    local_rows = local_params[0]
    rows, depth = local_rows.shape
    own = rounded(local_rows)
    seq_width = ssd_input.shape[1]
    blocks = start_state.shape[0]
    block = block_input.shape[0] // blocks
    fast = (
        cores == 2
        and chips == 4
        and rows % 8 == 0
        and replicas & (replicas - 1) == 0
        and depth % (128 * replicas) == 0
    )

    def send(value, axis, k):
        count = dict(rep=replicas, line=chips, core=cores)[axis]
        return lax.ppermute(value, axis, [(i, i ^ k) for i in range(count)])

    def send_each(values, axis):
        values = [(k, v) for k, v in enumerate(values, 1)]
        return [sent for sent in reversed([send(v, axis, k) for k, v in reversed(values)])]

    if fast:
        far = send(own, "line", 3)
        near = send(own, "line", 1)
        order = (0, 2, 6, 1, 7, 3, 4, 5)
    else:
        late = [lax.all_gather(own, ("line", "core"), axis=0, tiled=True)]
        weights = []
        order = (0,)

    early = [[], []]
    states = [start_state[b].reshape(seq_width, STATE) for b in range(blocks)]
    states, own_late = lax.optimization_barrier((states, own))
    for b in range(blocks):
        seq = slice(b * block, (b + 1) * block)
        for part, (at, steps) in enumerate(((0, 6), (6, 2))):
            early[part].append(
                early_products(
                    out_grad[seq], ssd_input[seq], states[b], at, steps, seq_width // 8
                )
            )
    if fast:
        pieces = column_pieces(block_input, own_late, replicas)
        far, _ = lax.optimization_barrier((far, pieces))
        pieces = [pieces[0]] + send_each(pieces[1:], "rep")
        far, early[0] = lax.optimization_barrier((far, early[0]))
        middle = send(far, "line", 1)
        middle, early[1], pieces[-1] = lax.optimization_barrier((middle, early[1], pieces[-1]))
        pair = send(jnp.concatenate([own, far], axis=0), "core", 1)
        weights = [own, near, far, pair, send(near, "core", 1)]
        middle, weights = lax.optimization_barrier((middle, weights))
        late = [middle, send(middle, "core", 1)]

    begun = []
    if fast:
        begun = [
            first_projection(block_input[b * block : (b + 1) * block], weights)
            for b in range(blocks)
        ]

    grads, mine, other = [], [], []
    for b in range(blocks):
        seq = slice(b * block, (b + 1) * block)
        parts = ssd_backward(
            block_input[seq],
            step_bias,
            decay_log,
            [early[0][b][0], early[1][b][0]],
            [early[0][b][1], early[1][b][1]],
            begun[b : b + 1],
            late,
            order,
        )
        for kept, part in zip((grads, mine, other), parts):
            kept.append(part)
    grad, mine, other = (
        kept[0] if blocks == 1 else jnp.concatenate(kept, axis=1) for kept in (grads, mine, other)
    )
    block_grad = block_gradient(grad, weights + late)

    if not fast:
        gradient = lax.psum_scatter(
            contract(grad, block_input, ((1,), (0,))),
            ("line", "core"),
            scatter_dimension=0,
            tiled=True,
        )
        pseudo = global_params - (local_rows - inner_rate * gradient)
        mean_pseudo = lax.psum(pseudo.astype(jnp.bfloat16), "rep").astype(jnp.float32) / replicas
        new_momentum = momentum_decay * momentum + mean_pseudo
        new_params = global_params - outer_rate * (mean_pseudo + momentum_decay * new_momentum)
        return (block_grad, new_params, new_momentum)

    tokens = blocks * block
    other = send(other, "core", 1)
    other, pieces = lax.optimization_barrier((other, pieces))
    both = jnp.concatenate([mine, other], axis=0)
    plane = [both] + send_each([both] * (replicas - 1), "rep")
    twin = send(jnp.concatenate([p[:tokens] for p in pieces], axis=0), "core", 1)
    sums = gradient_slice(plane, pieces, twin, chips)
    sums = [sums[0]] + send_each(sums[1:], "line")
    sums = sums[:1] + sums[:0:-1]
    sums, block_grad = lax.optimization_barrier((sums, block_grad))
    stepped = stepped_slice(sums, pieces)
    stepped = [stepped] + send_each([stepped] * (replicas - 1), "rep")
    stepped = lax.optimization_barrier(stepped[:1] + stepped[:0:-1])
    stepped = stepped[:1] + stepped[:0:-1]
    new_params, new_momentum = outer_step(global_params, momentum, stepped)
    return (block_grad, new_params, new_momentum)


def solution(mesh):
    replicas, shards = mesh.shape["rep"], mesh.shape["fsdp"]
    cores = 2 if shards % 2 == 0 else 1
    sizes = (replicas, shards // cores, cores)
    apart = jax.sharding.Mesh(mesh.devices.reshape(sizes), ("rep", "line", "core"))
    fsdp = ("line", "core")
    rows = P(("rep", "line", "core"), None)
    placed = (
        rows,
        rows,
        rows,
        P(("rep", "line", "core"), None, None),
        P(),
        P(),
        P("rep", fsdp, None),
        P(fsdp, None),
        P(fsdp, None),
    )
    return jax.shard_map(
        functools.partial(on_device, sizes),
        mesh=apart,
        in_specs=placed,
        out_specs=(rows, P(fsdp, None), P(fsdp, None)),
        check_vma=False,
    )
```

```python
import functools

import jax
import jax.numpy as jnp
from jax import lax
from jax.experimental import pallas as pl
from jax.experimental.pallas import tpu as pltpu
from jax.sharding import PartitionSpec as P

STATE = 64
LOG2E = 1.4426950408889634

inner_rate = 0.002
outer_rate = 0.7
momentum_decay = 0.9

VMEM_LIMIT = 20 * 1024 * 1024


def params(**more):
    return pltpu.CompilerParams(vmem_limit_bytes=VMEM_LIMIT, **more)


def whole_vmem(count):
    return [pl.BlockSpec(memory_space=pltpu.VMEM)] * count


def contract(left, right, dims):
    return lax.dot_general(left, right, (dims, ((), ())), preferred_element_type=jnp.float32)


def terms(value, count):
    out = []
    for _ in range(count):
        out.append(value.astype(jnp.bfloat16))
        value = value - out[-1].astype(jnp.float32)
    return out


def round_kernel(wide_ref, out_ref):
    out_ref[...] = wide_ref[...].astype(out_ref.dtype)


def rounded(wide):
    return pl.pallas_call(
        round_kernel,
        in_specs=whole_vmem(1),
        out_specs=pl.BlockSpec(memory_space=pltpu.VMEM),
        out_shape=jax.ShapeDtypeStruct(wide.shape, jnp.bfloat16),
        compiler_params=params(),
        name="rounded",
    )(wide)


def early_kernel(cot_ref, val_ref, state_ref, cross_ref, enter_ref):
    block = cot_ref.shape[0]
    lanes = lax.broadcasted_iota(jnp.int32, (block, 2 * STATE), 1)
    rows = lax.broadcasted_iota(jnp.int32, (block, block), 0)
    cols = lax.broadcasted_iota(jnp.int32, (block, block), 1)
    causal = rows >= cols
    low = lanes < STATE
    square = (2 * STATE, 2 * STATE)
    same_head = (lax.broadcasted_iota(jnp.int32, square, 0) < STATE) == (
        lax.broadcasted_iota(jnp.int32, square, 1) < STATE
    )
    for pair in range(cot_ref.shape[1] // (2 * STATE)):
        span = slice(pair * 2 * STATE, (pair + 1) * 2 * STATE)
        cot = cot_ref[:, span]
        val = val_ref[:, span]
        zero = jnp.zeros_like(cot)
        for odd in range(2):
            one = jnp.where(low, zero, cot) if odd else jnp.where(low, cot, zero)
            cross = contract(one, val, ((1,), (1,)))
            cross_ref[2 * pair + odd] = jnp.where(causal, cross, 0.0).astype(cross_ref.dtype)
        state = state_ref[span, :]
        wide = jnp.concatenate([state, state], axis=1)
        wide = jnp.where(same_head, wide, jnp.zeros_like(wide))
        enter_ref[:, span] = contract(cot, wide, ((1,), (0,)))


def early_products(out_grad, ssd_input, state, first, steps, piece):
    block = out_grad.shape[0]
    width = steps * piece
    heads = width // STATE
    return pl.pallas_call(
        early_kernel,
        grid=(steps,),
        in_specs=[
            pl.BlockSpec((block, piece), lambda i: (0, first + i)),
            pl.BlockSpec((block, piece), lambda i: (0, first + i)),
            pl.BlockSpec((piece, STATE), lambda i: (first + i, 0)),
        ],
        out_specs=[
            pl.BlockSpec((heads // steps, block, block), lambda i: (i, 0, 0)),
            pl.BlockSpec((block, piece), lambda i: (0, i)),
        ],
        out_shape=[
            jax.ShapeDtypeStruct((heads, block, block), jnp.bfloat16),
            jax.ShapeDtypeStruct((block, width), jnp.float32),
        ],
        compiler_params=params(),
        cost_estimate=pl.CostEstimate(flops=1, bytes_accessed=1, transcendentals=0),
        name="early_products",
    )(out_grad, ssd_input, state)


def stacked(refs):
    if len(refs) == 1:
        return refs[0][...]
    return jnp.concatenate([r[...].astype(jnp.float32) for r in refs], axis=0).astype(jnp.bfloat16)


def own_place(cores):
    return lax.axis_index("rep"), lax.axis_index("line") * cores + lax.axis_index("core")


def shard_rows(index, k, rows):
    return pl.ds(pl.multiple_of((index ^ k) * rows, 8), rows)


def first_kernel(rows_ref, *refs):
    refs[-1][...] = contract(stacked(refs[:-1]), rows_ref[...], ((1,), (1,)))


def first_projection(rows_in, weights):
    rows = sum(w.shape[0] for w in weights)
    return pl.pallas_call(
        first_kernel,
        in_specs=whole_vmem(1 + len(weights)),
        out_specs=pl.BlockSpec(memory_space=pltpu.VMEM),
        out_shape=jax.ShapeDtypeStruct((rows, rows_in.shape[0]), jnp.float32),
        compiler_params=params(),
        cost_estimate=pl.CostEstimate(flops=1, bytes_accessed=1, transcendentals=0),
        name="first_projection",
    )(rows_in, *weights)


def ssd_kernel(order, first, rows_ref, bias_ref, decay_ref, *rest):
    shards = len(order)
    cross_refs, enter_refs, rest = rest[:2], rest[2:4], rest[4:]
    _, spot = own_place(2) if shards > 1 else (0, 0)
    ahead = cross_refs[0].shape[0]
    first_ref, rest = (rest[0], rest[1:]) if first else (None, rest)
    weight_refs, rest = rest[: shards - first], rest[shards - first :]
    grad_ref, mine_ref, other_ref, proj_ref, col_ref, out_ref = rest
    block = rows_ref.shape[0]
    heads = bias_ref.shape[1]
    per = weight_refs[0].shape[0]
    arrived = contract(stacked(weight_refs), rows_ref[...], ((1,), (1,)))
    if shards == 1:
        proj_ref[...] = arrived
    else:
        for at, k in enumerate(order):
            source, line = (first_ref, at) if at < first else (arrived, at - first)
            proj_ref[shard_rows(spot, k, per), :] = source[line * per : (line + 1) * per]
    key_t = proj_ref[:STATE, :]
    query_t = proj_ref[STATE : 2 * STATE, :]
    bias_t = jnp.broadcast_to(bias_ref[...], (block, heads)).T
    rate = jnp.exp(jnp.broadcast_to(decay_ref[...], (block, heads)).T)
    raw = proj_ref[2 * STATE :, :] + bias_t
    step_t = jnp.maximum(raw, 0.0) + jnp.log1p(jnp.exp(-jnp.abs(raw)))
    up = lax.broadcasted_iota(jnp.int32, (block, block), 0)
    across = lax.broadcasted_iota(jnp.int32, (block, block), 1)
    before = jnp.where(up <= across, 1.0, 0.0).astype(jnp.bfloat16)
    after = jnp.where(up >= across, 1.0, 0.0).astype(jnp.bfloat16)
    cum_t = LOG2E * contract(
        jnp.concatenate(terms(-step_t * rate, 3), axis=1),
        jnp.concatenate([before] * 3, axis=0),
        ((1,), (0,)),
    )
    cum = cum_t.T
    step = step_t.T
    query = query_t.T
    query_high, query_low = terms(query, 2)
    key_high, key_low = terms(key_t, 2)
    scores = contract(
        jnp.concatenate([query_high, query_high, query_low], axis=1),
        jnp.concatenate([key_high, key_low, key_high], axis=0),
        ((1,), (0,)),
    )
    entered = jnp.exp2(cum)
    query_twice = jnp.concatenate([query, query], axis=1)
    low = lax.broadcasted_iota(jnp.int32, (block, 2 * STATE), 1) < STATE
    head_of = lax.broadcasted_iota(jnp.int32, (block, heads), 1)
    below = lax.broadcasted_iota(jnp.int32, (block, heads), 0) < STATE

    score_grad = jnp.zeros((block, block), jnp.float32)
    query_grad = jnp.zeros((block, 2 * STATE), jnp.float32)
    row_sums = jnp.zeros((block, heads), jnp.float32)
    for h0 in range(0, heads, 4):
        left, right = [], []
        for h in range(h0, h0 + 4):
            span = cum[:, h : h + 1] - cum_t[h : h + 1, :]
            cross = cross_refs[0][h] if h < ahead else cross_refs[1][h - ahead]
            weight = cross.astype(jnp.float32) * jnp.exp2(jnp.minimum(span, 0.0))
            score_grad = score_grad + weight * step_t[h : h + 1, :]
            mixed = weight * scores
            col_ref[h : h + 1, :] = jnp.sum(mixed, axis=0, keepdims=True)
            left.append(mixed.astype(jnp.bfloat16))
            right.append(jnp.where(head_of == h, step, 0.0).astype(jnp.bfloat16))
        for h in range(h0, h0 + 4, 2):
            gain = jnp.where(low, entered[:, h : h + 1], entered[:, h + 1 : h + 2])
            at = (h if h < ahead else h - ahead) * STATE
            part = enter_refs[int(h >= ahead)][:, at : at + 2 * STATE] * gain
            query_grad = query_grad + part
            left.append((part * query_twice).astype(jnp.bfloat16))
            right.append(
                jnp.where(head_of == jnp.where(below, h, h + 1), 1.0, 0.0).astype(jnp.bfloat16)
            )
        row_sums = row_sums + contract(
            jnp.concatenate(left, axis=1), jnp.concatenate(right, axis=0), ((1,), (0,))
        )

    cols_t = col_ref[...]
    cum_grad = row_sums.T - step_t * cols_t
    later = contract(
        jnp.concatenate(terms(cum_grad, 2), axis=1),
        jnp.concatenate([after] * 2, axis=0),
        ((1,), (0,)),
    )
    step_grad = cols_t - rate * later
    raw_grad = step_grad / (1.0 + jnp.exp(-raw))
    score_grad = score_grad.astype(jnp.bfloat16)
    out_ref[:STATE, :] = contract(query_t.astype(jnp.bfloat16), score_grad, ((1,), (0,)))
    query_all = (query_grad[:, :STATE] + query_grad[:, STATE:]).T
    out_ref[STATE : 2 * STATE, :] = query_all + contract(key_high, score_grad, ((1,), (1,)))
    out_ref[2 * STATE :, :] = raw_grad
    if shards == 1:
        grad_ref[...] = out_ref[...].astype(jnp.bfloat16)
        mine_ref[...] = jnp.zeros_like(mine_ref)
        other_ref[...] = jnp.zeros_like(other_ref)
        return
    core = spot % 2
    for part, ref in ((core, mine_ref), (1 - core, other_ref)):
        of_core = [out_ref[shard_rows(f + part, 0, per), :] for f in range(0, shards, 2)]
        ref[...] = jnp.concatenate(of_core, axis=0).astype(jnp.bfloat16)
    for at, k in enumerate(order):
        proj_ref[at * per : (at + 1) * per, :] = out_ref[shard_rows(spot, k, per), :]
    grad_ref[...] = proj_ref[...].astype(jnp.bfloat16)


def ssd_backward(rows_in, step_bias, decay_log, cross, enter, first, weights, order):
    block = rows_in.shape[0]
    heads = step_bias.shape[0]
    cols = len(order) * weights[0].shape[0]
    half = (cols // 2, block)
    return pl.pallas_call(
        functools.partial(ssd_kernel, order, len(order) - len(weights)),
        in_specs=whole_vmem(7 + len(first) + len(weights)),
        out_specs=whole_vmem(3),
        out_shape=[
            jax.ShapeDtypeStruct((cols, block), jnp.bfloat16),
            jax.ShapeDtypeStruct(half, jnp.bfloat16),
            jax.ShapeDtypeStruct(half, jnp.bfloat16),
        ],
        scratch_shapes=[
            pltpu.VMEM((cols, block), jnp.float32),
            pltpu.VMEM((heads, block), jnp.float32),
            pltpu.VMEM((cols, block), jnp.float32),
        ],
        compiler_params=params(),
        cost_estimate=pl.CostEstimate(flops=1, bytes_accessed=1, transcendentals=0),
        name="ssd_backward",
    )(rows_in, step_bias.reshape(1, -1), decay_log.reshape(1, -1), *cross, *enter, *first, *weights)


def block_grad_kernel(grad_ref, *refs):
    out_ref = refs[-1]
    weights = stacked(refs[:-1])
    out_ref[...] = contract(grad_ref[...].T, weights, ((1,), (0,))).astype(out_ref.dtype)


def block_gradient(grad, weights):
    depth = weights[0].shape[1]
    cols, block = grad.shape
    return pl.pallas_call(
        block_grad_kernel,
        in_specs=whole_vmem(1 + len(weights)),
        out_specs=pl.BlockSpec(memory_space=pltpu.VMEM),
        out_shape=jax.ShapeDtypeStruct((block, depth), jnp.bfloat16),
        compiler_params=params(),
        cost_estimate=pl.CostEstimate(
            flops=2 * block * cols * depth, bytes_accessed=4 * cols * depth, transcendentals=0
        ),
        name="block_gradient",
    )(grad, *weights)


def pieces_kernel(rows_ref, own_ref, *outs):
    block = rows_ref.shape[0]
    rep, _ = own_place(2)
    width = outs[0].shape[1]
    for k, out in enumerate(outs):
        cols = pl.ds(pl.multiple_of((rep ^ k) * width, 128), width)
        out[:block, :] = rows_ref[:, cols]
        out[block:, :] = own_ref[:, cols]


def column_pieces(rows_in, own, replicas):
    tokens, depth = rows_in.shape
    shape = (tokens + own.shape[0], depth // replicas)
    return pl.pallas_call(
        pieces_kernel,
        in_specs=whole_vmem(2),
        out_specs=whole_vmem(replicas),
        out_shape=[jax.ShapeDtypeStruct(shape, jnp.bfloat16)] * replicas,
        compiler_params=params(),
        name="column_pieces",
    )(rows_in, own)


def slice_kernel(replicas, *refs):
    grads, pieces, refs = refs[:replicas], refs[replicas : 2 * replicas], refs[2 * replicas :]
    twin, outs, total = refs[0], refs[1:-1], refs[-1]
    tokens = twin.shape[0] // replicas
    rows = total.shape[0]
    left, right = [], []
    for other in range(2):
        for k in range(replicas):
            left.append(grads[k][other * rows : (other + 1) * rows, :])
            right.append(
                twin[k * tokens : (k + 1) * tokens, :] if other else pieces[k][:tokens, :]
            )
    total[...] = contract(
        jnp.concatenate(left, axis=1), jnp.concatenate(right, axis=0), ((1,), (0,))
    )
    per = outs[0].shape[0]
    chip = lax.axis_index("line")
    for k, out in enumerate(outs):
        out[...] = total[shard_rows(chip, k, per), :].astype(jnp.bfloat16)


def gradient_slice(grads, pieces, twin, chips):
    rows = grads[0].shape[0] // (2 * chips)
    width = twin.shape[1]
    return pl.pallas_call(
        functools.partial(slice_kernel, len(pieces)),
        in_specs=whole_vmem(1 + 2 * len(pieces)),
        out_specs=whole_vmem(chips),
        out_shape=[jax.ShapeDtypeStruct((rows, width), jnp.bfloat16)] * chips,
        scratch_shapes=[pltpu.VMEM((rows * chips, width), jnp.float32)],
        compiler_params=params(),
        name="gradient_slice",
    )(*grads, *pieces, twin)


def stepped_kernel(chips, *refs):
    sums, pieces, out_ref = refs[:chips], refs[chips:-1], refs[-1]
    rows = out_ref.shape[0]
    total = sums[0][...].astype(jnp.float32)
    for part in sums[1:]:
        total = total + part[...].astype(jnp.float32)
    level = pieces[0][-rows:, :].astype(jnp.float32)
    for piece in pieces[1:]:
        level = level + piece[-rows:, :].astype(jnp.float32)
    mean = (level - inner_rate * total) * (1.0 / len(pieces))
    out_ref[...] = mean.astype(jnp.bfloat16)


def stepped_slice(sums, pieces):
    return pl.pallas_call(
        functools.partial(stepped_kernel, len(sums)),
        in_specs=whole_vmem(len(sums) + len(pieces)),
        out_specs=pl.BlockSpec(memory_space=pltpu.VMEM),
        out_shape=jax.ShapeDtypeStruct(sums[0].shape, jnp.bfloat16),
        compiler_params=params(),
        name="stepped_slice",
    )(*sums, *pieces)


def outer_kernel(par_ref, mom_ref, *refs):
    stepped, (new_par, new_mom, all_ref) = refs[:-3], refs[-3:]
    width = stepped[0].shape[1]
    for k, part in enumerate(stepped):
        all_ref[lax.axis_index("rep") ^ k] = part[...].astype(jnp.float32)
    for r in range(len(stepped)):
        cols = slice(r * width, (r + 1) * width)
        old = par_ref[:, cols]
        pseudo = old - all_ref[r]
        fresh = momentum_decay * mom_ref[:, cols] + pseudo
        new_mom[:, cols] = fresh
        new_par[:, cols] = old - outer_rate * (pseudo + momentum_decay * fresh)


def outer_step(global_params, momentum, stepped):
    return pl.pallas_call(
        outer_kernel,
        in_specs=whole_vmem(2 + len(stepped)),
        out_specs=whole_vmem(2),
        out_shape=[jax.ShapeDtypeStruct(global_params.shape, jnp.float32)] * 2,
        scratch_shapes=[pltpu.VMEM((len(stepped),) + stepped[0].shape, jnp.float32)],
        compiler_params=params(),
        name="outer_step",
    )(global_params, momentum, *stepped)


def on_device(
    sizes,
    block_input,
    ssd_input,
    out_grad,
    start_state,
    step_bias,
    decay_log,
    local_params,
    global_params,
    momentum,
):
    replicas, chips, cores = sizes
    local_rows = local_params[0]
    rows, depth = local_rows.shape
    own = rounded(local_rows)
    seq_width = ssd_input.shape[1]
    blocks = start_state.shape[0]
    block = block_input.shape[0] // blocks
    fast = (
        cores == 2
        and chips == 4
        and rows % 8 == 0
        and replicas & (replicas - 1) == 0
        and depth % (128 * replicas) == 0
    )

    def send(value, axis, k):
        count = dict(rep=replicas, line=chips, core=cores)[axis]
        return lax.ppermute(value, axis, [(i, i ^ k) for i in range(count)])

    def send_each(values, axis):
        values = [(k, v) for k, v in enumerate(values, 1)]
        return [sent for sent in reversed([send(v, axis, k) for k, v in reversed(values)])]

    if fast:
        far = send(own, "line", 3)
        near = send(own, "line", 1)
        order = (0, 2, 6, 1, 7, 3, 4, 5)
    else:
        late = [lax.all_gather(own, ("line", "core"), axis=0, tiled=True)]
        weights = []
        order = (0,)

    early = [[], []]
    states = [start_state[b].reshape(seq_width, STATE) for b in range(blocks)]
    states, own_late = lax.optimization_barrier((states, own))
    for b in range(blocks):
        seq = slice(b * block, (b + 1) * block)
        for part, (at, steps) in enumerate(((0, 6), (6, 2))):
            early[part].append(
                early_products(
                    out_grad[seq], ssd_input[seq], states[b], at, steps, seq_width // 8
                )
            )
    if fast:
        pieces = column_pieces(block_input, own_late, replicas)
        far, _ = lax.optimization_barrier((far, pieces))
        pieces = [pieces[0]] + send_each(pieces[1:], "rep")
        far, early[0] = lax.optimization_barrier((far, early[0]))
        middle = send(far, "line", 1)
        middle, early[1], pieces[-1] = lax.optimization_barrier((middle, early[1], pieces[-1]))
        pair = send(jnp.concatenate([own, far], axis=0), "core", 1)
        weights = [own, near, far, pair, send(near, "core", 1)]
        middle, weights = lax.optimization_barrier((middle, weights))
        late = [middle, send(middle, "core", 1)]

    begun = []
    if fast:
        begun = [
            first_projection(block_input[b * block : (b + 1) * block], weights)
            for b in range(blocks)
        ]

    grads, mine, other = [], [], []
    for b in range(blocks):
        seq = slice(b * block, (b + 1) * block)
        parts = ssd_backward(
            block_input[seq],
            step_bias,
            decay_log,
            [early[0][b][0], early[1][b][0]],
            [early[0][b][1], early[1][b][1]],
            begun[b : b + 1],
            late,
            order,
        )
        for kept, part in zip((grads, mine, other), parts):
            kept.append(part)
    grad, mine, other = (
        kept[0] if blocks == 1 else jnp.concatenate(kept, axis=1) for kept in (grads, mine, other)
    )
    block_grad = block_gradient(grad, weights + late)

    if not fast:
        gradient = lax.psum_scatter(
            contract(grad, block_input, ((1,), (0,))),
            ("line", "core"),
            scatter_dimension=0,
            tiled=True,
        )
        pseudo = global_params - (local_rows - inner_rate * gradient)
        mean_pseudo = lax.psum(pseudo.astype(jnp.bfloat16), "rep").astype(jnp.float32) / replicas
        new_momentum = momentum_decay * momentum + mean_pseudo
        new_params = global_params - outer_rate * (mean_pseudo + momentum_decay * new_momentum)
        return (block_grad, new_params, new_momentum)

    tokens = blocks * block
    other = send(other, "core", 1)
    other, pieces = lax.optimization_barrier((other, pieces))
    both = jnp.concatenate([mine, other], axis=0)
    plane = [both] + send_each([both] * (replicas - 1), "rep")
    plane = lax.optimization_barrier(plane[:1] + plane[:0:-1])
    plane = plane[:1] + plane[:0:-1]
    twin = send(jnp.concatenate([p[:tokens] for p in pieces], axis=0), "core", 1)
    sums = gradient_slice(plane, pieces, twin, chips)
    sums = [sums[0]] + send_each(sums[1:], "line")
    sums = sums[:1] + sums[:0:-1]
    sums, block_grad = lax.optimization_barrier((sums, block_grad))
    stepped = stepped_slice(sums, pieces)
    stepped = [stepped] + send_each([stepped] * (replicas - 1), "rep")
    stepped = lax.optimization_barrier(stepped[:1] + stepped[:0:-1])
    stepped = stepped[:1] + stepped[:0:-1]
    new_params, new_momentum = outer_step(global_params, momentum, stepped)
    return (block_grad, new_params, new_momentum)


def solution(mesh):
    replicas, shards = mesh.shape["rep"], mesh.shape["fsdp"]
    cores = 2 if shards % 2 == 0 else 1
    sizes = (replicas, shards // cores, cores)
    apart = jax.sharding.Mesh(mesh.devices.reshape(sizes), ("rep", "line", "core"))
    fsdp = ("line", "core")
    rows = P(("rep", "line", "core"), None)
    placed = (
        rows,
        rows,
        rows,
        P(("rep", "line", "core"), None, None),
        P(),
        P(),
        P("rep", fsdp, None),
        P(fsdp, None),
        P(fsdp, None),
    )
    return jax.shard_map(
        functools.partial(on_device, sizes),
        mesh=apart,
        in_specs=placed,
        out_specs=(rows, P(fsdp, None), P(fsdp, None)),
        check_vma=False,
    )
```

```python
import functools

import jax
import jax.numpy as jnp
from jax import lax
from jax.experimental import pallas as pl
from jax.experimental.pallas import tpu as pltpu
from jax.sharding import PartitionSpec as P

STATE = 64
LOG2E = 1.4426950408889634

inner_rate = 0.002
outer_rate = 0.7
momentum_decay = 0.9

VMEM_LIMIT = 20 * 1024 * 1024


def params(**more):
    return pltpu.CompilerParams(vmem_limit_bytes=VMEM_LIMIT, **more)


def whole_vmem(count):
    return [pl.BlockSpec(memory_space=pltpu.VMEM)] * count


def contract(left, right, dims):
    return lax.dot_general(left, right, (dims, ((), ())), preferred_element_type=jnp.float32)


def terms(value, count):
    out = []
    for _ in range(count):
        out.append(value.astype(jnp.bfloat16))
        value = value - out[-1].astype(jnp.float32)
    return out


def round_kernel(wide_ref, out_ref):
    out_ref[...] = wide_ref[...].astype(out_ref.dtype)


def rounded(wide):
    return pl.pallas_call(
        round_kernel,
        in_specs=whole_vmem(1),
        out_specs=pl.BlockSpec(memory_space=pltpu.VMEM),
        out_shape=jax.ShapeDtypeStruct(wide.shape, jnp.bfloat16),
        compiler_params=params(),
        name="rounded",
    )(wide)


def early_kernel(cot_ref, val_ref, state_ref, cross_ref, enter_ref):
    block = cot_ref.shape[0]
    lanes = lax.broadcasted_iota(jnp.int32, (block, 2 * STATE), 1)
    rows = lax.broadcasted_iota(jnp.int32, (block, block), 0)
    cols = lax.broadcasted_iota(jnp.int32, (block, block), 1)
    causal = rows >= cols
    low = lanes < STATE
    square = (2 * STATE, 2 * STATE)
    same_head = (lax.broadcasted_iota(jnp.int32, square, 0) < STATE) == (
        lax.broadcasted_iota(jnp.int32, square, 1) < STATE
    )
    for pair in range(cot_ref.shape[1] // (2 * STATE)):
        span = slice(pair * 2 * STATE, (pair + 1) * 2 * STATE)
        cot = cot_ref[:, span]
        val = val_ref[:, span]
        zero = jnp.zeros_like(cot)
        for odd in range(2):
            one = jnp.where(low, zero, cot) if odd else jnp.where(low, cot, zero)
            cross = contract(one, val, ((1,), (1,)))
            cross_ref[2 * pair + odd] = jnp.where(causal, cross, 0.0).astype(cross_ref.dtype)
        state = state_ref[span, :]
        wide = jnp.concatenate([state, state], axis=1)
        wide = jnp.where(same_head, wide, jnp.zeros_like(wide))
        enter_ref[:, span] = contract(cot, wide, ((1,), (0,)))


def early_products(out_grad, ssd_input, state, first, steps, piece):
    block = out_grad.shape[0]
    width = steps * piece
    heads = width // STATE
    return pl.pallas_call(
        early_kernel,
        grid=(steps,),
        in_specs=[
            pl.BlockSpec((block, piece), lambda i: (0, first + i)),
            pl.BlockSpec((block, piece), lambda i: (0, first + i)),
            pl.BlockSpec((piece, STATE), lambda i: (first + i, 0)),
        ],
        out_specs=[
            pl.BlockSpec((heads // steps, block, block), lambda i: (i, 0, 0)),
            pl.BlockSpec((block, piece), lambda i: (0, i)),
        ],
        out_shape=[
            jax.ShapeDtypeStruct((heads, block, block), jnp.bfloat16),
            jax.ShapeDtypeStruct((block, width), jnp.float32),
        ],
        compiler_params=params(),
        cost_estimate=pl.CostEstimate(flops=1, bytes_accessed=1, transcendentals=0),
        name="early_products",
    )(out_grad, ssd_input, state)


def stacked(refs):
    if len(refs) == 1:
        return refs[0][...]
    return jnp.concatenate([r[...].astype(jnp.float32) for r in refs], axis=0).astype(jnp.bfloat16)


def own_place(cores):
    return lax.axis_index("rep"), lax.axis_index("line") * cores + lax.axis_index("core")


def shard_rows(index, k, rows):
    return pl.ds(pl.multiple_of((index ^ k) * rows, 8), rows)


def first_kernel(rows_ref, *refs):
    refs[-1][...] = contract(stacked(refs[:-1]), rows_ref[...], ((1,), (1,)))


def first_projection(rows_in, weights):
    rows = sum(w.shape[0] for w in weights)
    return pl.pallas_call(
        first_kernel,
        in_specs=whole_vmem(1 + len(weights)),
        out_specs=pl.BlockSpec(memory_space=pltpu.VMEM),
        out_shape=jax.ShapeDtypeStruct((rows, rows_in.shape[0]), jnp.float32),
        compiler_params=params(),
        cost_estimate=pl.CostEstimate(flops=1, bytes_accessed=1, transcendentals=0),
        name="first_projection",
    )(rows_in, *weights)


def ssd_kernel(order, first, rows_ref, bias_ref, decay_ref, *rest):
    shards = len(order)
    cross_refs, enter_refs, rest = rest[:2], rest[2:4], rest[4:]
    _, spot = own_place(2) if shards > 1 else (0, 0)
    ahead = cross_refs[0].shape[0]
    first_ref, rest = (rest[0], rest[1:]) if first else (None, rest)
    weight_refs, rest = rest[: shards - first], rest[shards - first :]
    grad_ref, mine_ref, other_ref, proj_ref, col_ref, out_ref = rest
    block = rows_ref.shape[0]
    heads = bias_ref.shape[1]
    per = weight_refs[0].shape[0]
    arrived = contract(stacked(weight_refs), rows_ref[...], ((1,), (1,)))
    if shards == 1:
        proj_ref[...] = arrived
    else:
        for at, k in enumerate(order):
            source, line = (first_ref, at) if at < first else (arrived, at - first)
            proj_ref[shard_rows(spot, k, per), :] = source[line * per : (line + 1) * per]
    key_t = proj_ref[:STATE, :]
    query_t = proj_ref[STATE : 2 * STATE, :]
    bias_t = jnp.broadcast_to(bias_ref[...], (block, heads)).T
    rate = jnp.exp(jnp.broadcast_to(decay_ref[...], (block, heads)).T)
    raw = proj_ref[2 * STATE :, :] + bias_t
    step_t = jnp.maximum(raw, 0.0) + jnp.log1p(jnp.exp(-jnp.abs(raw)))
    up = lax.broadcasted_iota(jnp.int32, (block, block), 0)
    across = lax.broadcasted_iota(jnp.int32, (block, block), 1)
    before = jnp.where(up <= across, 1.0, 0.0).astype(jnp.bfloat16)
    after = jnp.where(up >= across, 1.0, 0.0).astype(jnp.bfloat16)
    cum_t = LOG2E * contract(
        jnp.concatenate(terms(-step_t * rate, 3), axis=1),
        jnp.concatenate([before] * 3, axis=0),
        ((1,), (0,)),
    )
    cum = cum_t.T
    step = step_t.T
    query = query_t.T
    query_high, query_low = terms(query, 2)
    key_high, key_low = terms(key_t, 2)
    scores = contract(
        jnp.concatenate([query_high, query_high, query_low], axis=1),
        jnp.concatenate([key_high, key_low, key_high], axis=0),
        ((1,), (0,)),
    )
    entered = jnp.exp2(cum)
    query_twice = jnp.concatenate([query, query], axis=1)
    low = lax.broadcasted_iota(jnp.int32, (block, 2 * STATE), 1) < STATE
    head_of = lax.broadcasted_iota(jnp.int32, (block, heads), 1)
    below = lax.broadcasted_iota(jnp.int32, (block, heads), 0) < STATE

    score_grad = jnp.zeros((block, block), jnp.float32)
    query_grad = jnp.zeros((block, 2 * STATE), jnp.float32)
    row_sums = jnp.zeros((block, heads), jnp.float32)
    for h0 in range(0, heads, 4):
        left, right = [], []
        for h in range(h0, h0 + 4):
            span = cum[:, h : h + 1] - cum_t[h : h + 1, :]
            cross = cross_refs[0][h] if h < ahead else cross_refs[1][h - ahead]
            weight = cross.astype(jnp.float32) * jnp.exp2(jnp.minimum(span, 0.0))
            score_grad = score_grad + weight * step_t[h : h + 1, :]
            mixed = weight * scores
            col_ref[h : h + 1, :] = jnp.sum(mixed, axis=0, keepdims=True)
            left.append(mixed.astype(jnp.bfloat16))
            right.append(jnp.where(head_of == h, step, 0.0).astype(jnp.bfloat16))
        for h in range(h0, h0 + 4, 2):
            gain = jnp.where(low, entered[:, h : h + 1], entered[:, h + 1 : h + 2])
            at = (h if h < ahead else h - ahead) * STATE
            part = enter_refs[int(h >= ahead)][:, at : at + 2 * STATE] * gain
            query_grad = query_grad + part
            left.append((part * query_twice).astype(jnp.bfloat16))
            right.append(
                jnp.where(head_of == jnp.where(below, h, h + 1), 1.0, 0.0).astype(jnp.bfloat16)
            )
        row_sums = row_sums + contract(
            jnp.concatenate(left, axis=1), jnp.concatenate(right, axis=0), ((1,), (0,))
        )

    cols_t = col_ref[...]
    cum_grad = row_sums.T - step_t * cols_t
    later = contract(
        jnp.concatenate(terms(cum_grad, 2), axis=1),
        jnp.concatenate([after] * 2, axis=0),
        ((1,), (0,)),
    )
    step_grad = cols_t - rate * later
    raw_grad = step_grad / (1.0 + jnp.exp(-raw))
    score_grad = score_grad.astype(jnp.bfloat16)
    out_ref[:STATE, :] = contract(query_t.astype(jnp.bfloat16), score_grad, ((1,), (0,)))
    query_all = (query_grad[:, :STATE] + query_grad[:, STATE:]).T
    out_ref[STATE : 2 * STATE, :] = query_all + contract(key_high, score_grad, ((1,), (1,)))
    out_ref[2 * STATE :, :] = raw_grad
    if shards == 1:
        grad_ref[...] = out_ref[...].astype(jnp.bfloat16)
        mine_ref[...] = jnp.zeros_like(mine_ref)
        other_ref[...] = jnp.zeros_like(other_ref)
        return
    core = spot % 2
    for part, ref in ((core, mine_ref), (1 - core, other_ref)):
        of_core = [out_ref[shard_rows(f + part, 0, per), :] for f in range(0, shards, 2)]
        ref[...] = jnp.concatenate(of_core, axis=0).astype(jnp.bfloat16)
    for at, k in enumerate(order):
        proj_ref[at * per : (at + 1) * per, :] = out_ref[shard_rows(spot, k, per), :]
    grad_ref[...] = proj_ref[...].astype(jnp.bfloat16)


def ssd_backward(rows_in, step_bias, decay_log, cross, enter, first, weights, order):
    block = rows_in.shape[0]
    heads = step_bias.shape[0]
    cols = len(order) * weights[0].shape[0]
    half = (cols // 2, block)
    return pl.pallas_call(
        functools.partial(ssd_kernel, order, len(order) - len(weights)),
        in_specs=whole_vmem(7 + len(first) + len(weights)),
        out_specs=whole_vmem(3),
        out_shape=[
            jax.ShapeDtypeStruct((cols, block), jnp.bfloat16),
            jax.ShapeDtypeStruct(half, jnp.bfloat16),
            jax.ShapeDtypeStruct(half, jnp.bfloat16),
        ],
        scratch_shapes=[
            pltpu.VMEM((cols, block), jnp.float32),
            pltpu.VMEM((heads, block), jnp.float32),
            pltpu.VMEM((cols, block), jnp.float32),
        ],
        compiler_params=params(),
        cost_estimate=pl.CostEstimate(flops=1, bytes_accessed=1, transcendentals=0),
        name="ssd_backward",
    )(rows_in, step_bias.reshape(1, -1), decay_log.reshape(1, -1), *cross, *enter, *first, *weights)


def block_grad_kernel(grad_ref, *refs):
    out_ref = refs[-1]
    weights = stacked(refs[:-1])
    out_ref[...] = contract(grad_ref[...].T, weights, ((1,), (0,))).astype(out_ref.dtype)


def block_gradient(grad, weights):
    depth = weights[0].shape[1]
    cols, block = grad.shape
    return pl.pallas_call(
        block_grad_kernel,
        in_specs=whole_vmem(1 + len(weights)),
        out_specs=pl.BlockSpec(memory_space=pltpu.VMEM),
        out_shape=jax.ShapeDtypeStruct((block, depth), jnp.bfloat16),
        compiler_params=params(),
        cost_estimate=pl.CostEstimate(
            flops=2 * block * cols * depth, bytes_accessed=4 * cols * depth, transcendentals=0
        ),
        name="block_gradient",
    )(grad, *weights)


def pieces_kernel(rows_ref, own_ref, *outs):
    block = rows_ref.shape[0]
    rep, _ = own_place(2)
    width = outs[0].shape[1]
    for k, out in enumerate(outs):
        cols = pl.ds(pl.multiple_of((rep ^ k) * width, 128), width)
        out[:block, :] = rows_ref[:, cols]
        out[block:, :] = own_ref[:, cols]


def column_pieces(rows_in, own, replicas):
    tokens, depth = rows_in.shape
    shape = (tokens + own.shape[0], depth // replicas)
    return pl.pallas_call(
        pieces_kernel,
        in_specs=whole_vmem(2),
        out_specs=whole_vmem(replicas),
        out_shape=[jax.ShapeDtypeStruct(shape, jnp.bfloat16)] * replicas,
        compiler_params=params(),
        name="column_pieces",
    )(rows_in, own)


def slice_kernel(replicas, *refs):
    grads, pieces, refs = refs[:replicas], refs[replicas : 2 * replicas], refs[2 * replicas :]
    twin, outs, total = refs[0], refs[1:-1], refs[-1]
    tokens = twin.shape[0] // replicas
    rows = total.shape[0]
    left, right = [], []
    for other in range(2):
        for k in range(replicas):
            left.append(grads[k][other * rows : (other + 1) * rows, :])
            right.append(
                twin[k * tokens : (k + 1) * tokens, :] if other else pieces[k][:tokens, :]
            )
    total[...] = contract(
        jnp.concatenate(left, axis=1), jnp.concatenate(right, axis=0), ((1,), (0,))
    )
    per = outs[0].shape[0]
    chip = lax.axis_index("line")
    for k, out in enumerate(outs):
        out[...] = total[shard_rows(chip, k, per), :].astype(jnp.bfloat16)


def gradient_slice(grads, pieces, twin, chips):
    rows = grads[0].shape[0] // (2 * chips)
    width = twin.shape[1]
    return pl.pallas_call(
        functools.partial(slice_kernel, len(pieces)),
        in_specs=whole_vmem(1 + 2 * len(pieces)),
        out_specs=whole_vmem(chips),
        out_shape=[jax.ShapeDtypeStruct((rows, width), jnp.bfloat16)] * chips,
        scratch_shapes=[pltpu.VMEM((rows * chips, width), jnp.float32)],
        compiler_params=params(),
        name="gradient_slice",
    )(*grads, *pieces, twin)


def stepped_kernel(chips, *refs):
    sums, pieces, out_ref = refs[:chips], refs[chips:-1], refs[-1]
    rows = out_ref.shape[0]
    total = sums[0][...].astype(jnp.float32)
    for part in sums[1:]:
        total = total + part[...].astype(jnp.float32)
    level = pieces[0][-rows:, :].astype(jnp.float32)
    for piece in pieces[1:]:
        level = level + piece[-rows:, :].astype(jnp.float32)
    mean = (level - inner_rate * total) * (1.0 / len(pieces))
    out_ref[...] = mean.astype(jnp.bfloat16)


def stepped_slice(sums, pieces):
    return pl.pallas_call(
        functools.partial(stepped_kernel, len(sums)),
        in_specs=whole_vmem(len(sums) + len(pieces)),
        out_specs=pl.BlockSpec(memory_space=pltpu.VMEM),
        out_shape=jax.ShapeDtypeStruct(sums[0].shape, jnp.bfloat16),
        compiler_params=params(),
        name="stepped_slice",
    )(*sums, *pieces)


def outer_kernel(par_ref, mom_ref, *refs):
    stepped, (new_par, new_mom, all_ref) = refs[:-3], refs[-3:]
    width = stepped[0].shape[1]
    for k, part in enumerate(stepped):
        all_ref[lax.axis_index("rep") ^ k] = part[...].astype(jnp.float32)
    for r in range(len(stepped)):
        cols = slice(r * width, (r + 1) * width)
        old = par_ref[:, cols]
        pseudo = old - all_ref[r]
        fresh = momentum_decay * mom_ref[:, cols] + pseudo
        new_mom[:, cols] = fresh
        new_par[:, cols] = old - outer_rate * (pseudo + momentum_decay * fresh)


def outer_step(global_params, momentum, stepped):
    return pl.pallas_call(
        outer_kernel,
        in_specs=whole_vmem(2 + len(stepped)),
        out_specs=whole_vmem(2),
        out_shape=[jax.ShapeDtypeStruct(global_params.shape, jnp.float32)] * 2,
        scratch_shapes=[pltpu.VMEM((len(stepped),) + stepped[0].shape, jnp.float32)],
        compiler_params=params(),
        name="outer_step",
    )(global_params, momentum, *stepped)


def on_device(
    sizes,
    block_input,
    ssd_input,
    out_grad,
    start_state,
    step_bias,
    decay_log,
    local_params,
    global_params,
    momentum,
):
    replicas, chips, cores = sizes
    local_rows = local_params[0]
    rows, depth = local_rows.shape
    own = rounded(local_rows)
    seq_width = ssd_input.shape[1]
    blocks = start_state.shape[0]
    block = block_input.shape[0] // blocks
    fast = (
        cores == 2
        and chips == 4
        and rows % 8 == 0
        and replicas & (replicas - 1) == 0
        and depth % (128 * replicas) == 0
    )

    def send(value, axis, k):
        count = dict(rep=replicas, line=chips, core=cores)[axis]
        return lax.ppermute(value, axis, [(i, i ^ k) for i in range(count)])

    def send_each(values, axis):
        values = [(k, v) for k, v in enumerate(values, 1)]
        return [sent for sent in reversed([send(v, axis, k) for k, v in reversed(values)])]

    if fast:
        far = send(own, "line", 3)
        near = send(own, "line", 1)
        order = (0, 2, 6, 1, 7, 3, 4, 5)
    else:
        late = [lax.all_gather(own, ("line", "core"), axis=0, tiled=True)]
        weights = []
        order = (0,)

    early = [[], []]
    states = [start_state[b].reshape(seq_width, STATE) for b in range(blocks)]
    states, own_late = lax.optimization_barrier((states, own))
    for b in range(blocks):
        seq = slice(b * block, (b + 1) * block)
        for part, (at, steps) in enumerate(((0, 6), (6, 2))):
            early[part].append(
                early_products(
                    out_grad[seq], ssd_input[seq], states[b], at, steps, seq_width // 8
                )
            )
    if fast:
        pieces = column_pieces(block_input, own_late, replicas)
        far, _ = lax.optimization_barrier((far, pieces))
        pieces = [pieces[0]] + send_each(pieces[1:], "rep")
        far, early[0] = lax.optimization_barrier((far, early[0]))
        middle = send(far, "line", 1)
        middle, early[1], pieces[-1] = lax.optimization_barrier((middle, early[1], pieces[-1]))
        pair = send(jnp.concatenate([own, far], axis=0), "core", 1)
        weights = [own, near, far, pair, send(near, "core", 1)]
        middle, weights = lax.optimization_barrier((middle, weights))
        late = [middle, send(middle, "core", 1)]

    begun = []
    if fast:
        begun = [
            first_projection(block_input[b * block : (b + 1) * block], weights)
            for b in range(blocks)
        ]

    grads, mine, other = [], [], []
    for b in range(blocks):
        seq = slice(b * block, (b + 1) * block)
        parts = ssd_backward(
            block_input[seq],
            step_bias,
            decay_log,
            [early[0][b][0], early[1][b][0]],
            [early[0][b][1], early[1][b][1]],
            begun[b : b + 1],
            late,
            order,
        )
        for kept, part in zip((grads, mine, other), parts):
            kept.append(part)
    grad, mine, other = (
        kept[0] if blocks == 1 else jnp.concatenate(kept, axis=1) for kept in (grads, mine, other)
    )
    block_grad = block_gradient(grad, weights + late)

    if not fast:
        gradient = lax.psum_scatter(
            contract(grad, block_input, ((1,), (0,))),
            ("line", "core"),
            scatter_dimension=0,
            tiled=True,
        )
        pseudo = global_params - (local_rows - inner_rate * gradient)
        mean_pseudo = lax.psum(pseudo.astype(jnp.bfloat16), "rep").astype(jnp.float32) / replicas
        new_momentum = momentum_decay * momentum + mean_pseudo
        new_params = global_params - outer_rate * (mean_pseudo + momentum_decay * new_momentum)
        return (block_grad, new_params, new_momentum)

    tokens = blocks * block
    other = send(other, "core", 1)
    other, pieces = lax.optimization_barrier((other, pieces))
    both = jnp.concatenate([mine, other], axis=0)
    plane = [both] + send_each([both] * (replicas - 1), "rep")
    twin = send(jnp.concatenate([p[:tokens] for p in pieces], axis=0), "core", 1)
    plane, twin = lax.optimization_barrier((plane[:1] + plane[:0:-1], twin))
    plane = plane[:1] + plane[:0:-1]
    sums = gradient_slice(plane, pieces, twin, chips)
    sums = [sums[0]] + send_each(sums[1:], "line")
    sums = sums[:1] + sums[:0:-1]
    sums, block_grad = lax.optimization_barrier((sums, block_grad))
    stepped = stepped_slice(sums, pieces)
    stepped = [stepped] + send_each([stepped] * (replicas - 1), "rep")
    stepped = lax.optimization_barrier(stepped[:1] + stepped[:0:-1])
    stepped = stepped[:1] + stepped[:0:-1]
    new_params, new_momentum = outer_step(global_params, momentum, stepped)
    return (block_grad, new_params, new_momentum)


def solution(mesh):
    replicas, shards = mesh.shape["rep"], mesh.shape["fsdp"]
    cores = 2 if shards % 2 == 0 else 1
    sizes = (replicas, shards // cores, cores)
    apart = jax.sharding.Mesh(mesh.devices.reshape(sizes), ("rep", "line", "core"))
    fsdp = ("line", "core")
    rows = P(("rep", "line", "core"), None)
    placed = (
        rows,
        rows,
        rows,
        P(("rep", "line", "core"), None, None),
        P(),
        P(),
        P("rep", fsdp, None),
        P(fsdp, None),
        P(fsdp, None),
    )
    return jax.shard_map(
        functools.partial(on_device, sizes),
        mesh=apart,
        in_specs=placed,
        out_specs=(rows, P(fsdp, None), P(fsdp, None)),
        check_vma=False,
    )
```
